128 devices in a mesh: replica: 64 (over z, y, x), shard: 2 (over core).
Axes of the slice: x: 4, y: 4, z: 4, core: 2. Of those that a mesh axis runs over, the one named last changes fastest.
Arguments:
- tokens: bfloat16 [49152, 960], P(('replica', 'shard')), may hold values from -6 to 6
- starts: int32 [49152], P(('replica', 'shard')), may hold values from 0 to 383, as said below
- out_grad: bfloat16 [49152, 960], P(('replica', 'shard')), may hold values from -6 to 6
- norm_attn: bfloat16 [960], P('shard'), may hold values from 0.5 to 1.5
- norm_mlp: bfloat16 [960], P('shard'), may hold values from 0.5 to 1.5
- qkv_weight: bfloat16 [960, 1600], P('shard'), may hold values from -0.1875 to 0.1875
- out_weight: bfloat16 [960, 960], P('shard'), may hold values from -0.5 to 0.5
- gate_up_weight: bfloat16 [960, 5120], P('shard'), may hold values from -0.1875 to 0.1875
- down_weight: bfloat16 [2560, 960], P('shard'), may hold values from -0.25 to 0.25
Outputs:
- mixed: bfloat16 [49152, 960], P(('replica', 'shard'))
- input_grad: float32 [49152, 960], P(('replica', 'shard'))
- grad_norm_attn: float32 [960], P('shard')
- grad_norm_mlp: float32 [960], P('shard')
- grad_qkv: float32 [960, 1600], P('shard')
- grad_out: float32 [960, 960], P('shard')
- grad_gate_up: float32 [960, 5120], P('shard')
- grad_down: float32 [2560, 960], P('shard')
The draws below stay inside these ranges and needn't reach their ends.
Inputs may be any that keep to these rules, and one draw needn't show every extreme that they name: starts[r] is the first row, counted within the 384 rows of r's device, of the sequence that holds r; sequences are whole on a device; the first device holds one sequence of 384 rows and the last row of all is a sequence of its own.
All inputs are finite; a program needn't handle non-finite values.
Results may differ from the reference program's by a relative error of at most 0.02.
Values may be sent and summed in bfloat16 or wider, within the bound.
A program may use at most 192 MiB of HBM per device.

```python
import jax
import jax.numpy as jnp
from jax import lax

D = 960
QUERY_HEADS = 15
KEY_VALUE_HEADS = 5
HEAD_SIZE = 64
FF = 2560
TOK_DEV = 384
QKV = 1600
TOKENS = 49152


def draw_starts(key, part):
    key = jax.random.fold_in(key, 11)
    token_rows = jnp.arange(TOKENS, dtype=jnp.int32)
    local = token_rows % TOK_DEV
    device = token_rows // TOK_DEV
    coin = jax.random.randint(key, (TOKENS,), 0, 64)
    breaks = (coin == 0) | (local == 0)
    breaks = jnp.where(device == 0, local == 0, breaks)
    breaks = breaks | (token_rows == TOKENS - 1)
    first = lax.cummax(jnp.where(breaks, token_rows, 0), axis=0)
    return (first - device * TOK_DEV).astype(jnp.int32)


def level_of(stream_key, dims, shards, smallest, high):
    level, own = 1.0, jax.random.fold_in(stream_key, 6)
    for dim, parts in shards:
        draws = jnp.exp(jax.random.uniform(jax.random.fold_in(own, dim), (parts,), jnp.float32, smallest / len(shards), high / len(shards)))
        level = level * jnp.repeat(draws, dims[dim] // parts).reshape([-1 if axis == dim else 1 for axis in range(len(dims))])
    return level


def scatter_about(rng, dims, width, most, shards=(), held_as=jnp.bfloat16):
    array = jax.random.normal(rng, dims, jnp.float32) * width
    if len(shards) > 0:
        array = level_of(rng, dims, shards, -0.22, 0.18) * array
    return jnp.clip(array, min=-most, max=most).astype(held_as)


def setup_inputs(seed: int = 0) -> dict:
    splits = jax.random.split(jax.random.key(seed), 10)
    tokens = scatter_about(splits[0], (TOKENS, D), 1.0, 6.0, ((0, 128),))
    starts = draw_starts(jax.random.fold_in(splits[9], 71), 0)
    out_grad = scatter_about(splits[2], (TOKENS, D), 1.0, 6.0, ((0, 128),))
    norm_attn = jnp.clip(1.0 + 0.1 * jax.random.normal(splits[3], (D,), jnp.float32), 0.5, 1.5).astype(jnp.bfloat16)
    norm_mlp = jnp.clip(1.0 + 0.1 * jax.random.normal(splits[4], (D,), jnp.float32), 0.5, 1.5).astype(jnp.bfloat16)
    qkv_weight = scatter_about(splits[5], (D, QKV), D ** -0.5, 0.1875, ((0, 2),))
    out_weight = scatter_about(splits[6], (QUERY_HEADS * HEAD_SIZE, D), (QUERY_HEADS * HEAD_SIZE // 8) ** -0.5, 0.5, ((0, 2),))
    gate_up_weight = scatter_about(splits[7], (D, 2 * FF), D ** -0.5, 0.1875, ((0, 2),))
    down_weight = scatter_about(splits[8], (FF, D), (FF // 4) ** -0.5, 0.25, ((0, 2),))
    return {"tokens": tokens, "starts": starts, "out_grad": out_grad, "norm_attn": norm_attn, "norm_mlp": norm_mlp, "qkv_weight": qkv_weight, "out_weight": out_weight, "gate_up_weight": gate_up_weight, "down_weight": down_weight}


@jax.custom_vjp
def low(v):
    return lax.optimization_barrier(v.astype(jnp.bfloat16)).astype(jnp.float32)

@jax.custom_vjp
def low_back(v):
    return v

def low_keep(v):
    return (low(v), None)

def low_pass(kept, grad):
    return (grad,)

def back_keep(v):
    return (v, None)

def back_low(kept, grad):
    return (low(grad),)
low.defvjp(low_keep, low_pass)
low_back.defvjp(back_keep, back_low)
EPSILON = 1e-05
HIGH = lax.Precision.HIGHEST

def rms_scale(values, gain):
    return values * lax.rsqrt(lax.optimization_barrier(jnp.mean(values * values, axis=-1, keepdims=True)) + EPSILON) * gain

def rope_tables(starts):
    token_rows = jnp.arange(starts.shape[0], dtype=jnp.int32)
    position = (token_rows - starts).astype(jnp.float32)
    half = HEAD_SIZE // 2
    freq = jnp.exp(-jnp.log(jnp.float32(10000.0)) * jnp.arange(half, dtype=jnp.float32) * 2.0 / HEAD_SIZE)
    angle = position[:, None] * freq[None, :]
    return (jnp.cos(angle)[:, None, :], jnp.sin(angle)[:, None, :])

def rotate_halves(values, cosine_table, sine_table):
    half = HEAD_SIZE // 2
    first = values[..., :half]
    second = values[..., half:]
    return jnp.concatenate([first * cosine_table - second * sine_table, second * cosine_table + first * sine_table], axis=-1)

def block(values, starts, gain_one, gain_two, w_qkv, w_out, w_gu, w_down):
    token_rows = values.shape[0]
    group_factor = QUERY_HEADS // KEY_VALUE_HEADS
    hidden_one = low(rms_scale(values, gain_one))
    joint_projection = low_back(jnp.dot(hidden_one, w_qkv, precision=HIGH))
    cosine_table, sine_table = rope_tables(starts)
    query_rows = low(rotate_halves(joint_projection[:, :QUERY_HEADS * HEAD_SIZE].reshape(token_rows, QUERY_HEADS, HEAD_SIZE), cosine_table, sine_table))
    key = low(rotate_halves(joint_projection[:, QUERY_HEADS * HEAD_SIZE:(QUERY_HEADS + KEY_VALUE_HEADS) * HEAD_SIZE].reshape(token_rows, KEY_VALUE_HEADS, HEAD_SIZE), cosine_table, sine_table))
    value_rows = low(joint_projection[:, (QUERY_HEADS + KEY_VALUE_HEADS) * HEAD_SIZE:].reshape(token_rows, KEY_VALUE_HEADS, HEAD_SIZE))
    grouped_query = query_rows.reshape(token_rows, KEY_VALUE_HEADS, group_factor, HEAD_SIZE)
    scores = jnp.einsum('qhgd,khd->hgqk', grouped_query, key, precision=HIGH)
    scores = low_back(scores * HEAD_SIZE ** (-0.5))
    index = jnp.arange(token_rows, dtype=jnp.int32)
    seen = (starts[:, None] == starts[None, :]) & (index[:, None] >= index[None, :])
    scores = jnp.where(seen[None, None], scores, -1e+30)
    probs = jax.nn.softmax(scores, axis=-1)
    attended = jnp.einsum('hgqk,khd->qhgd', low(probs), value_rows, precision=HIGH).reshape(token_rows, QUERY_HEADS * HEAD_SIZE)
    attended = low(low_back(attended))
    mid = values + low_back(jnp.dot(attended, w_out, precision=HIGH))
    hidden_two = low(rms_scale(mid, gain_two))
    gate_up = low_back(jnp.dot(hidden_two, w_gu, precision=HIGH))
    inner = low(jax.nn.silu(gate_up[:, :FF]) * gate_up[:, FF:])
    return mid + low_back(jnp.dot(inner, w_down, precision=HIGH))

def reference(tokens, starts, out_grad, norm_attn, norm_mlp, qkv_weight, out_weight, gate_up_weight, down_weight):
    blocks = TOKENS // TOK_DEV

    def forward(values, gain_one, gain_two, w_qkv, w_out, w_gu, w_down):
        stacked = values.reshape(blocks, TOK_DEV, D)
        starts_blocks = starts.reshape(blocks, TOK_DEV)

        def one_block(pair):
            return block(pair[0], pair[1], gain_one, gain_two, w_qkv, w_out, w_gu, w_down)
        result = lax.map(jax.checkpoint(one_block), (stacked, starts_blocks))
        return result.reshape(TOKENS, D)
    inputs = (tokens.astype(jnp.float32), norm_attn.astype(jnp.float32), norm_mlp.astype(jnp.float32), qkv_weight.astype(jnp.float32), out_weight.astype(jnp.float32), gate_up_weight.astype(jnp.float32), down_weight.astype(jnp.float32))
    output, pullback = jax.vjp(forward, *inputs)
    grads = pullback(out_grad.astype(jnp.float32))
    return (output.astype(jnp.bfloat16), grads[0], grads[1], grads[2], grads[3], grads[4], grads[5], grads[6])
```

```python
import math

import jax
import jax.numpy as jnp
from jax import lax
from jax.experimental import pallas as pl
from jax.experimental.pallas import tpu as pltpu
from jax.sharding import PartitionSpec as P

QUERY_HEADS = 15
KEY_VALUE_HEADS = 5
HEAD_SIZE = 64
FF = 2560


EPSILON = 1e-05


def in_one_piece(arrays, axis, dim, along):
    widths = [math.prod(a.shape[along:]) for a in arrays]
    both = jnp.concatenate(
        [a.reshape(*a.shape[:along], w) for a, w in zip(arrays, widths)], axis=along
    )
    filled = lax.all_gather(both, axis, axis=dim, tiled=True)
    parts = jnp.split(filled, [sum(widths[:k]) for k in range(1, len(widths))], axis=along)
    return tuple(
        (b.reshape(*filled.shape[:along], *a.shape[along:]) for a, b in zip(arrays, parts))
    )


def norm_rows(values, gain):
    scale_inv = lax.rsqrt(jnp.mean(values * values, axis=-1, keepdims=True) + EPSILON)
    normed = values * scale_inv
    return (normed, scale_inv, normed * gain)


def norm_back(grad_scaled, normed, scale_inv, gain):
    grad_gain = jnp.sum(grad_scaled * normed, axis=0)
    grad_normed = grad_scaled * gain
    grad_in = scale_inv * (
        grad_normed - normed * jnp.mean(grad_normed * normed, axis=-1, keepdims=True)
    )
    return (grad_in, grad_gain)


def rope_tables(starts):
    token_rows = jnp.arange(starts.shape[0], dtype=jnp.int32)
    position = (token_rows - starts).astype(jnp.float32)
    half = HEAD_SIZE // 2
    freq = jnp.exp(
        -jnp.log(jnp.float32(10000.0)) * jnp.arange(half, dtype=jnp.float32) * 2.0 / HEAD_SIZE
    )
    angle = position[:, None] * freq[None, :]
    return (jnp.cos(angle)[:, None, :], jnp.sin(angle)[:, None, :])


def rotate_halves(values, cosine_table, sine_table):
    half = HEAD_SIZE // 2
    first = values[..., :half]
    second = values[..., half:]
    return jnp.concatenate(
        [first * cosine_table - second * sine_table, second * cosine_table + first * sine_table],
        axis=-1,
    )


def rotate_back(grads, cosine_table, sine_table):
    half = HEAD_SIZE // 2
    first = grads[..., :half]
    second = grads[..., half:]
    return jnp.concatenate(
        [first * cosine_table + second * sine_table, second * cosine_table - first * sine_table],
        axis=-1,
    )


def transpose_dot(left, right):
    return jnp.einsum("ta,tb->ab", left, right, preferred_element_type=jnp.float32)


MESH = pl.DeviceIdType.MESH
LANES = 128
ROWS = 16
GROUPS = ((4, 3, 3), (3, 4, 3), (3, 3, 3), (3, 3, 4))
DOWN_STRIP = 8
GU_STRIP = 40
QKV_STRIP = 13
OUT_STRIP = 8
GU_FIRST = 16
GAIN_TILE = 30 * QKV_STRIP
OUT_FIRST = 400


def neighbours():
    r = lax.axis_index("replica")
    x = lax.rem(r, 4)
    y = lax.rem(lax.div(r, 4), 4)
    z = lax.div(r, 16)
    out = []
    for place, stride in ((x, 1), (y, 4), (z, 16)):
        ahead = r + stride * (lax.rem(place + 1, 4) - place)
        behind = r + stride * (lax.rem(place + 3, 4) - place)
        out.append((place, ahead, behind))
    return out


def add_into(dst, at, terms, count):
    block = 8 if count % 8 == 0 else count

    def step(i, _):
        o = i * block
        total = dst[pl.ds(at + o, block)].astype(jnp.float32)
        for ref, off in terms:
            total = total + ref[pl.ds(off + o, block)].astype(jnp.float32)
        dst[pl.ds(at + o, block)] = total.astype(jnp.bfloat16)
        return 0

    if count == block:
        step(0, 0)
    else:
        lax.fori_loop(0, count // block, step, 0)


def travel(units, work, extra, final, result, send, recv, back_send, back_recv, started):
    core = lax.axis_index("shard")
    near = neighbours()
    bases = []
    at = 0
    for n in units:
        bases.append(at)
        at += 64 * n
    seg = [jnp.int32(b) for b in bases]
    segs = [[] for _ in units]
    extra_at = 0
    for phase in range(3):
        plan = []
        for color, n in enumerate(units):
            place, ahead, behind = near[(color + phase) % 3]
            chunk = (16, 4, 1)[phase] * n
            first = chunk // 2
            second = chunk - first
            base = seg[color]
            segs[color].append(base)
            xa, xb = extra_at, extra_at + first
            yp, ym = extra_at + chunk, extra_at + 2 * chunk
            extra_at += 3 * chunk
            mine = base + chunk * place
            plus = base + chunk * lax.rem(place + 1, 4)
            minus = base + chunk * lax.rem(place + 3, 4)
            far = base + chunk * lax.rem(place + 2, 4)

            def copy(k, src, count, dst, to, color=color):
                c = pltpu.make_async_remote_copy(
                    src_ref=work.at[pl.ds(src, count)],
                    dst_ref=extra.at[pl.ds(dst, count)],
                    send_sem=send.at[color * 18 + phase * 6 + k],
                    recv_sem=recv.at[color * 18 + phase * 6 + k],
                    device_id=(to, core),
                    device_id_type=MESH,
                )
                started.append(c)
                return c

            s1 = copy(0, far, first, xa, ahead)
            s2 = copy(1, far + first, second, xb, behind)
            s3 = copy(2, plus + first, second, yp + first, ahead)
            s4 = copy(3, minus, first, ym, behind)
            s5 = copy(4, plus, first, yp, ahead)
            s6 = copy(5, minus + first, second, ym + first, behind)
            s1.start()
            s2.start()
            s3.start()
            s4.start()
            plan.append((s1, s2, s3, s4, s5, s6, first, second, chunk, xa, xb, yp, ym, mine, plus, minus))
        yield
        for s1, s2, s3, s4, s5, s6, first, second, chunk, xa, xb, yp, ym, mine, plus, minus in plan:
            s1.wait_recv()
            add_into(work, plus, [(extra, xa)], first)
            s5.start()
            s2.wait_recv()
            add_into(work, minus + first, [(extra, xb)], second)
            s6.start()
        yield
        for color, (s1, s2, s3, s4, s5, s6, first, second, chunk, xa, xb, yp, ym, mine, plus, minus) in enumerate(plan):
            for s in (s3, s4, s5, s6):
                s.wait_recv()
            add_into(work, mine, [(extra, yp), (extra, ym)], chunk)
            seg[color] = mine
    for phase in (2, 1, 0):
        plan = []
        for color, n in enumerate(units):
            place, ahead, behind = near[(color + phase) % 3]
            chunk = (16, 4, 1)[phase] * n
            first = chunk // 2
            second = chunk - first
            base = segs[color][phase]
            mine = base + chunk * place
            plus = base + chunk * lax.rem(place + 1, 4)
            minus = base + chunk * lax.rem(place + 3, 4)

            def copy(k, source, src, count, dst, to, color=color):
                c = pltpu.make_async_remote_copy(
                    src_ref=source.at[pl.ds(src, count)],
                    dst_ref=result.at[pl.ds(dst, count)],
                    send_sem=back_send.at[color * 12 + phase * 4 + k],
                    recv_sem=back_recv.at[color * 12 + phase * 4 + k],
                    device_id=(to, core),
                    device_id_type=MESH,
                )
                started.append(c)
                return c

            source = work if phase == 2 else result
            t1 = copy(0, source, mine, chunk, mine, ahead)
            t2 = copy(1, source, mine, chunk, mine, behind)
            t3 = copy(2, result, minus, first, minus, ahead)
            t4 = copy(3, result, plus + first, second, plus + first, behind)
            t1.start()
            t2.start()
            if phase == 2:
                keep = pltpu.make_async_copy(
                    work.at[pl.ds(mine, chunk)], result.at[pl.ds(mine, chunk)], final.at[color]
                )
                keep.start()
                plan.append((t1, t2, t3, t4, keep))
            else:
                plan.append((t1, t2, t3, t4, None))
        yield
        for t1, t2, t3, t4, keep in plan:
            t1.wait_recv()
            t3.start()
            t2.wait_recv()
            t4.start()
            if keep is not None:
                keep.wait()
        yield
        for t1, t2, t3, t4, keep in plan:
            t3.wait_recv()
            t4.wait_recv()


def reduce_kernel(
    down, gu, qkv, out, gains, res0, res1, res2, res3,
    own_down, own_gu, own_qkv, own_out, own_gain,
    got_down, got_gu, got_qkv, got_out, got_gain,
    w0, w1, w2, w3, e0, e1, e2, e3,
    own_sem, pair_send, pair_recv, send, recv, back_send, back_recv, final,
):
    r = lax.axis_index("replica")
    core = lax.axis_index("shard")
    other = 1 - core
    barrier = pltpu.get_barrier_semaphore()
    pl.semaphore_signal(barrier, inc=1, device_id=(r, other), device_id_type=MESH)
    for _, ahead, behind in neighbours():
        pl.semaphore_signal(barrier, inc=1, device_id=(ahead, core), device_id_type=MESH)
        pl.semaphore_signal(barrier, inc=1, device_id=(behind, core), device_id_type=MESH)
    pl.semaphore_wait(barrier, 7)

    half = GU_FIRST * ROWS
    pieces = (
        (down, own_down, got_down, 1280, 0, 1280),
        (gu, own_gu, got_gu, 480, 0, half),
        (gu, own_gu, got_gu, 480, half, 480 - half),
        (qkv, own_qkv, got_qkv, 480, 0, 480),
        (out, own_out, got_out, 480, 0, 480),
        (gains, own_gain, got_gain, 16, 0, 16),
    )
    started, locals_, pairs = [], [], []
    for k, (full, own, got, rows, skip, count) in enumerate(pieces):
        theirs = pl.multiple_of(other * rows + skip, 16)
        mine = pl.multiple_of(core * rows + skip, 16)
        c = pltpu.make_async_remote_copy(
            src_ref=full.at[pl.ds(theirs, count)],
            dst_ref=got.at[pl.ds(skip, count)],
            send_sem=pair_send.at[k],
            recv_sem=pair_recv.at[k],
            device_id=(r, other),
            device_id_type=MESH,
        )
        c.start()
        started.append(c)
        pairs.append(c)
        o = pltpu.make_async_copy(full.at[pl.ds(mine, count)], own.at[pl.ds(skip, count)], own_sem.at[k])
        o.start()
        locals_.append(o)

    def strips(work, at, own, got, strip, first, count, width):
        def step(i, _):
            rows = pl.ds(pl.multiple_of((first + i) * ROWS, ROWS), ROWS)
            for j in range(strip):
                lanes = min(LANES, width - j * LANES)
                cols = pl.ds(j * LANES, lanes)
                total = own[rows, cols].astype(jnp.float32) + got[rows, cols].astype(jnp.float32)
                work[at + i * strip + j, :, pl.ds(0, lanes)] = total.astype(jnp.bfloat16)
            return 0

        lax.fori_loop(0, count, step, 0)

    def ready(k):
        locals_[k].wait()
        pairs[k].wait_recv()

    def group(g, work, extra, result):
        if g == 0:
            ready(0)
            strips(work, 0, own_down, got_down, DOWN_STRIP, 0, 80, 960)
        if g == 1:
            ready(1)
            strips(work, 0, own_gu, got_gu, GU_STRIP, 0, GU_FIRST, 5120)
        if g == 2:
            ready(2)
            strips(work, 0, own_gu, got_gu, GU_STRIP, GU_FIRST, 30 - GU_FIRST, 5120)
        if g == 3:
            ready(3)
            strips(work, 0, own_qkv, got_qkv, QKV_STRIP, 0, 30, 1600)
            ready(4)
            strips(work, OUT_FIRST, own_out, got_out, OUT_STRIP, 0, 30, 960)
            ready(5)
            work[GAIN_TILE] = (own_gain[...].astype(jnp.float32) + got_gain[...].astype(jnp.float32)).astype(jnp.bfloat16)
        yield from travel(
            GROUPS[g], work, extra, final.at[g], result,
            send.at[g], recv.at[g], back_send.at[g], back_recv.at[g], started,
        )

    gens = [
        group(g, w, e, res)
        for g, (w, e, res) in enumerate(((w0, e0, res0), (w1, e1, res1), (w2, e2, res2), (w3, e3, res3)))
    ]
    live = [True] * 4
    turn = 0
    while any(live):
        for g in range(4):
            if live[g] and turn >= 1 * g:
                try:
                    next(gens[g])
                except StopIteration:
                    live[g] = False
        turn += 1
    for c in started:
        c.wait_send()


def summed_over_chips(down, gu, qkv, out, gains):
    tiles = [64 * sum(u) for u in GROUPS]
    extras = [sum(3 * 21 * n for n in u) for u in GROUPS]
    bf = jnp.bfloat16
    dma = pltpu.SemaphoreType.DMA
    return pl.pallas_call(
        reduce_kernel,
        out_shape=[jax.ShapeDtypeStruct((t, ROWS, LANES), bf) for t in tiles],
        in_specs=[pl.BlockSpec(memory_space=pl.ANY)] * 5,
        out_specs=[pl.BlockSpec(memory_space=pl.ANY)] * 4,
        scratch_shapes=[
            *[pltpu.VMEM(s, bf) for s in ((1280, 960), (480, 5120), (480, 1600), (480, 960), (16, 128))],
            *[pltpu.VMEM(s, bf) for s in ((1280, 960), (480, 5120), (480, 1600), (480, 960), (16, 128))],
            *[pltpu.VMEM((t, ROWS, LANES), bf) for t in tiles],
            *[pltpu.VMEM((t, ROWS, LANES), bf) for t in extras],
            dma((6,)), dma((6,)), dma((6,)),
            dma((4, 54)), dma((4, 54)), dma((4, 36)), dma((4, 36)), dma((4, 3)),
        ],
        compiler_params=pltpu.CompilerParams(
            collective_id=0, has_side_effects=True, vmem_limit_bytes=60 * 1024 * 1024
        ),
        name="sum_over_chips",
    )(down, gu, qkv, out, gains)


def widen_kernel(r0, r1, r2, r3, ro, rg, down, gu, qkv, out, gain):
    i = pl.program_id(0)

    def strip(dst, s, src, tiles, width):
        for j in range(tiles):
            lanes = min(LANES, width - j * LANES)
            dst[pl.ds(s * ROWS, ROWS), pl.ds(j * LANES, lanes)] = src[
                s * tiles + j, :, pl.ds(0, lanes)
            ].astype(jnp.float32)

    for s in range(5):
        strip(down, s, r0, DOWN_STRIP, 960)
    for s in range(2):
        strip(qkv, s, r3, QKV_STRIP, 1600)
        strip(out, s, ro, OUT_STRIP, 960)

    @pl.when(i < 8)
    def _():
        for s in range(2):
            strip(gu, s, r1, GU_STRIP, 5120)

    @pl.when(i >= 8)
    def _():
        for s in range(2):
            strip(gu, s, r2, GU_STRIP, 5120)

    gain[...] = rg[0].astype(jnp.float32)


def widened(r0, r1, r2, r3):
    def tiles(count, index):
        return pl.BlockSpec((count, ROWS, LANES), lambda i: (index(i), 0, 0))

    def late(i):
        return jnp.minimum(i, 14)

    f32 = jnp.float32
    return pl.pallas_call(
        widen_kernel,
        grid=(16,),
        in_specs=[
            tiles(40, lambda i: i),
            tiles(80, lambda i: jnp.minimum(i, 7)),
            tiles(80, lambda i: jnp.clip(i - 8, 0, 6)),
            tiles(26, late),
            tiles(16, lambda i: 25 + late(i)),
            tiles(1, lambda i: GAIN_TILE),
        ],
        out_specs=[
            pl.BlockSpec((80, 960), lambda i: (i, 0)),
            pl.BlockSpec((32, 5120), lambda i: (late(i), 0)),
            pl.BlockSpec((32, 1600), lambda i: (late(i), 0)),
            pl.BlockSpec((32, 960), lambda i: (late(i), 0)),
            pl.BlockSpec((16, 128), lambda i: (0, 0)),
        ],
        out_shape=[
            jax.ShapeDtypeStruct((1280, 960), f32),
            jax.ShapeDtypeStruct((480, 5120), f32),
            jax.ShapeDtypeStruct((480, 1600), f32),
            jax.ShapeDtypeStruct((480, 960), f32),
            jax.ShapeDtypeStruct((16, 128), f32),
        ],
        name="widen",
    )(r0, r1, r2, r3, r3, r3)


def gains_to_tiles(one, two):
    lines = [
        jnp.pad(g.astype(jnp.bfloat16).reshape(2, 480), ((0, 0), (0, 32))).reshape(2, 4, 128)
        for g in (one, two)
    ]
    both = jnp.concatenate(lines, axis=1)
    return jnp.pad(both, ((0, 0), (0, 8), (0, 0))).reshape(32, 128)


def per_device(
    tokens,
    starts,
    out_grad,
    norm_attn,
    norm_mlp,
    qkv_weight,
    out_weight,
    gate_up_weight,
    down_weight,
):
    token_rows = tokens.shape[0]
    group_factor = QUERY_HEADS // KEY_VALUE_HEADS
    scale = HEAD_SIZE ** (-0.5)
    owned = (norm_attn, norm_mlp, qkv_weight, out_weight, gate_up_weight, down_weight)
    gathered = (
        lax.all_gather(owned[0], "shard", axis=0, tiled=True),
        *in_one_piece((owned[1], owned[2], owned[3], owned[4]), "shard", 0, 1),
        lax.all_gather(owned[5], "shard", axis=0, tiled=True),
    )
    gain_one = gathered[0].astype(jnp.float32)
    gain_two = gathered[1].astype(jnp.float32)
    w_qkv, w_out, w_gu, w_down = (gathered[2], gathered[3], gathered[4], gathered[5])
    values = tokens.astype(jnp.float32)
    normed_one, inv_one, scaled_one = norm_rows(values, gain_one)
    hidden_one = scaled_one.astype(jnp.bfloat16)
    joint_projection = jnp.dot(hidden_one, w_qkv, preferred_element_type=jnp.float32)
    cosine_table, sine_table = rope_tables(starts)
    query_rows = rotate_halves(
        joint_projection[:, : QUERY_HEADS * HEAD_SIZE].reshape(token_rows, QUERY_HEADS, HEAD_SIZE),
        cosine_table,
        sine_table,
    ).astype(jnp.bfloat16)
    key_rot = rotate_halves(
        joint_projection[
            :, QUERY_HEADS * HEAD_SIZE : (QUERY_HEADS + KEY_VALUE_HEADS) * HEAD_SIZE
        ].reshape(token_rows, KEY_VALUE_HEADS, HEAD_SIZE),
        cosine_table,
        sine_table,
    ).astype(jnp.bfloat16)
    value_rows = (
        joint_projection[:, (QUERY_HEADS + KEY_VALUE_HEADS) * HEAD_SIZE :]
        .reshape(token_rows, KEY_VALUE_HEADS, HEAD_SIZE)
        .astype(jnp.bfloat16)
    )
    grouped_query = query_rows.reshape(token_rows, KEY_VALUE_HEADS, group_factor, HEAD_SIZE)
    scores = (
        jnp.einsum("qhgd,khd->hgqk", grouped_query, key_rot, preferred_element_type=jnp.float32)
        * scale
    )
    index = jnp.arange(token_rows, dtype=jnp.int32)
    seen = (starts[:, None] == starts[None, :]) & (index[:, None] >= index[None, :])
    scores = jnp.where(seen[None, None], scores, -1e30)
    peak = jnp.max(scores, axis=-1, keepdims=True)
    expo = jnp.exp(scores - peak)
    probs = expo / jnp.sum(expo, axis=-1, keepdims=True)
    probs_low = probs.astype(jnp.bfloat16)
    attended = jnp.einsum(
        "hgqk,khd->qhgd", probs_low, value_rows, preferred_element_type=jnp.float32
    )
    attended = attended.reshape(token_rows, QUERY_HEADS * HEAD_SIZE).astype(jnp.bfloat16)
    mid = values + jnp.dot(attended, w_out, preferred_element_type=jnp.float32)
    normed_two, inv_two, scaled_two = norm_rows(mid, gain_two)
    hidden_two = scaled_two.astype(jnp.bfloat16)
    gate_up = jnp.dot(hidden_two, w_gu, preferred_element_type=jnp.float32)
    gate = gate_up[:, :FF]
    upper = gate_up[:, FF:]
    sigma = jax.nn.sigmoid(gate)
    inner = (gate * sigma * upper).astype(jnp.bfloat16)
    result = mid + jnp.dot(inner, w_down, preferred_element_type=jnp.float32)
    mixed = result.astype(jnp.bfloat16)
    back_one, back_two = (gain_one, gain_two)
    b_qkv, b_out, b_gu, b_down = (w_qkv, w_out, w_gu, w_down)
    grad_down = transpose_dot(inner, out_grad)
    grad_inner = jnp.dot(out_grad, b_down.T, preferred_element_type=jnp.float32)
    grad_upper = grad_inner * gate * sigma
    grad_gate = grad_inner * upper * sigma * (1.0 + gate * (1.0 - sigma))
    grad_gu = jnp.concatenate([grad_gate, grad_upper], axis=1).astype(jnp.bfloat16)
    grad_gate_up = transpose_dot(hidden_two, grad_gu)
    grad_hidden_two = jnp.dot(grad_gu, b_gu.T, preferred_element_type=jnp.float32)
    grad_mid_norm, grad_gain_two = norm_back(grad_hidden_two, normed_two, inv_two, back_two)
    grad_mid = out_grad.astype(jnp.float32) + grad_mid_norm
    grad_attn = grad_mid.astype(jnp.bfloat16)
    grad_out = transpose_dot(attended, grad_attn)
    attended_gradient = jnp.dot(grad_attn, b_out.T, preferred_element_type=jnp.float32).astype(
        jnp.bfloat16
    )
    grouped_gradient = attended_gradient.reshape(
        token_rows, KEY_VALUE_HEADS, group_factor, HEAD_SIZE
    )
    grad_probs = jnp.einsum(
        "qhgd,khd->hgqk", grouped_gradient, value_rows, preferred_element_type=jnp.float32
    )
    value_gradient = jnp.einsum(
        "hgqk,qhgd->khd", probs_low, grouped_gradient, preferred_element_type=jnp.float32
    )
    delta = jnp.sum(grad_probs * probs, axis=-1, keepdims=True)
    grad_scores = (probs * (grad_probs - delta)).astype(jnp.bfloat16)
    grad_query = (
        jnp.einsum("hgqk,khd->qhgd", grad_scores, key_rot, preferred_element_type=jnp.float32)
        * scale
    )
    key_gradient = (
        jnp.einsum("hgqk,qhgd->khd", grad_scores, grouped_query, preferred_element_type=jnp.float32)
        * scale
    )
    grad_query = rotate_back(
        grad_query.reshape(token_rows, QUERY_HEADS, HEAD_SIZE), cosine_table, sine_table
    )
    key_gradient = rotate_back(key_gradient, cosine_table, sine_table)
    grad_joint = jnp.concatenate(
        [
            grad_query.reshape(token_rows, QUERY_HEADS * HEAD_SIZE),
            key_gradient.reshape(token_rows, KEY_VALUE_HEADS * HEAD_SIZE),
            value_gradient.reshape(token_rows, KEY_VALUE_HEADS * HEAD_SIZE),
        ],
        axis=1,
    ).astype(jnp.bfloat16)
    grad_qkv = transpose_dot(hidden_one, grad_joint)
    grad_hidden_one = jnp.dot(grad_joint, b_qkv.T, preferred_element_type=jnp.float32)
    grad_in_norm, grad_gain_one = norm_back(grad_hidden_one, normed_one, inv_one, back_one)
    input_grad = grad_mid + grad_in_norm
    bf = jnp.bfloat16
    sums = summed_over_chips(
        grad_down.astype(bf), grad_gate_up.astype(bf), grad_qkv.astype(bf), grad_out.astype(bf),
        gains_to_tiles(grad_gain_one, grad_gain_two),
    )
    full_down, full_gu, full_qkv, full_out, gain = widened(*sums)
    return (
        mixed,
        input_grad,
        gain[0:4].reshape(512)[:480],
        gain[4:8].reshape(512)[:480],
        full_qkv,
        full_out,
        full_gu,
        full_down,
    )


def solution(mesh):
    return jax.shard_map(
        per_device,
        mesh=mesh,
        in_specs=(
            P(("replica", "shard"), None),
            P(("replica", "shard")),
            P(("replica", "shard"), None),
            P("shard"),
            P("shard"),
            P("shard", None),
            P("shard", None),
            P("shard", None),
            P("shard", None),
        ),
        out_specs=(
            P(("replica", "shard"), None),
            P(("replica", "shard"), None),
            P("shard"),
            P("shard"),
            P("shard", None),
            P("shard", None),
            P("shard", None),
            P("shard", None),
        ),
        check_vma=False,
    )
```

```python
import functools

import jax
import jax.numpy as jnp
from jax import lax
from jax.experimental import pallas as pl
from jax.experimental.pallas import tpu as pltpu
from jax.sharding import PartitionSpec as P

D = 960
HALF = D // 2
QUERY_HEADS = 15
KEY_VALUE_HEADS = 5
GROUP = QUERY_HEADS // KEY_VALUE_HEADS
HEAD_SIZE = 64
FF = 2560
TOK = 384
QKV = 1600
EPSILON = 1e-05
SCALE = HEAD_SIZE**-0.5
HIDDEN = -1e30

MESH = pl.DeviceIdType.MESH
F32 = jnp.float32
BF16 = jnp.bfloat16
LANES = 128
ROWS = 16
BLOCK = 48

FF_CHUNKS = 5
FF_TILES = 384
FF_USED = 360
OUT_BASE = FF_CHUNKS * FF_TILES
OUT_TILES = 256
OUT_USED = 225
QKV_BASE = OUT_BASE + OUT_TILES
QKV_TILES = 384
QKV_USED = 375
GAIN_TILE = 375
TILES = QKV_BASE + QKV_TILES
BOX = 376
UNITS = (2, 2, 2)
OUT_UNITS = (2, 2)
FF_EXTRA = 378
OUT_EXTRA_BASE = FF_CHUNKS * FF_EXTRA
QKV_EXTRA_BASE = OUT_EXTRA_BASE + 252
EXTRA = QKV_EXTRA_BASE + FF_EXTRA
STEPS = 13

OUT_TICK = 2 * FF_CHUNKS
ATTN_TICK = OUT_TICK + 1
LAST_TICK = ATTN_TICK + KEY_VALUE_HEADS
TICKS = LAST_TICK + 1 + STEPS


def mm(a, b):
    return lax.dot_general(a, b, (((1,), (0,)), ((), ())), preferred_element_type=F32)


def mm_nt(a, b):
    return lax.dot_general(a, b, (((1,), (1,)), ((), ())), preferred_element_type=F32)


def neighbours():
    r = lax.axis_index("replica")
    x = lax.rem(r, 4)
    y = lax.rem(lax.div(r, 4), 4)
    z = lax.div(r, 16)
    out = []
    for place, stride in ((x, 1), (y, 4), (z, 16)):
        ahead = r + stride * (lax.rem(place + 1, 4) - place)
        behind = r + stride * (lax.rem(place + 3, 4) - place)
        out.append((place, ahead, behind))
    return out


def add_into(dst, at, terms, count):
    block = 8 if count % 8 == 0 else count

    def step(i, _):
        o = i * block
        total = dst[pl.ds(at + o, block)].astype(F32)
        for ref, off in terms:
            total = total + ref[pl.ds(off + o, block)].astype(F32)
        dst[pl.ds(at + o, block)] = total.astype(BF16)
        return 0

    if count == block:
        step(0, 0)
    else:
        lax.fori_loop(0, count // block, step, 0)


class Travel:
    def __init__(self, work, extra, result, sems, group, base, extra_base, units):
        self.work, self.extra, self.result, self.group = work, extra, result, group
        self.send, self.recv, self.back_send, self.back_recv, self.keep_sem = sems
        core = lax.axis_index("shard")
        near = neighbours()
        self.there, self.back, self.keeps = [[], [], []], [[], [], []], []
        for color, n in enumerate(units):
            seg = base + 64 * n * color
            at = extra_base + 63 * n * color
            for phase in range(3):
                place, ahead, behind = near[(color + phase) % 3]
                chunk = (16, 4, 1)[phase] * n
                first = chunk // 2
                second = chunk - first
                mine = seg + chunk * place
                plus = seg + chunk * lax.rem(place + 1, 4)
                minus = seg + chunk * lax.rem(place + 3, 4)
                far = seg + chunk * lax.rem(place + 2, 4)
                xa, xb, yp, ym = at, at + first, at + chunk, at + 2 * chunk
                at = at + 3 * chunk

                def out(k, src, count, dst, to, color=color, phase=phase):
                    index = color * 18 + phase * 6 + k
                    return pltpu.make_async_remote_copy(
                        src_ref=work.at[pl.ds(src, count)],
                        dst_ref=extra.at[pl.ds(dst, count)],
                        send_sem=self.send.at[group, index],
                        recv_sem=self.recv.at[group, index],
                        device_id=(to, core),
                        device_id_type=MESH,
                    )

                def home(k, source, at, count, to, color=color, phase=phase):
                    index = color * 12 + phase * 4 + k
                    return pltpu.make_async_remote_copy(
                        src_ref=source.at[pl.ds(at, count)],
                        dst_ref=result.at[pl.ds(at, count)],
                        send_sem=self.back_send.at[group, index],
                        recv_sem=self.back_recv.at[group, index],
                        device_id=(to, core),
                        device_id_type=MESH,
                    )

                self.there[phase].append((
                    (
                        lambda out=out, far=far, first=first, xa=xa, to=ahead: out(0, far, first, xa, to),
                        lambda out=out, far=far, first=first, second=second, xb=xb, to=behind: out(1, far + first, second, xb, to),
                        lambda out=out, plus=plus, first=first, second=second, yp=yp, to=ahead: out(2, plus + first, second, yp + first, to),
                        lambda out=out, minus=minus, first=first, ym=ym, to=behind: out(3, minus, first, ym, to),
                        lambda out=out, plus=plus, first=first, yp=yp, to=ahead: out(4, plus, first, yp, to),
                        lambda out=out, minus=minus, first=first, second=second, ym=ym, to=behind: out(5, minus + first, second, ym + first, to),
                    ),
                    (first, second, chunk, xa, xb, yp, ym, mine, plus, minus),
                ))
                source = work if phase == 2 else result
                self.back[phase].append((
                    lambda home=home, source=source, mine=mine, chunk=chunk, to=ahead: home(0, source, mine, chunk, to),
                    lambda home=home, source=source, mine=mine, chunk=chunk, to=behind: home(1, source, mine, chunk, to),
                    lambda home=home, minus=minus, first=first, to=ahead: home(2, result, minus, first, to),
                    lambda home=home, plus=plus, first=first, second=second, to=behind: home(3, result, plus + first, second, to),
                ))
                if phase == 2:
                    self.keeps.append(
                        lambda mine=mine, chunk=chunk, color=color: pltpu.make_async_copy(
                            work.at[pl.ds(mine, chunk)],
                            result.at[pl.ds(mine, chunk)],
                            self.keep_sem.at[group, color],
                        )
                    )
                seg = mine

    def step(self, k):
        if k < 6 and k % 2 == 1:
            for c, (first, second, chunk, xa, xb, yp, ym, mine, plus, minus) in self.there[k // 2]:
                c[0]().wait_recv()
                add_into(self.work, plus, [(self.extra, xa)], first)
                c[4]().start()
                c[1]().wait_recv()
                add_into(self.work, minus + first, [(self.extra, xb)], second)
                c[5]().start()
            return
        if k in (2, 4, 6):
            for c, (first, second, chunk, xa, xb, yp, ym, mine, plus, minus) in self.there[k // 2 - 1]:
                for i in (2, 3, 4, 5):
                    c[i]().wait_recv()
                add_into(self.work, mine, [(self.extra, yp), (self.extra, ym)], chunk)
        if k in (0, 2, 4):
            for c, _ in self.there[k // 2]:
                for i in (0, 1, 2, 3):
                    c[i]().start()
        if k in (7, 9, 11):
            phase = (11 - k) // 2
            for n, c in enumerate(self.back[phase]):
                c[0]().wait_recv()
                c[2]().start()
                c[1]().wait_recv()
                c[3]().start()
                if phase == 2:
                    self.keeps[n]().wait()
        if k in (8, 10, 12):
            for c in self.back[(12 - k) // 2]:
                c[2]().wait_recv()
                c[3]().wait_recv()
        if k in (6, 8, 10):
            phase = (10 - k) // 2
            for n, c in enumerate(self.back[phase]):
                c[0]().start()
                c[1]().start()
                if phase == 2:
                    self.keeps[n]().start()

    def finish(self):
        for phase in range(3):
            for c, _ in self.there[phase]:
                for i in range(6):
                    c[i]().wait_send()
            for c in self.back[phase]:
                for i in range(4):
                    c[i]().wait_send()


def layer_kernel(
    tokens, starts, out_grad, gains, qkv_w, out_w, gu_w, down_w,
    mixed, input_grad, result, gu_far, down_far,
    tok, dyt, dyp, gain_far, wqkv, wout, wg, wd,
    cosine, sine, bias, hbuf, h1t, h2t, qs, ks, vs, ps, os, qt, dot_, ot,
    x1, yacc, dh2, kvt, dqkv, gacc1, gacc2, gain_sum, box, work, extra,
    in_sem, own_sem, load_sem, w_send, w_recv, pair_send, pair_recv, out_sem,
    send, recv, back_send, back_recv, keep_sem,
):
    r = lax.axis_index("replica")
    core = lax.axis_index("shard")
    other = 1 - core
    sems = (send, recv, back_send, back_recv, keep_sem)

    copy_tok = pltpu.make_async_copy(tokens, h2t, in_sem.at[0])
    copy_dy = pltpu.make_async_copy(out_grad, dyt, in_sem.at[1])
    copy_tok.start()
    copy_dy.start()
    mine480 = pl.ds(pl.multiple_of(core * HALF, 16), HALF)
    other480 = pl.ds(pl.multiple_of(other * HALF, 16), HALF)
    own_qkv = pltpu.make_async_copy(qkv_w, wqkv.at[mine480], own_sem.at[0])
    own_out = pltpu.make_async_copy(out_w, wout.at[mine480], own_sem.at[1])
    own_qkv.start()
    own_out.start()

    barrier = pltpu.get_barrier_semaphore()
    pl.semaphore_signal(barrier, inc=1, device_id=(r, other), device_id_type=MESH)
    near = neighbours()
    for _, ahead, behind in near:
        pl.semaphore_signal(barrier, inc=1, device_id=(ahead, core), device_id_type=MESH)
        pl.semaphore_signal(barrier, inc=1, device_id=(behind, core), device_id_type=MESH)
    pl.semaphore_wait(barrier, 1 + 2 * len(near))

    def push(k, src, dst):
        return pltpu.make_async_remote_copy(
            src_ref=src, dst_ref=dst, send_sem=w_send.at[k], recv_sem=w_recv.at[k],
            device_id=(r, other), device_id_type=MESH,
        )

    def ff_push(j):
        out = []
        for q in range(4):
            cols = pl.ds(pl.multiple_of(q * 1280 + j * 256, 256), 256)
            out.append(push(3 + 5 * j + q, gu_w.at[:, cols], gu_far.at[:, cols]))
        cols = pl.ds(pl.multiple_of(j * 256, 256), 256)
        out.append(push(3 + 5 * j + 4, down_w.at[:, cols], down_far.at[:, cols]))
        return out

    push_gain = push(0, gains, gain_far)
    push_qkv = push(1, qkv_w, wqkv.at[mine480])
    push_out = push(2, out_w, wout.at[mine480])
    push_gain.start()
    push_qkv.start()
    push_out.start()
    for j in range(FF_CHUNKS):
        for c in ff_push(j):
            c.start()

    def loads(j):
        slot = lax.rem(j, 2)
        out = []
        for q in range(4):
            cols = pl.ds(pl.multiple_of(q * 1280 + j * 256, 256), 256)
            for i, (src, rows) in enumerate(((gu_w, mine480), (gu_far, other480))):
                out.append(pltpu.make_async_copy(src.at[:, cols], wg.at[slot, q, rows], load_sem.at[slot, 2 * q + i]))
        cols = pl.ds(pl.multiple_of(j * 256, 256), 256)
        out.append(pltpu.make_async_copy(down_w.at[:, cols], wd.at[slot, core], load_sem.at[slot, 8]))
        out.append(pltpu.make_async_copy(down_far.at[:, cols], wd.at[slot, other], load_sem.at[slot, 9]))
        return out

    def start_loads(j):
        for c in ff_push(j):
            c.wait_recv()
        for c in loads(j):
            c.start()

    lane = lax.broadcasted_iota(jnp.int32, (TOK, LANES), 1)
    low = lane < HEAD_SIZE
    early = lax.rem(lane, HEAD_SIZE) < HEAD_SIZE // 2

    def swap(t):
        return jnp.where(early, pltpu.roll(t, LANES - 32, 1), pltpu.roll(t, 32, 1))

    def rope(t):
        return t * cosine[...] + swap(t) * sine[...]

    def rope_back(t):
        return t * cosine[...] - swap(t) * sine[...]

    def transpose(t):
        return jnp.transpose(t.astype(F32)).astype(BF16)

    line = starts[...].astype(F32)
    row = lax.broadcasted_iota(jnp.int32, (TOK, TOK), 0)
    column = lax.broadcasted_iota(jnp.int32, (TOK, TOK), 1)
    across = jnp.broadcast_to(line, (TOK, TOK))
    down_col = jnp.sum(jnp.where(row == column, across, 0.0), axis=1, keepdims=True)
    bias[...] = jnp.where((down_col == across) & (row >= column), 0.0, HIDDEN)
    position = lax.broadcasted_iota(jnp.int32, (TOK, LANES), 0).astype(F32) - down_col
    index = lax.rem(lane, 32).astype(F32)
    freq = jnp.exp(-jnp.log(jnp.full((TOK, LANES), 10000.0, F32)) * index * 2.0 / HEAD_SIZE)
    angle = position * freq
    cosine[...] = jnp.cos(angle)
    sine[...] = jnp.where(early, -jnp.sin(angle), jnp.sin(angle))

    push_gain.wait_recv()

    def gain(k):
        return (gains[k : k + 1, :].astype(F32) + gain_far[k : k + 1, :].astype(F32))[:, :D]

    def rows_of(i):
        return pl.ds(pl.multiple_of(i * BLOCK, BLOCK), BLOCK)

    def normed(x):
        inv = lax.rsqrt(jnp.mean(x * x, axis=-1, keepdims=True) + EPSILON)
        return x * inv, inv

    copy_tok.wait()
    copy_dy.wait()
    for t in range(8):
        w = min(LANES, D - t * LANES)
        place = slice(t * LANES, t * LANES + w)
        tok[:, place] = transpose(h2t[place, :])
        dyp[:, place] = transpose(dyt[place, :])

    def norm_one(i, _):
        rows = rows_of(i)
        n, _inv = normed(tok[rows, :].astype(F32))
        hbuf[rows, :] = (n * gain(0)).astype(BF16)
        return 0

    lax.fori_loop(0, TOK // BLOCK, norm_one, 0)

    def transposed(dst, src):
        for t in range(8):
            w = min(LANES, D - t * LANES)
            dst[t * LANES : t * LANES + w, :] = transpose(src[:, t * LANES : t * LANES + w])

    transposed(h1t, hbuf)

    own_qkv.wait()
    push_qkv.wait_recv()
    for n0 in range(0, QKV, 256):
        width = min(256, QKV - n0)
        joint = mm(hbuf[...], wqkv[:, n0 : n0 + width])
        for c0 in range(0, width, LANES):
            t = (n0 + c0) // LANES
            if c0 + LANES <= width:
                tile = joint[:, c0 : c0 + LANES]
            else:
                piece = joint[:, c0:width]
                tile = jnp.concatenate([piece, piece], axis=1)
            turned = rope(tile) if t < 10 else tile
            if t < 8:
                flipped = transpose(turned)
                w = min(LANES, D - t * LANES)
                qt[t * LANES : t * LANES + w, :] = flipped[:w]
            for part in range(2):
                b = 2 * t + part
                here = low if part == 0 else jnp.logical_not(low)
                if b < QUERY_HEADS:
                    qs[b] = jnp.where(here, turned, 0.0).astype(BF16)
                elif b < QUERY_HEADS + 2 * KEY_VALUE_HEADS:
                    both = jnp.where(here, turned, pltpu.roll(turned, HEAD_SIZE, 1)).astype(BF16)
                    if b < QUERY_HEADS + KEY_VALUE_HEADS:
                        ks[b - QUERY_HEADS] = both
                    else:
                        vs[b - QUERY_HEADS - KEY_VALUE_HEADS] = both

    def attend(g, _):
        for i in range(GROUP):
            h = GROUP * g + i
            s = mm_nt(qs[h], ks[g]) * SCALE + bias[...]
            e = jnp.exp(s - jnp.max(s, axis=-1, keepdims=True))
            p = (e * (1.0 / jnp.sum(e, axis=-1, keepdims=True))).astype(BF16)
            ps[h] = p
            os[h] = mm(p, vs[g]).astype(BF16)
        return 0

    lax.fori_loop(0, KEY_VALUE_HEADS, attend, 0)

    def pair_tile(t):
        a = os[2 * t].astype(F32)
        if 2 * t + 1 < QUERY_HEADS:
            a = jnp.where(low, a, os[2 * t + 1].astype(F32))
        return a

    for t in range(8):
        w = min(LANES, D - t * LANES)
        tile = pair_tile(t)
        hbuf[:, t * LANES : t * LANES + w] = tile[:, :w].astype(BF16)
        ot[t * LANES : t * LANES + w, :] = jnp.transpose(tile).astype(BF16)[:w]

    own_out.wait()
    push_out.wait_recv()
    for n0 in range(0, D, 256):
        cols = slice(n0, min(D, n0 + 256))
        x1[:, cols] = tok[:, cols].astype(F32) + mm(hbuf[...], wout[:, cols])

    start_loads(0)
    start_loads(1)

    def norm_two(i, _):
        rows = rows_of(i)
        x = x1[rows, :]
        n, _inv = normed(x)
        hbuf[rows, :] = (n * gain(1)).astype(BF16)
        yacc[rows, :] = x
        dh2[rows, :] = jnp.zeros((BLOCK, D), F32)
        return 0

    lax.fori_loop(0, TOK // BLOCK, norm_two, 0)
    transposed(h2t, hbuf)

    def pair(k, slot, first, count, base):
        return pltpu.make_async_remote_copy(
            src_ref=box.at[slot, other, pl.ds(first, count)],
            dst_ref=work.at[pl.ds(base + first, count)],
            send_sem=pair_send.at[k],
            recv_sem=pair_recv.at[k],
            device_id=(r, other),
            device_id_type=MESH,
        )

    def tile_columns(slot, half, at, value, count):
        for c in range(count):
            block = value[:, c * LANES : (c + 1) * LANES]
            n = block.shape[0] // ROWS
            box[slot, half, pl.ds(at + c * n, n)] = block.astype(BF16).reshape(n, ROWS, LANES)

    def folded(value):
        n = value.shape[0] // 2
        left = lax.broadcasted_iota(jnp.int32, (n, LANES), 1) < HEAD_SIZE
        return jnp.where(left, value[:n], value[n:])

    def feed_forward(tick):
        j, s = lax.div(tick, 2), lax.rem(tick, 2)
        slot = lax.rem(j, 2)

        @pl.when(s == 0)
        def _():
            for c in loads(j):
                c.wait()

        gate = mm(hbuf[...], wg[slot, s])
        upper = mm(hbuf[...], wg[slot, 2 + s])
        grad = mm(dyp[:, :D], wd[slot, s])
        sigma = jax.nn.sigmoid(gate)
        silu = gate * sigma
        inner_low = (silu * upper).astype(BF16)
        dgate = (grad * upper * sigma * (1.0 + gate * (1.0 - sigma))).astype(BF16)
        dupper = (grad * silu).astype(BF16)
        yacc[...] += mm_nt(inner_low, wd[slot, s])
        dh2[...] += mm_nt(dgate, wg[slot, s]) + mm_nt(dupper, wg[slot, 2 + s])
        for half in range(2):
            left = h2t[half * HALF : (half + 1) * HALF, :]
            tile_columns(slot, half, s * 120, mm(left, dgate), 2)
            tile_columns(slot, half, s * 120 + 60, mm(left, dupper), 2)
        tile_columns(slot, s, 240, mm(dyt[...], inner_low), 2)

        @pl.when(s == 1)
        def _():
            pair(j, slot, 0, FF_USED, j * FF_TILES).start()

            @pl.when(j + 2 < FF_CHUNKS)
            def _():
                start_loads(j + 2)

    def gain_rows(value):
        return jnp.sum(value.reshape(BLOCK // 8, 8, D), axis=0)

    def output_projection():
        gacc2[...] = jnp.zeros((8, D), F32)

        def back_two(i, _):
            rows = rows_of(i)
            n, inv = normed(x1[rows, :])
            d = dh2[rows, :]
            gacc2[...] += gain_rows(d * n)
            dn = d * gain(1)
            dx = dyp[rows, :D].astype(F32) + inv * (dn - n * jnp.mean(dn * n, axis=-1, keepdims=True))
            dh2[rows, :] = dx
            da = dx.astype(BF16)
            dyp[rows, : 7 * LANES] = da[:, : 7 * LANES]
            last = da[:, 7 * LANES :]
            dyp[rows, 7 * LANES :] = jnp.concatenate([last, last], axis=1)
            return 0

        lax.fori_loop(0, TOK // BLOCK, back_two, 0)
        transposed(h2t, yacc)
        pltpu.make_async_copy(h2t, mixed, out_sem.at[0]).start()
        for half in range(2):
            v = mm(ot[half * HALF : (half + 1) * HALF, :], dyp[...])
            tile_columns(1, half, 0, v, 7)
            tile_columns(1, half, 210, folded(v[:, 7 * LANES :]), 1)
        pair(5, 1, 0, OUT_USED, OUT_BASE).start()
        for n0 in range(0, D, 256):
            width = min(256, D - n0)
            v = mm_nt(dyp[:, :D], wout[n0 : n0 + width, :])
            for c0 in range(0, width, LANES):
                t = (n0 + c0) // LANES
                if c0 + LANES <= width:
                    tile = v[:, c0 : c0 + LANES]
                else:
                    piece = v[:, c0:width]
                    tile = jnp.concatenate([piece, piece], axis=1)
                w = min(LANES, D - t * LANES)
                dot_[t * LANES : t * LANES + w, :] = transpose(tile)[:w]
                qs[2 * t] = jnp.where(low, tile, 0.0).astype(BF16)
                if 2 * t + 1 < QUERY_HEADS:
                    qs[2 * t + 1] = jnp.where(low, 0.0, tile).astype(BF16)

    def attend_back(g):
        key_t = jnp.zeros((HEAD_SIZE, TOK), F32)
        value_t = jnp.zeros((HEAD_SIZE, TOK), F32)
        for i in range(GROUP):
            h = GROUP * g + i
            dp = mm_nt(qs[h], vs[g])
            low_p = ps[h]
            p = low_p.astype(F32)
            delta = jnp.sum(dp * p, axis=-1, keepdims=True)
            ds = (p * (dp - delta)).astype(BF16)
            os[h] = rope_back(mm(ds, ks[g]) * SCALE).astype(BF16)
            rows = pl.ds(pl.multiple_of(h * HEAD_SIZE, HEAD_SIZE), HEAD_SIZE)
            key_t = key_t + mm(qt[rows, :], ds)
            value_t = value_t + mm(dot_[rows, :], low_p)
        kvt[pl.ds(pl.multiple_of(HEAD_SIZE * (1 + g), HEAD_SIZE), HEAD_SIZE), :] = key_t * SCALE
        kvt[pl.ds(pl.multiple_of(HEAD_SIZE * (6 + g), HEAD_SIZE), HEAD_SIZE), :] = value_t
        kvt[HEAD_SIZE * 11 : HEAD_SIZE * 12, :] = value_t

    def joint_projection():
        for t in range(13):
            if t < 7:
                tile = pair_tile(t)
            else:
                tile = jnp.transpose(kvt[(t - 7) * LANES : (t - 6) * LANES, :])
                if t < 10:
                    tile = rope_back(tile)
                if t == 7:
                    tile = jnp.where(low, pair_tile(7), tile)
            dqkv[:, t * LANES : (t + 1) * LANES] = tile.astype(BF16)
        for half in range(2):
            left = h1t[half * HALF : (half + 1) * HALF, :]
            for n0 in range(0, 1536, 256):
                v = mm(left, dqkv[:, n0 : n0 + 256])
                tile_columns(0, half, n0 // LANES * 30, v, 2)
            v = mm(left, dqkv[:, 1536:])
            tile_columns(0, half, 360, folded(v), 1)
        pair(6, 0, 0, QKV_USED, QKV_BASE).start()
        for n0 in range(0, D, 256):
            cols = slice(n0, min(D, n0 + 256))
            yacc[:, cols] = mm_nt(dqkv[:, :QKV], wqkv[cols, :])
        gacc1[...] = jnp.zeros((8, D), F32)

        def back_one(i, _):
            rows = rows_of(i)
            n, inv = normed(tok[rows, :].astype(F32))
            d = yacc[rows, :]
            gacc1[...] += gain_rows(d * n)
            dn = d * gain(0)
            dh2[rows, :] += inv * (dn - n * jnp.mean(dn * n, axis=-1, keepdims=True))
            return 0

        lax.fori_loop(0, TOK // BLOCK, back_one, 0)
        for t in range(8):
            place = slice(t * LANES, min(D, (t + 1) * LANES))
            kvt[place, :] = jnp.transpose(dh2[:, place])
        pltpu.make_async_copy(kvt, input_grad, out_sem.at[1]).start()
        gain_sum[...] = jnp.zeros((ROWS, LANES), F32)
        for k, acc in enumerate((gacc1, gacc2)):
            total = jnp.sum(acc[...], axis=0, keepdims=True)
            for t in range(8):
                w = min(LANES, D - t * LANES)
                gain_sum[8 * k + t : 8 * k + t + 1, :w] = total[:, t * LANES : t * LANES + w]
        for half in range(2):
            box[0, half, GAIN_TILE] = gain_sum[...].astype(BF16)
        pair(7, 0, GAIN_TILE, 1, QKV_BASE).start()

    def add_own(slot, base, count):
        def step(i, _):
            o = i * 5
            total = work[pl.ds(base + o, 5)].astype(F32) + box[slot, core, pl.ds(o, 5)].astype(F32)
            work[pl.ds(base + o, 5)] = total.astype(BF16)
            return 0

        lax.fori_loop(0, count // 5, step, 0)

    ff_travel = functools.partial(Travel, work, extra, result, sems)

    def of_ff(g):
        return ff_travel(g, g * FF_TILES, g * FF_EXTRA, UNITS)

    of_out = ff_travel(5, OUT_BASE, OUT_EXTRA_BASE, OUT_UNITS)
    of_qkv = ff_travel(6, QKV_BASE, QKV_EXTRA_BASE, UNITS)

    def travel(tick):
        for k in range(STEPS - 1, -1, -1):
            since = tick - 2 - k

            @pl.when((since >= 0) & (since <= 2 * FF_CHUNKS - 2) & (lax.rem(since + 64, 2) == 0))
            def _(k=k, since=since):
                g = lax.div(since, 2)
                if k == 0:
                    c = pair(g, lax.rem(g, 2), 0, FF_USED, g * FF_TILES)
                    c.wait()
                    add_own(lax.rem(g, 2), g * FF_TILES, FF_USED)
                of_ff(g).step(k)

        @pl.when(tick > OUT_TICK)
        def _():
            for k in range(STEPS):

                @pl.when(tick == OUT_TICK + 1 + k)
                def _(k=k):
                    if k == 0:
                        pair(5, 1, 0, OUT_USED, OUT_BASE).wait()
                        add_own(1, OUT_BASE, OUT_USED)
                    of_out.step(k)

        @pl.when(tick > LAST_TICK)
        def _():
            for k in range(STEPS):

                @pl.when(tick == LAST_TICK + 1 + k)
                def _(k=k):
                    if k == 0:
                        pair(6, 0, 0, QKV_USED, QKV_BASE).wait()
                        add_own(0, QKV_BASE, QKV_USED)
                        pair(7, 0, GAIN_TILE, 1, QKV_BASE).wait()
                        at = QKV_BASE + GAIN_TILE
                        work[at] = (work[at].astype(F32) + box[0, core, GAIN_TILE].astype(F32)).astype(BF16)
                    of_qkv.step(k)

    def tick_body(tick, _):
        @pl.when(tick < OUT_TICK)
        def _():
            feed_forward(tick)

        @pl.when(tick == OUT_TICK)
        def _():
            output_projection()

        @pl.when((tick >= ATTN_TICK) & (tick < LAST_TICK))
        def _():
            attend_back(tick - ATTN_TICK)

        @pl.when(tick == LAST_TICK)
        def _():
            joint_projection()

        travel(tick)
        return 0

    lax.fori_loop(0, TICKS, tick_body, 0)

    pltpu.make_async_copy(h2t, mixed, out_sem.at[0]).wait()
    pltpu.make_async_copy(kvt, input_grad, out_sem.at[1]).wait()
    push_gain.wait_send()
    push_qkv.wait_send()
    push_out.wait_send()

    def finish(g, _):
        for c in ff_push(g):
            c.wait_send()
        of_ff(g).finish()
        return 0

    lax.fori_loop(0, FF_CHUNKS, finish, 0)
    of_out.finish()
    of_qkv.finish()


def layer(tokens, starts, out_grad, gains, qkv_w, out_w, gu_w, down_w):
    vm = pltpu.VMEM
    dma = pltpu.SemaphoreType.DMA
    hbm = pl.BlockSpec(memory_space=pl.ANY)
    near = pl.BlockSpec(memory_space=pltpu.VMEM)
    shape = jax.ShapeDtypeStruct
    return pl.pallas_call(
        layer_kernel,
        out_shape=[
            shape((D, TOK), BF16),
            shape((D, TOK), F32),
            shape((TILES, ROWS, LANES), BF16),
            shape((HALF, 2 * FF), BF16),
            shape((D, FF // 2), BF16),
        ],
        in_specs=[hbm, near, hbm, near, hbm, hbm, hbm, hbm],
        out_specs=[hbm] * 5,
        scratch_shapes=[
            vm((TOK, D), BF16),
            vm((D, TOK), BF16),
            vm((TOK, 1024), BF16),
            vm((16, 1024), BF16),
            vm((D, QKV), BF16),
            vm((D, D), BF16),
            vm((2, 4, D, 256), BF16),
            vm((2, 2, D, 256), BF16),
            vm((TOK, LANES), F32),
            vm((TOK, LANES), F32),
            vm((TOK, TOK), F32),
            vm((TOK, D), BF16),
            vm((D, TOK), BF16),
            vm((D, TOK), BF16),
            vm((QUERY_HEADS, TOK, LANES), BF16),
            vm((KEY_VALUE_HEADS, TOK, LANES), BF16),
            vm((KEY_VALUE_HEADS, TOK, LANES), BF16),
            vm((QUERY_HEADS, TOK, TOK), BF16),
            vm((QUERY_HEADS, TOK, LANES), BF16),
            vm((D, TOK), BF16),
            vm((D, TOK), BF16),
            vm((D, TOK), BF16),
            vm((TOK, D), F32),
            vm((TOK, D), F32),
            vm((TOK, D), F32),
            vm((D, TOK), F32),
            vm((TOK, 13 * LANES), BF16),
            vm((8, D), F32),
            vm((8, D), F32),
            vm((ROWS, LANES), F32),
            vm((2, 2, BOX, ROWS, LANES), BF16),
            vm((TILES, ROWS, LANES), BF16),
            vm((EXTRA, ROWS, LANES), BF16),
            dma((2,)), dma((2,)), dma((2, 10)),
            dma((28,)), dma((28,)), dma((8,)), dma((8,)), dma((2,)),
            dma((7, 54)), dma((7, 54)), dma((7, 36)), dma((7, 36)), dma((7, 3)),
        ],
        compiler_params=pltpu.CompilerParams(
            collective_id=0, has_side_effects=True, vmem_limit_bytes=VMEM_LIMIT
        ),
        name="layer",
    )(tokens, starts, out_grad, gains, qkv_w, out_w, gu_w, down_w)


VMEM_LIMIT = 64 * 1024 * 1024 - 256 * 1024


def widen_kernel(
    res, mixed_in, grad_in, down, gu, qkv, out, gain, mixed, grad,
    rv, down_v, gu_v, qkv_v, out_v, in_sem, out_sem, pass_sem,
):
    bounds = [FF_TILES * j for j in range(FF_CHUNKS)] + [OUT_BASE, QKV_BASE]
    counts = [FF_USED] * FF_CHUNKS + [OUT_USED, QKV_USED + 1]
    loads = [
        pltpu.make_async_copy(res.at[pl.ds(b, n)], rv.at[pl.ds(b, n)], in_sem.at[i])
        for i, (b, n) in enumerate(zip(bounds, counts))
    ]
    for c in loads:
        c.start()
    passed = [
        pltpu.make_async_copy(mixed_in, mixed, pass_sem.at[0]),
        pltpu.make_async_copy(grad_in, grad, pass_sem.at[1]),
    ]
    for c in passed:
        c.start()
    stores = []

    def store(src, dst):
        c = pltpu.make_async_copy(src, dst, out_sem.at[len(stores)])
        c.start()
        stores.append(c)

    def column(at, n):
        return rv[pl.ds(at, n)].astype(F32).reshape(n * ROWS, LANES)

    def last_column(at, n):
        both = column(at, n)
        return both[:, :HEAD_SIZE], pltpu.roll(both, HEAD_SIZE, 1)[:, :HEAD_SIZE]

    for j in range(FF_CHUNKS):
        loads[j].wait()
        base = FF_TILES * j
        for s in range(2):
            for w in range(2):
                first = w * FF + s * 1280 + j * 256
                for c in range(2):
                    gu_v[:, first + c * LANES : first + (c + 1) * LANES] = column(base + (s * 2 + w) * 60 + c * 30, 30)
                cols = pl.ds(first, 256)
                store(gu_v.at[:, cols], gu.at[:, cols])
        first = 256 * j
        for c in range(2):
            down_v[:, first + c * LANES : first + (c + 1) * LANES] = column(base + 240 + c * 60, 60)
        cols = pl.ds(first, 256)
        store(down_v.at[:, cols], down.at[:, cols])
    loads[5].wait()
    for c in range(7):
        out_v[:, c * LANES : (c + 1) * LANES] = column(OUT_BASE + c * 30, 30)
    a, b = last_column(OUT_BASE + 210, 15)
    out_v[:240, 7 * LANES :] = a
    out_v[240:, 7 * LANES :] = b
    store(out_v, out)
    loads[6].wait()
    for c in range(12):
        qkv_v[:, c * LANES : (c + 1) * LANES] = column(QKV_BASE + c * 30, 30)
    a, b = last_column(QKV_BASE + 360, 15)
    qkv_v[:240, 12 * LANES :] = a
    qkv_v[240:, 12 * LANES :] = b
    store(qkv_v, qkv)
    gain[...] = rv[QKV_BASE + GAIN_TILE].astype(F32)
    for c in stores:
        c.wait()
    for c in passed:
        c.wait()


def widened(result, mixed, grad):
    vm = pltpu.VMEM
    dma = pltpu.SemaphoreType.DMA
    hbm = pl.BlockSpec(memory_space=pl.ANY)
    shape = jax.ShapeDtypeStruct
    sizes = [(D, FF // 2), (HALF, 2 * FF), (HALF, QKV), (HALF, D)]
    return pl.pallas_call(
        widen_kernel,
        out_shape=[shape(s, F32) for s in sizes]
        + [shape((ROWS, LANES), F32), shape((D, TOK), BF16), shape((D, TOK), F32)],
        in_specs=[hbm] * 3,
        out_specs=[hbm] * 4 + [pl.BlockSpec(memory_space=vm), hbm, hbm],
        scratch_shapes=[
            vm((TILES, ROWS, LANES), BF16),
            *[vm(s, F32) for s in sizes],
            dma((7,)), dma((27,)), dma((2,)),
        ],
        compiler_params=pltpu.CompilerParams(vmem_limit_bytes=48 * 1024 * 1024),
        name="widen",
    )(result, mixed, grad)


def per_device(
    tokens, starts, out_grad, norm_attn, norm_mlp, qkv_weight, out_weight, gate_up_weight, down_weight
):
    core = lax.axis_index("shard")
    both = jnp.stack([norm_attn, norm_mlp])
    gains = jnp.where(
        core == 0, jnp.pad(both, ((0, 14), (0, 544))), jnp.pad(both, ((0, 14), (HALF, 64)))
    )
    mixed, input_grad, result, _, _ = layer(
        tokens.T, starts.reshape(1, TOK), out_grad.T, gains, qkv_weight, out_weight, gate_up_weight, down_weight.T
    )
    down, gu, qkv, out, gain, mixed, input_grad = widened(result, mixed, input_grad)
    first = core * HALF
    gain_one = lax.dynamic_slice(gain[:8].reshape(1024), (first,), (HALF,))
    gain_two = lax.dynamic_slice(gain[8:].reshape(1024), (first,), (HALF,))
    return mixed.T, input_grad.T, gain_one, gain_two, qkv, out, gu, down.T


def solution(mesh):
    rows, weights = P(("replica", "shard"), None), P("shard", None)
    return jax.shard_map(
        per_device,
        mesh=mesh,
        in_specs=(
            rows, P(("replica", "shard")), rows, P("shard"), P("shard"), weights, weights, weights, weights,
        ),
        out_specs=(rows, rows, P("shard"), P("shard"), weights, weights, weights, weights),
        check_vma=False,
    )
```

```python
import functools

import jax
import jax.numpy as jnp
from jax import lax
from jax.experimental import pallas as pl
from jax.experimental.pallas import tpu as pltpu
from jax.sharding import PartitionSpec as P

D = 960
HALF = D // 2
QUERY_HEADS = 15
KEY_VALUE_HEADS = 5
GROUP = QUERY_HEADS // KEY_VALUE_HEADS
HEAD_SIZE = 64
FF = 2560
TOK = 384
QKV = 1600
EPSILON = 1e-05
SCALE = HEAD_SIZE**-0.5
HIDDEN = -1e30

MESH = pl.DeviceIdType.MESH
F32 = jnp.float32
BF16 = jnp.bfloat16
LANES = 128
ROWS = 16
BLOCK = 48

FF_CHUNKS = 5
FF_TILES = 384
FF_USED = 360
OUT_BASE = FF_CHUNKS * FF_TILES
OUT_TILES = 256
OUT_USED = 225
QKV_BASE = OUT_BASE + OUT_TILES
QKV_TILES = 384
QKV_USED = 375
GAIN_TILE = 375
TILES = QKV_BASE + QKV_TILES
BOX = 376
UNITS = (2, 2, 2)
OUT_UNITS = (2, 2)
FF_EXTRA = 378
OUT_EXTRA_BASE = FF_CHUNKS * FF_EXTRA
QKV_EXTRA_BASE = OUT_EXTRA_BASE + 252
EXTRA = QKV_EXTRA_BASE + FF_EXTRA
FF_HOPS = (2, 1, 1)
OUT_HOPS = (2, 1, 1)
QKV_HOPS = (2, 1, 1)


def steps_of(hops):
    return 7 + 2 * sum(h - 1 for h in hops)


OUT_TICK = 2 * FF_CHUNKS
ATTN_TICK = OUT_TICK + 1
LAST_TICK = ATTN_TICK + KEY_VALUE_HEADS
TICKS = max(2 * FF_CHUNKS + 2 * steps_of(FF_HOPS) - 1, LAST_TICK + 1 + steps_of(QKV_HOPS))


def mm(a, b):
    return lax.dot_general(a, b, (((1,), (0,)), ((), ())), preferred_element_type=F32)


def mm_nt(a, b):
    return lax.dot_general(a, b, (((1,), (1,)), ((), ())), preferred_element_type=F32)


def neighbours():
    r = lax.axis_index("replica")
    x = lax.rem(r, 4)
    y = lax.rem(lax.div(r, 4), 4)
    z = lax.div(r, 16)
    out = []
    for place, stride in ((x, 1), (y, 4), (z, 16)):
        ahead = r + stride * (lax.rem(place + 1, 4) - place)
        behind = r + stride * (lax.rem(place + 3, 4) - place)
        across = r + stride * (lax.rem(place + 2, 4) - place)
        out.append((place, ahead, behind, across))
    return out


def add_into(dst, at, terms, count):
    block = 8 if count % 8 == 0 else count

    def step(i, _):
        o = i * block
        total = dst[pl.ds(at + o, block)].astype(F32)
        for ref, off in terms:
            total = total + ref[pl.ds(off + o, block)].astype(F32)
        dst[pl.ds(at + o, block)] = total.astype(BF16)
        return 0

    if count == block:
        step(0, 0)
    else:
        lax.fori_loop(0, count // block, step, 0)


class Travel:
    def __init__(self, work, extra, result, sems, group, base, extra_base, units, hops):
        self.work, self.extra, self.result = work, extra, result
        send, recv, back_send, back_recv, keep_sem = sems
        self.hops = hops
        core = lax.axis_index("shard")
        near = neighbours()
        self.there, self.back, self.keeps = [[], [], []], [[], [], []], []
        for color, n in enumerate(units):
            seg = base + 64 * n * color
            at = extra_base + 63 * n * color
            for phase in range(3):
                place, ahead, behind, across = near[(color + phase) % 3]
                chunk = (16, 4, 1)[phase] * n
                first = chunk // 2
                second = chunk - first
                mine = seg + chunk * place
                plus = seg + chunk * lax.rem(place + 1, 4)
                minus = seg + chunk * lax.rem(place + 3, 4)
                far = seg + chunk * lax.rem(place + 2, 4)
                xa, xb, yp, ym = at, at + first, at + chunk, at + 2 * chunk
                at = at + 3 * chunk

                def out(k, src, count, dst, to, color=color, phase=phase):
                    index = color * 18 + phase * 6 + k
                    return lambda: pltpu.make_async_remote_copy(
                        src_ref=work.at[pl.ds(src, count)],
                        dst_ref=extra.at[pl.ds(dst, count)],
                        send_sem=send.at[group, index],
                        recv_sem=recv.at[group, index],
                        device_id=(to, core),
                        device_id_type=MESH,
                    )

                def home(k, source, at, count, to, color=color, phase=phase):
                    index = color * 12 + phase * 4 + k
                    return lambda: pltpu.make_async_remote_copy(
                        src_ref=source.at[pl.ds(at, count)],
                        dst_ref=result.at[pl.ds(at, count)],
                        send_sem=back_send.at[group, index],
                        recv_sem=back_recv.at[group, index],
                        device_id=(to, core),
                        device_id_type=MESH,
                    )

                source = work if phase == 2 else result
                if hops[phase] == 2:
                    copies = (
                        out(0, far, first, xa, ahead),
                        out(1, far + first, second, xb, behind),
                        out(2, plus + first, second, yp + first, ahead),
                        out(3, minus, first, ym, behind),
                        out(4, plus, first, yp, ahead),
                        out(5, minus + first, second, ym + first, behind),
                    )
                    backs = (
                        home(0, source, mine, chunk, ahead),
                        home(1, source, mine, chunk, behind),
                        home(2, result, minus, first, ahead),
                        home(3, result, plus + first, second, behind),
                    )
                else:
                    copies = (
                        out(0, far, chunk, xa, across),
                        out(1, plus, chunk, yp, ahead),
                        out(2, minus, chunk, ym, behind),
                    )
                    backs = (
                        home(0, source, mine, chunk, across),
                        home(1, source, mine, chunk, ahead),
                        home(2, source, mine, chunk, behind),
                    )
                self.there[phase].append((copies, (first, second, chunk, xa, xb, yp, ym, mine, plus, minus)))
                self.back[phase].append(backs)
                if phase == 2:
                    self.keeps.append(
                        lambda mine=mine, chunk=chunk, color=color: pltpu.make_async_copy(
                            work.at[pl.ds(mine, chunk)],
                            result.at[pl.ds(mine, chunk)],
                            keep_sem.at[group, color],
                        )
                    )
                seg = mine

    def start(self, phase):
        for c, _ in self.there[phase]:
            for i in range(4 if self.hops[phase] == 2 else 3):
                c[i]().start()

    def mid(self, phase):
        for c, (first, second, chunk, xa, xb, yp, ym, mine, plus, minus) in self.there[phase]:
            c[0]().wait_recv()
            add_into(self.work, plus, [(self.extra, xa)], first)
            c[4]().start()
            c[1]().wait_recv()
            add_into(self.work, minus + first, [(self.extra, xb)], second)
            c[5]().start()

    def end(self, phase, color):
        c, (first, second, chunk, xa, xb, yp, ym, mine, plus, minus) = self.there[phase][color]
        terms = [(self.extra, yp), (self.extra, ym)]
        if self.hops[phase] == 2:
            waits = c[2:]
        else:
            waits = c
            terms.append((self.extra, xa))
        for w in waits:
            w().wait_recv()
        add_into(self.work, mine, terms, chunk)

    def back_start(self, phase, color):
        c = self.back[phase][color]
        for i in range(2 if self.hops[phase] == 2 else 3):
            c[i]().start()
        if phase == 2:
            self.keeps[color]().start()

    def back_mid(self, phase):
        for c in self.back[phase]:
            c[0]().wait_recv()
            c[2]().start()
            c[1]().wait_recv()
            c[3]().start()

    def back_end(self, phase, color):
        c = self.back[phase][color]
        for w in c[2:] if self.hops[phase] == 2 else c:
            w().wait_recv()
        if phase == 2:
            self.keeps[color]().wait()

    def step(self, k):
        colors = range(len(self.keeps))
        steps = [[("start", 0)]]
        for phase in range(3):
            if self.hops[phase] == 2:
                steps.append([("mid", phase)])
            steps.append([("turn", phase)])
        for phase in (2, 1, 0):
            if self.hops[phase] == 2:
                steps.append([("back_mid", phase)])
            steps.append([("back_turn", phase)])
        if k >= len(steps):
            return
        for kind, phase in steps[k]:
            if kind == "start":
                self.start(phase)
            elif kind == "mid":
                self.mid(phase)
            elif kind == "back_mid":
                self.back_mid(phase)
            elif kind == "turn":
                for color in colors:
                    self.end(phase, color)
                    if phase < 2:
                        for i in range(4 if self.hops[phase + 1] == 2 else 3):
                            self.there[phase + 1][color][0][i]().start()
                    else:
                        self.back_start(2, color)
            else:
                for color in colors:
                    self.back_end(phase, color)
                    if phase > 0:
                        self.back_start(phase - 1, color)

    def finish(self):
        for phase in range(3):
            for c, _ in self.there[phase]:
                for i in c:
                    i().wait_send()
            for c in self.back[phase]:
                for i in c:
                    i().wait_send()


def layer_kernel(
    tokens, starts, out_grad, gains, qkv_w, out_w, gu_w, down_w,
    mixed, input_grad, result, gu_far, down_far,
    tok, dyt, dyp, gain_far, wqkv, wout, wg, wd,
    cosine, sine, bias, hbuf, h1t, h2t, qs, ks, vs, ps, os, qt, dot_, ot,
    x1, yacc, dh2, kvt, dqkv, gacc1, gacc2, gain_sum, box, work, extra,
    in_sem, own_sem, load_sem, w_send, w_recv, pair_send, pair_recv, out_sem,
    send, recv, back_send, back_recv, keep_sem,
):
    r = lax.axis_index("replica")
    core = lax.axis_index("shard")
    other = 1 - core
    sems = (send, recv, back_send, back_recv, keep_sem)

    copy_tok = pltpu.make_async_copy(tokens, h2t, in_sem.at[0])
    copy_dy = pltpu.make_async_copy(out_grad, dyt, in_sem.at[1])
    copy_tok.start()
    copy_dy.start()
    mine480 = pl.ds(pl.multiple_of(core * HALF, 16), HALF)
    other480 = pl.ds(pl.multiple_of(other * HALF, 16), HALF)
    own_qkv = pltpu.make_async_copy(qkv_w, wqkv.at[mine480], own_sem.at[0])
    own_out = pltpu.make_async_copy(out_w, wout.at[mine480], own_sem.at[1])
    own_qkv.start()
    own_out.start()

    barrier = pltpu.get_barrier_semaphore()
    pl.semaphore_signal(barrier, inc=1, device_id=(r, other), device_id_type=MESH)
    near = neighbours()
    for _, *chips in near:
        for chip in chips:
            pl.semaphore_signal(barrier, inc=1, device_id=(chip, core), device_id_type=MESH)

    def push(k, src, dst):
        return pltpu.make_async_remote_copy(
            src_ref=src, dst_ref=dst, send_sem=w_send.at[k], recv_sem=w_recv.at[k],
            device_id=(r, other), device_id_type=MESH,
        )

    def ff_push(j):
        out = []
        for q in range(4):
            cols = pl.ds(pl.multiple_of(q * 1280 + j * 256, 256), 256)
            out.append(push(3 + 5 * j + q, gu_w.at[:, cols], gu_far.at[:, cols]))
        cols = pl.ds(pl.multiple_of(j * 256, 256), 256)
        out.append(push(3 + 5 * j + 4, down_w.at[:, cols], down_far.at[:, cols]))
        return out

    def loads(j):
        slot = lax.rem(j, 2)
        out = []
        for q in range(4):
            cols = pl.ds(pl.multiple_of(q * 1280 + j * 256, 256), 256)
            for i, (src, rows) in enumerate(((gu_w, mine480), (gu_far, other480))):
                out.append(pltpu.make_async_copy(src.at[:, cols], wg.at[slot, q, rows], load_sem.at[slot, 2 * q + i]))
        cols = pl.ds(pl.multiple_of(j * 256, 256), 256)
        out.append(pltpu.make_async_copy(down_w.at[:, cols], wd.at[slot, core], load_sem.at[slot, 8]))
        out.append(pltpu.make_async_copy(down_far.at[:, cols], wd.at[slot, other], load_sem.at[slot, 9]))
        return out

    def start_loads(j):
        for c in ff_push(j):
            c.wait_recv()
        for c in loads(j):
            c.start()

    lane = lax.broadcasted_iota(jnp.int32, (TOK, LANES), 1)
    low = lane < HEAD_SIZE
    early = lax.rem(lane, HEAD_SIZE) < HEAD_SIZE // 2

    def swap(t):
        return jnp.where(early, pltpu.roll(t, LANES - 32, 1), pltpu.roll(t, 32, 1))

    def rope(t):
        return t * cosine[...] + swap(t) * sine[...]

    def rope_back(t):
        return t * cosine[...] - swap(t) * sine[...]

    def transpose(t):
        return jnp.transpose(t.astype(F32)).astype(BF16)

    line = starts[...].astype(F32)
    row = lax.broadcasted_iota(jnp.int32, (TOK, TOK), 0)
    column = lax.broadcasted_iota(jnp.int32, (TOK, TOK), 1)
    across = jnp.broadcast_to(line, (TOK, TOK))
    down_col = jnp.sum(jnp.where(row == column, across, 0.0), axis=1, keepdims=True)
    bias[...] = jnp.where((down_col == across) & (row >= column), 0.0, HIDDEN)
    position = lax.broadcasted_iota(jnp.int32, (TOK, LANES), 0).astype(F32) - down_col
    index = lax.rem(lane, 32).astype(F32)
    freq = jnp.exp(-jnp.log(jnp.full((TOK, LANES), 10000.0, F32)) * index * 2.0 / HEAD_SIZE)
    angle = position * freq
    cosine[...] = jnp.cos(angle)
    sine[...] = jnp.where(early, -jnp.sin(angle), jnp.sin(angle))

    copy_tok.wait()
    copy_dy.wait()
    for t in range(8):
        w = min(LANES, D - t * LANES)
        place = slice(t * LANES, t * LANES + w)
        tok[:, place] = transpose(h2t[place, :])
        dyp[:, place] = transpose(dyt[place, :])

    pl.semaphore_wait(barrier, 1 + 3 * len(near))
    push_gain = push(0, gains, gain_far)
    push_qkv = push(1, qkv_w, wqkv.at[mine480])
    push_out = push(2, out_w, wout.at[mine480])
    push_gain.start()
    push_qkv.start()
    push_out.start()
    for j in range(FF_CHUNKS):
        for c in ff_push(j):
            c.start()
    push_gain.wait_recv()

    def gain(k):
        return (gains[k : k + 1, :].astype(F32) + gain_far[k : k + 1, :].astype(F32))[:, :D]

    def rows_of(i):
        return pl.ds(pl.multiple_of(i * BLOCK, BLOCK), BLOCK)

    def normed(x):
        inv = lax.rsqrt(jnp.mean(x * x, axis=-1, keepdims=True) + EPSILON)
        return x * inv, inv

    def norm_one(i, _):
        rows = rows_of(i)
        n, _inv = normed(tok[rows, :].astype(F32))
        hbuf[rows, :] = (n * gain(0)).astype(BF16)
        return 0

    lax.fori_loop(0, TOK // BLOCK, norm_one, 0)

    def transposed(dst, src):
        for t in range(8):
            w = min(LANES, D - t * LANES)
            dst[t * LANES : t * LANES + w, :] = transpose(src[:, t * LANES : t * LANES + w])

    transposed(h1t, hbuf)

    own_qkv.wait()
    push_qkv.wait_recv()
    for n0 in range(0, QKV, 256):
        width = min(256, QKV - n0)
        joint = mm(hbuf[...], wqkv[:, n0 : n0 + width])
        for c0 in range(0, width, LANES):
            t = (n0 + c0) // LANES
            if c0 + LANES <= width:
                tile = joint[:, c0 : c0 + LANES]
            else:
                piece = joint[:, c0:width]
                tile = jnp.concatenate([piece, piece], axis=1)
            turned = rope(tile) if t < 10 else tile
            if t < 8:
                flipped = transpose(turned)
                w = min(LANES, D - t * LANES)
                qt[t * LANES : t * LANES + w, :] = flipped[:w]
            for part in range(2):
                b = 2 * t + part
                here = low if part == 0 else jnp.logical_not(low)
                if b < QUERY_HEADS:
                    qs[b] = jnp.where(here, turned, 0.0).astype(BF16)
                elif b < QUERY_HEADS + 2 * KEY_VALUE_HEADS:
                    both = jnp.where(here, turned, pltpu.roll(turned, HEAD_SIZE, 1)).astype(BF16)
                    if b < QUERY_HEADS + KEY_VALUE_HEADS:
                        ks[b - QUERY_HEADS] = both
                    else:
                        vs[b - QUERY_HEADS - KEY_VALUE_HEADS] = both

    start_loads(0)
    start_loads(1)

    def attend(g, _):
        for i in range(GROUP):
            h = GROUP * g + i
            s = mm_nt(qs[h], ks[g]) * SCALE + bias[...]
            e = jnp.exp(s - jnp.max(s, axis=-1, keepdims=True))
            p = (e * (1.0 / jnp.sum(e, axis=-1, keepdims=True))).astype(BF16)
            ps[h] = p
            os[h] = mm(p, vs[g]).astype(BF16)
        return 0

    lax.fori_loop(0, KEY_VALUE_HEADS, attend, 0)

    def pair_tile(t):
        a = os[2 * t].astype(F32)
        if 2 * t + 1 < QUERY_HEADS:
            a = jnp.where(low, a, os[2 * t + 1].astype(F32))
        return a

    for t in range(8):
        w = min(LANES, D - t * LANES)
        tile = pair_tile(t)
        hbuf[:, t * LANES : t * LANES + w] = tile[:, :w].astype(BF16)
        ot[t * LANES : t * LANES + w, :] = jnp.transpose(tile).astype(BF16)[:w]

    own_out.wait()
    push_out.wait_recv()
    for n0 in range(0, D, 256):
        cols = slice(n0, min(D, n0 + 256))
        x1[:, cols] = tok[:, cols].astype(F32) + mm(hbuf[...], wout[:, cols])

    def norm_two(i, _):
        rows = rows_of(i)
        x = x1[rows, :]
        n, _inv = normed(x)
        hbuf[rows, :] = (n * gain(1)).astype(BF16)
        yacc[rows, :] = x
        dh2[rows, :] = jnp.zeros((BLOCK, D), F32)
        return 0

    lax.fori_loop(0, TOK // BLOCK, norm_two, 0)
    transposed(h2t, hbuf)

    def pair(k, slot, first, count, base):
        return pltpu.make_async_remote_copy(
            src_ref=box.at[slot, other, pl.ds(first, count)],
            dst_ref=work.at[pl.ds(base + first, count)],
            send_sem=pair_send.at[k],
            recv_sem=pair_recv.at[k],
            device_id=(r, other),
            device_id_type=MESH,
        )

    def tile_columns(slot, half, at, value, count):
        for c in range(count):
            block = value[:, c * LANES : (c + 1) * LANES]
            n = block.shape[0] // ROWS
            box[slot, half, pl.ds(at + c * n, n)] = block.astype(BF16).reshape(n, ROWS, LANES)

    def folded(value):
        n = value.shape[0] // 2
        left = lax.broadcasted_iota(jnp.int32, (n, LANES), 1) < HEAD_SIZE
        return jnp.where(left, value[:n], value[n:])

    def feed_forward(tick):
        j, s = lax.div(tick, 2), lax.rem(tick, 2)
        slot = lax.rem(j, 2)

        @pl.when(s == 0)
        def _():
            for c in loads(j):
                c.wait()

        gate = mm(hbuf[...], wg[slot, s])
        upper = mm(hbuf[...], wg[slot, 2 + s])
        grad = mm(dyp[:, :D], wd[slot, s])
        sigma = jax.nn.sigmoid(gate)
        silu = gate * sigma
        inner_low = (silu * upper).astype(BF16)
        dgate = (grad * upper * sigma * (1.0 + gate * (1.0 - sigma))).astype(BF16)
        dupper = (grad * silu).astype(BF16)
        yacc[...] += mm_nt(inner_low, wd[slot, s])
        dh2[...] += mm_nt(dgate, wg[slot, s]) + mm_nt(dupper, wg[slot, 2 + s])
        for half in range(2):
            left = h2t[half * HALF : (half + 1) * HALF, :]
            tile_columns(slot, half, s * 120, mm(left, dgate), 2)
            tile_columns(slot, half, s * 120 + 60, mm(left, dupper), 2)
        tile_columns(slot, s, 240, mm(dyt[...], inner_low), 2)

        @pl.when(s == 1)
        def _():
            pair(j, slot, 0, FF_USED, j * FF_TILES).start()

            @pl.when(j + 2 < FF_CHUNKS)
            def _():
                start_loads(j + 2)

    def gain_rows(value):
        return jnp.sum(value.reshape(BLOCK // 8, 8, D), axis=0)

    def output_projection():
        gacc2[...] = jnp.zeros((8, D), F32)

        def back_two(i, _):
            rows = rows_of(i)
            n, inv = normed(x1[rows, :])
            d = dh2[rows, :]
            gacc2[...] += gain_rows(d * n)
            dn = d * gain(1)
            dx = dyp[rows, :D].astype(F32) + inv * (dn - n * jnp.mean(dn * n, axis=-1, keepdims=True))
            dh2[rows, :] = dx
            da = dx.astype(BF16)
            dyp[rows, : 7 * LANES] = da[:, : 7 * LANES]
            last = da[:, 7 * LANES :]
            dyp[rows, 7 * LANES :] = jnp.concatenate([last, last], axis=1)
            return 0

        lax.fori_loop(0, TOK // BLOCK, back_two, 0)
        transposed(h2t, yacc)
        pltpu.make_async_copy(h2t, mixed, out_sem.at[0]).start()
        for half in range(2):
            v = mm(ot[half * HALF : (half + 1) * HALF, :], dyp[...])
            tile_columns(1, half, 0, v, 7)
            tile_columns(1, half, 210, folded(v[:, 7 * LANES :]), 1)
        pair(5, 1, 0, OUT_USED, OUT_BASE).start()
        for n0 in range(0, D, 256):
            width = min(256, D - n0)
            v = mm_nt(dyp[:, :D], wout[n0 : n0 + width, :])
            for c0 in range(0, width, LANES):
                t = (n0 + c0) // LANES
                if c0 + LANES <= width:
                    tile = v[:, c0 : c0 + LANES]
                else:
                    piece = v[:, c0:width]
                    tile = jnp.concatenate([piece, piece], axis=1)
                w = min(LANES, D - t * LANES)
                dot_[t * LANES : t * LANES + w, :] = transpose(tile)[:w]
                qs[2 * t] = jnp.where(low, tile, 0.0).astype(BF16)
                if 2 * t + 1 < QUERY_HEADS:
                    qs[2 * t + 1] = jnp.where(low, 0.0, tile).astype(BF16)

    def attend_back(g):
        key_t = jnp.zeros((HEAD_SIZE, TOK), F32)
        value_t = jnp.zeros((HEAD_SIZE, TOK), F32)
        for i in range(GROUP):
            h = GROUP * g + i
            dp = mm_nt(qs[h], vs[g])
            low_p = ps[h]
            p = low_p.astype(F32)
            delta = jnp.sum(dp * p, axis=-1, keepdims=True)
            ds = (p * (dp - delta)).astype(BF16)
            os[h] = rope_back(mm(ds, ks[g]) * SCALE).astype(BF16)
            rows = pl.ds(pl.multiple_of(h * HEAD_SIZE, HEAD_SIZE), HEAD_SIZE)
            key_t = key_t + mm(qt[rows, :], ds)
            value_t = value_t + mm(dot_[rows, :], low_p)
        kvt[pl.ds(pl.multiple_of(HEAD_SIZE * (1 + g), HEAD_SIZE), HEAD_SIZE), :] = key_t * SCALE
        kvt[pl.ds(pl.multiple_of(HEAD_SIZE * (6 + g), HEAD_SIZE), HEAD_SIZE), :] = value_t
        kvt[HEAD_SIZE * 11 : HEAD_SIZE * 12, :] = value_t

    def joint_projection():
        for t in range(13):
            if t < 7:
                tile = pair_tile(t)
            else:
                tile = jnp.transpose(kvt[(t - 7) * LANES : (t - 6) * LANES, :])
                if t < 10:
                    tile = rope_back(tile)
                if t == 7:
                    tile = jnp.where(low, pair_tile(7), tile)
            dqkv[:, t * LANES : (t + 1) * LANES] = tile.astype(BF16)
        for half in range(2):
            left = h1t[half * HALF : (half + 1) * HALF, :]
            for n0 in range(0, 1536, 256):
                v = mm(left, dqkv[:, n0 : n0 + 256])
                tile_columns(0, half, n0 // LANES * 30, v, 2)
            v = mm(left, dqkv[:, 1536:])
            tile_columns(0, half, 360, folded(v), 1)
        pair(6, 0, 0, QKV_USED, QKV_BASE).start()
        for n0 in range(0, D, 256):
            cols = slice(n0, min(D, n0 + 256))
            yacc[:, cols] = mm_nt(dqkv[:, :QKV], wqkv[cols, :])
        gacc1[...] = jnp.zeros((8, D), F32)

        def back_one(i, _):
            rows = rows_of(i)
            n, inv = normed(tok[rows, :].astype(F32))
            d = yacc[rows, :]
            gacc1[...] += gain_rows(d * n)
            dn = d * gain(0)
            dh2[rows, :] += inv * (dn - n * jnp.mean(dn * n, axis=-1, keepdims=True))
            return 0

        lax.fori_loop(0, TOK // BLOCK, back_one, 0)
        for t in range(8):
            place = slice(t * LANES, min(D, (t + 1) * LANES))
            kvt[place, :] = jnp.transpose(dh2[:, place])
        pltpu.make_async_copy(kvt, input_grad, out_sem.at[1]).start()
        gain_sum[...] = jnp.zeros((ROWS, LANES), F32)
        for k, acc in enumerate((gacc1, gacc2)):
            total = jnp.sum(acc[...], axis=0, keepdims=True)
            for t in range(8):
                w = min(LANES, D - t * LANES)
                gain_sum[8 * k + t : 8 * k + t + 1, :w] = total[:, t * LANES : t * LANES + w]
        for half in range(2):
            box[0, half, GAIN_TILE] = gain_sum[...].astype(BF16)
        pair(7, 0, GAIN_TILE, 1, QKV_BASE).start()

    def add_own(slot, base, count):
        def step(i, _):
            o = i * 5
            total = work[pl.ds(base + o, 5)].astype(F32) + box[slot, core, pl.ds(o, 5)].astype(F32)
            work[pl.ds(base + o, 5)] = total.astype(BF16)
            return 0

        lax.fori_loop(0, count // 5, step, 0)

    ff_travel = functools.partial(Travel, work, extra, result, sems)

    def of_ff(g):
        return ff_travel(g, g * FF_TILES, g * FF_EXTRA, UNITS, FF_HOPS)

    of_out = ff_travel(5, OUT_BASE, OUT_EXTRA_BASE, OUT_UNITS, OUT_HOPS)
    of_qkv = ff_travel(6, QKV_BASE, QKV_EXTRA_BASE, UNITS, QKV_HOPS)

    def travel(tick):
        for k in range(steps_of(FF_HOPS) - 1, -1, -1):
            since = tick - 2 - 2 * k
            turn = lax.rem(since + 64, 4)

            @pl.when((since >= 0) & (since <= 2 * FF_CHUNKS - 2) & ((turn == 0) | (turn == 3)))
            def _(k=k, since=since):
                g = lax.div(since, 2)
                if k == 0:
                    c = pair(g, lax.rem(g, 2), 0, FF_USED, g * FF_TILES)
                    c.wait()
                    add_own(lax.rem(g, 2), g * FF_TILES, FF_USED)
                of_ff(g).step(k)

        @pl.when(tick > OUT_TICK)
        def _():
            for k in range(steps_of(OUT_HOPS)):

                @pl.when(tick == OUT_TICK + 1 + k)
                def _(k=k):
                    if k == 0:
                        pair(5, 1, 0, OUT_USED, OUT_BASE).wait()
                        add_own(1, OUT_BASE, OUT_USED)
                    of_out.step(k)

        @pl.when(tick > LAST_TICK)
        def _():
            for k in range(steps_of(QKV_HOPS)):

                @pl.when(tick == LAST_TICK + 1 + k)
                def _(k=k):
                    if k == 0:
                        pair(6, 0, 0, QKV_USED, QKV_BASE).wait()
                        add_own(0, QKV_BASE, QKV_USED)
                        pair(7, 0, GAIN_TILE, 1, QKV_BASE).wait()
                        at = QKV_BASE + GAIN_TILE
                        work[at] = (work[at].astype(F32) + box[0, core, GAIN_TILE].astype(F32)).astype(BF16)
                    of_qkv.step(k)

    def tick_body(tick, _):
        @pl.when(tick < OUT_TICK)
        def _():
            feed_forward(tick)

        @pl.when(tick == OUT_TICK)
        def _():
            output_projection()

        @pl.when((tick >= ATTN_TICK) & (tick < LAST_TICK))
        def _():
            attend_back(tick - ATTN_TICK)

        @pl.when(tick == LAST_TICK)
        def _():
            joint_projection()

        travel(tick)
        return 0

    lax.fori_loop(0, TICKS, tick_body, 0)

    pltpu.make_async_copy(h2t, mixed, out_sem.at[0]).wait()
    pltpu.make_async_copy(kvt, input_grad, out_sem.at[1]).wait()
    push_gain.wait_send()
    push_qkv.wait_send()
    push_out.wait_send()

    def finish(g, _):
        for c in ff_push(g):
            c.wait_send()
        of_ff(g).finish()
        return 0

    lax.fori_loop(0, FF_CHUNKS, finish, 0)
    of_out.finish()
    of_qkv.finish()


def layer(tokens, starts, out_grad, gains, qkv_w, out_w, gu_w, down_w):
    vm = pltpu.VMEM
    dma = pltpu.SemaphoreType.DMA
    hbm = pl.BlockSpec(memory_space=pl.ANY)
    near = pl.BlockSpec(memory_space=pltpu.VMEM)
    shape = jax.ShapeDtypeStruct
    return pl.pallas_call(
        layer_kernel,
        out_shape=[
            shape((D, TOK), BF16),
            shape((D, TOK), F32),
            shape((TILES, ROWS, LANES), BF16),
            shape((HALF, 2 * FF), BF16),
            shape((D, FF // 2), BF16),
        ],
        in_specs=[hbm, near, hbm, near, hbm, hbm, hbm, hbm],
        out_specs=[hbm] * 5,
        scratch_shapes=[
            vm((TOK, D), BF16),
            vm((D, TOK), BF16),
            vm((TOK, 1024), BF16),
            vm((16, 1024), BF16),
            vm((D, QKV), BF16),
            vm((D, D), BF16),
            vm((2, 4, D, 256), BF16),
            vm((2, 2, D, 256), BF16),
            vm((TOK, LANES), F32),
            vm((TOK, LANES), F32),
            vm((TOK, TOK), F32),
            vm((TOK, D), BF16),
            vm((D, TOK), BF16),
            vm((D, TOK), BF16),
            vm((QUERY_HEADS, TOK, LANES), BF16),
            vm((KEY_VALUE_HEADS, TOK, LANES), BF16),
            vm((KEY_VALUE_HEADS, TOK, LANES), BF16),
            vm((QUERY_HEADS, TOK, TOK), BF16),
            vm((QUERY_HEADS, TOK, LANES), BF16),
            vm((D, TOK), BF16),
            vm((D, TOK), BF16),
            vm((D, TOK), BF16),
            vm((TOK, D), F32),
            vm((TOK, D), F32),
            vm((TOK, D), F32),
            vm((D, TOK), F32),
            vm((TOK, 13 * LANES), BF16),
            vm((8, D), F32),
            vm((8, D), F32),
            vm((ROWS, LANES), F32),
            vm((2, 2, BOX, ROWS, LANES), BF16),
            vm((TILES, ROWS, LANES), BF16),
            vm((EXTRA, ROWS, LANES), BF16),
            dma((2,)), dma((2,)), dma((2, 10)),
            dma((28,)), dma((28,)), dma((8,)), dma((8,)), dma((2,)),
            dma((7, 54)), dma((7, 54)), dma((7, 36)), dma((7, 36)), dma((7, 3)),
        ],
        compiler_params=pltpu.CompilerParams(
            collective_id=0, has_side_effects=True, vmem_limit_bytes=VMEM_LIMIT
        ),
        name="layer",
    )(tokens, starts, out_grad, gains, qkv_w, out_w, gu_w, down_w)


VMEM_LIMIT = 64 * 1024 * 1024 - 256 * 1024


def widen_kernel(
    res, mixed_in, grad_in, down, gu, qkv, out, gain, mixed, grad,
    rv, down_v, gu_v, qkv_v, out_v, in_sem, out_sem, pass_sem,
):
    bounds = [FF_TILES * j for j in range(FF_CHUNKS)] + [OUT_BASE, QKV_BASE]
    counts = [FF_USED] * FF_CHUNKS + [OUT_USED, QKV_USED + 1]
    loads = [
        pltpu.make_async_copy(res.at[pl.ds(b, n)], rv.at[pl.ds(b, n)], in_sem.at[i])
        for i, (b, n) in enumerate(zip(bounds, counts))
    ]
    for c in loads:
        c.start()
    passed = [
        pltpu.make_async_copy(mixed_in, mixed, pass_sem.at[0]),
        pltpu.make_async_copy(grad_in, grad, pass_sem.at[1]),
    ]
    for c in passed:
        c.start()
    stores = []

    def store(src, dst):
        c = pltpu.make_async_copy(src, dst, out_sem.at[len(stores)])
        c.start()
        stores.append(c)

    def column(at, n):
        return rv[pl.ds(at, n)].astype(F32).reshape(n * ROWS, LANES)

    def last_column(at, n):
        both = column(at, n)
        return both[:, :HEAD_SIZE], pltpu.roll(both, HEAD_SIZE, 1)[:, :HEAD_SIZE]

    for j in range(FF_CHUNKS):
        loads[j].wait()
        base = FF_TILES * j
        for s in range(2):
            for w in range(2):
                first = w * FF + s * 1280 + j * 256
                for c in range(2):
                    gu_v[:, first + c * LANES : first + (c + 1) * LANES] = column(base + (s * 2 + w) * 60 + c * 30, 30)
                cols = pl.ds(first, 256)
                store(gu_v.at[:, cols], gu.at[:, cols])
        first = 256 * j
        for c in range(2):
            down_v[:, first + c * LANES : first + (c + 1) * LANES] = column(base + 240 + c * 60, 60)
        cols = pl.ds(first, 256)
        store(down_v.at[:, cols], down.at[:, cols])
    loads[5].wait()
    for c in range(7):
        out_v[:, c * LANES : (c + 1) * LANES] = column(OUT_BASE + c * 30, 30)
    a, b = last_column(OUT_BASE + 210, 15)
    out_v[:240, 7 * LANES :] = a
    out_v[240:, 7 * LANES :] = b
    store(out_v, out)
    loads[6].wait()
    for c in range(12):
        qkv_v[:, c * LANES : (c + 1) * LANES] = column(QKV_BASE + c * 30, 30)
    a, b = last_column(QKV_BASE + 360, 15)
    qkv_v[:240, 12 * LANES :] = a
    qkv_v[240:, 12 * LANES :] = b
    store(qkv_v, qkv)
    gain[...] = rv[QKV_BASE + GAIN_TILE].astype(F32)
    for c in stores:
        c.wait()
    for c in passed:
        c.wait()


def widened(result, mixed, grad):
    vm = pltpu.VMEM
    dma = pltpu.SemaphoreType.DMA
    hbm = pl.BlockSpec(memory_space=pl.ANY)
    shape = jax.ShapeDtypeStruct
    sizes = [(D, FF // 2), (HALF, 2 * FF), (HALF, QKV), (HALF, D)]
    return pl.pallas_call(
        widen_kernel,
        out_shape=[shape(s, F32) for s in sizes]
        + [shape((ROWS, LANES), F32), shape((D, TOK), BF16), shape((D, TOK), F32)],
        in_specs=[hbm] * 3,
        out_specs=[hbm] * 4 + [pl.BlockSpec(memory_space=vm), hbm, hbm],
        scratch_shapes=[
            vm((TILES, ROWS, LANES), BF16),
            *[vm(s, F32) for s in sizes],
            dma((7,)), dma((27,)), dma((2,)),
        ],
        compiler_params=pltpu.CompilerParams(vmem_limit_bytes=48 * 1024 * 1024),
        name="widen",
    )(result, mixed, grad)


def per_device(
    tokens, starts, out_grad, norm_attn, norm_mlp, qkv_weight, out_weight, gate_up_weight, down_weight
):
    core = lax.axis_index("shard")
    both = jnp.stack([norm_attn, norm_mlp])
    gains = jnp.where(
        core == 0, jnp.pad(both, ((0, 14), (0, 544))), jnp.pad(both, ((0, 14), (HALF, 64)))
    )
    mixed, input_grad, result, _, _ = layer(
        tokens.T, starts.reshape(1, TOK), out_grad.T, gains, qkv_weight, out_weight, gate_up_weight, down_weight.T
    )
    down, gu, qkv, out, gain, mixed, input_grad = widened(result, mixed, input_grad)
    first = core * HALF
    gain_one = lax.dynamic_slice(gain[:8].reshape(1024), (first,), (HALF,))
    gain_two = lax.dynamic_slice(gain[8:].reshape(1024), (first,), (HALF,))
    return mixed.T, input_grad.T, gain_one, gain_two, qkv, out, gu, down.T


def solution(mesh):
    rows, weights = P(("replica", "shard"), None), P("shard", None)
    return jax.shard_map(
        per_device,
        mesh=mesh,
        in_specs=(
            rows, P(("replica", "shard")), rows, P("shard"), P("shard"), weights, weights, weights, weights,
        ),
        out_specs=(rows, rows, P("shard"), P("shard"), weights, weights, weights, weights),
        check_vma=False,
    )
```

```python
import functools

import jax
import jax.numpy as jnp
from jax import lax
from jax.experimental import pallas as pl
from jax.experimental.pallas import tpu as pltpu
from jax.sharding import PartitionSpec as P

D = 960
HALF = D // 2
QUERY_HEADS = 15
KEY_VALUE_HEADS = 5
GROUP = QUERY_HEADS // KEY_VALUE_HEADS
HEAD_SIZE = 64
FF = 2560
TOK = 384
QKV = 1600
EPSILON = 1e-05
SCALE = HEAD_SIZE**-0.5
HIDDEN = -1e30

MESH = pl.DeviceIdType.MESH
F32 = jnp.float32
BF16 = jnp.bfloat16
LANES = 128
ROWS = 16
BLOCK = 48

FF_CHUNKS = 5
FF_TILES = 384
FF_USED = 360
OUT_BASE = FF_CHUNKS * FF_TILES
OUT_TILES = 256
OUT_USED = 225
QKV_BASE = OUT_BASE + OUT_TILES
QKV_TILES = 384
QKV_USED = 375
GAIN_TILE = 375
TILES = QKV_BASE + QKV_TILES
BOX = 376
UNITS = (2, 2, 2)
OUT_UNITS = (2, 2)
FF_EXTRA = 378
OUT_EXTRA_BASE = FF_CHUNKS * FF_EXTRA
QKV_EXTRA_BASE = OUT_EXTRA_BASE + 252
EXTRA = QKV_EXTRA_BASE + FF_EXTRA
FF_HOPS = (2, 1, 1)
OUT_HOPS = (2, 1, 1)
QKV_HOPS = (2, 1, 1)


def steps_of(hops):
    return 7 + 2 * sum(h - 1 for h in hops)


OUT_TICK = 2 * FF_CHUNKS
ATTN_TICK = OUT_TICK + 1
LAST_TICK = ATTN_TICK + KEY_VALUE_HEADS
TICKS = max(2 * FF_CHUNKS + 2 * steps_of(FF_HOPS) - 1, LAST_TICK + 1 + steps_of(QKV_HOPS))


def mm(a, b):
    return lax.dot_general(a, b, (((1,), (0,)), ((), ())), preferred_element_type=F32)


def mm_nt(a, b):
    return lax.dot_general(a, b, (((1,), (1,)), ((), ())), preferred_element_type=F32)


def neighbours():
    r = lax.axis_index("replica")
    x = lax.rem(r, 4)
    y = lax.rem(lax.div(r, 4), 4)
    z = lax.div(r, 16)
    out = []
    for place, stride in ((x, 1), (y, 4), (z, 16)):
        ahead = r + stride * (lax.rem(place + 1, 4) - place)
        behind = r + stride * (lax.rem(place + 3, 4) - place)
        across = r + stride * (lax.rem(place + 2, 4) - place)
        out.append((place, ahead, behind, across))
    return out


def add_into(dst, at, terms, count):
    block = 8 if count % 8 == 0 else count

    def step(i, _):
        o = i * block
        total = dst[pl.ds(at + o, block)].astype(F32)
        for ref, off in terms:
            total = total + ref[pl.ds(off + o, block)].astype(F32)
        dst[pl.ds(at + o, block)] = total.astype(BF16)
        return 0

    if count == block:
        step(0, 0)
    else:
        lax.fori_loop(0, count // block, step, 0)


class Travel:
    def __init__(self, near, core, work, extra, result, sems, group, base, extra_base, units, hops):
        self.work, self.extra, self.result = work, extra, result
        send, recv, back_send, back_recv, keep_sem = sems
        self.hops, self.units = hops, units
        self.there, self.back, self.keeps = [[], [], []], [[], [], []], []
        self.sent = 63 * sum(units)

        def copy(src, dst, send_sem, recv_sem, to):
            return pltpu.make_async_remote_copy(
                src_ref=src, dst_ref=dst, send_sem=send_sem, recv_sem=recv_sem, device_id=(to, core), device_id_type=MESH
            )

        partner = near[0][1]
        self.all_sent = [
            lambda sem=sem: copy(
                work.at[pl.ds(0, self.sent)], extra.at[pl.ds(0, self.sent)], sem.at[group], recv.at[group, 0], partner
            ).wait_send()
            for sem in (send, back_send)
        ]
        for color, n in enumerate(units):
            seg = base + 64 * sum(units[:color])
            at = extra_base + 63 * sum(units[:color])
            for phase in range(3):
                place, ahead, behind, across = near[(color + phase) % 3]
                chunk = (16, 4, 1)[phase] * n
                first = chunk // 2
                second = chunk - first
                mine = seg + chunk * place
                plus = seg + chunk * lax.rem(place + 1, 4)
                minus = seg + chunk * lax.rem(place + 3, 4)
                far = seg + chunk * lax.rem(place + 2, 4)
                xa, xb, yp, ym = at, at + first, at + chunk, at + 2 * chunk
                at = at + 3 * chunk
                slot = color * 9 + phase * 3

                def out(k, src, count, dst, to, slot=slot):
                    return lambda: copy(
                        work.at[pl.ds(src, count)], extra.at[pl.ds(dst, count)], send.at[group], recv.at[group, slot + k], to
                    )

                def home(k, source, at, count, to, slot=slot):
                    return lambda: copy(
                        source.at[pl.ds(at, count)], result.at[pl.ds(at, count)],
                        back_send.at[group], back_recv.at[group, slot + k], to,
                    )

                source = work if phase == 2 else result
                if hops[phase] == 2:
                    copies = (
                        out(0, far, first, xa, ahead),
                        out(1, far + first, second, xb, behind),
                        out(2, plus + first, second, yp + first, ahead),
                        out(2, minus, first, ym, behind),
                        out(2, plus, first, yp, ahead),
                        out(2, minus + first, second, ym + first, behind),
                        out(2, seg, 2 * chunk, yp, ahead),
                    )
                    backs = (
                        home(0, source, mine, chunk, ahead),
                        home(1, source, mine, chunk, behind),
                        home(2, result, minus, first, ahead),
                        home(2, result, plus + first, second, behind),
                        home(2, result, seg, chunk, ahead),
                    )
                else:
                    copies = (
                        out(0, far, chunk, xa, across),
                        out(0, plus, chunk, yp, ahead),
                        out(0, minus, chunk, ym, behind),
                        out(0, seg, 3 * chunk, xa, ahead),
                    )
                    backs = (
                        home(0, source, mine, chunk, across),
                        home(0, source, mine, chunk, ahead),
                        home(0, source, mine, chunk, behind),
                        home(0, result, seg, 3 * chunk, ahead),
                    )
                self.there[phase].append((copies, (first, second, chunk, xa, xb, yp, ym, mine, plus, minus)))
                self.back[phase].append(backs)
                if phase == 2:
                    self.keeps.append(
                        lambda mine=mine, chunk=chunk, color=color: pltpu.make_async_copy(
                            work.at[pl.ds(mine, chunk)],
                            result.at[pl.ds(mine, chunk)],
                            keep_sem.at[group, color],
                        )
                    )
                seg = mine

    def start(self, phase, color):
        for i in range(4 if self.hops[phase] == 2 else 3):
            self.there[phase][color][0][i]().start()

    def mid(self, phase, color):
        c, (first, second, chunk, xa, xb, yp, ym, mine, plus, minus) = self.there[phase][color]
        c[0]().wait_recv()
        add_into(self.work, plus, [(self.extra, xa)], first)
        c[4]().start()
        c[1]().wait_recv()
        add_into(self.work, minus + first, [(self.extra, xb)], second)
        c[5]().start()

    def end(self, phase, color):
        c, (first, second, chunk, xa, xb, yp, ym, mine, plus, minus) = self.there[phase][color]
        terms = [(self.extra, yp), (self.extra, ym)]
        if self.hops[phase] == 1:
            terms.append((self.extra, xa))
        c[-1]().wait_recv()
        add_into(self.work, mine, terms, chunk)

    def back_start(self, phase, color):
        c = self.back[phase][color]
        for i in range(2 if self.hops[phase] == 2 else 3):
            c[i]().start()
        if phase == 2:
            self.keeps[color]().start()

    def back_mid(self, phase, color):
        c = self.back[phase][color]
        c[0]().wait_recv()
        c[2]().start()
        c[1]().wait_recv()
        c[3]().start()

    def back_end(self, phase, color):
        self.back[phase][color][-1]().wait_recv()
        if phase == 2:
            self.keeps[color]().wait()

    def step(self, k):
        steps = [("start", 0)]
        for phase in range(3):
            if self.hops[phase] == 2:
                steps.append(("mid", phase))
            steps.append(("turn", phase))
        for phase in (2, 1, 0):
            if self.hops[phase] == 2:
                steps.append(("back_mid", phase))
            steps.append(("back_turn", phase))
        kind, phase = steps[k]
        for color in range(len(self.units)):
            if kind == "start":
                self.start(phase, color)
            elif kind == "mid":
                self.mid(phase, color)
            elif kind == "back_mid":
                self.back_mid(phase, color)
            elif kind == "turn":
                self.end(phase, color)
                if phase < 2:
                    self.start(phase + 1, color)
                else:
                    self.back_start(2, color)
            else:
                self.back_end(phase, color)
                if phase > 0:
                    self.back_start(phase - 1, color)

    def finish(self):
        for wait in self.all_sent:
            wait()


def layer_kernel(
    tokens, starts, out_grad, gains, qkv_w, out_w, gu_w, down_w,
    mixed, input_grad, result, gu_far, down_far,
    tok, dyt, dyp, gain_far, wqkv, wout, wg, wd,
    cosine, sine, bias, hbuf, h1t, h2t, qs, ks, vs, ps, os, qt, dot_, ot,
    x1, yacc, dh2, kvt, dqkv, gacc1, gacc2, gain_sum, box, work, extra,
    in_sem, own_sem, load_sem, w_send, w_recv, pair_send, pair_recv, out_sem,
    send, recv, back_send, back_recv, keep_sem,
):
    r = lax.axis_index("replica")
    core = lax.axis_index("shard")
    other = 1 - core
    sems = (send, recv, back_send, back_recv, keep_sem)

    copy_tok = pltpu.make_async_copy(tokens, h2t, in_sem.at[0])
    copy_dy = pltpu.make_async_copy(out_grad, dyt, in_sem.at[1])
    copy_tok.start()
    copy_dy.start()
    mine480 = pl.ds(pl.multiple_of(core * HALF, 16), HALF)
    other480 = pl.ds(pl.multiple_of(other * HALF, 16), HALF)
    own_qkv = pltpu.make_async_copy(qkv_w, wqkv.at[mine480], own_sem.at[0])
    own_out = pltpu.make_async_copy(out_w, wout.at[mine480], own_sem.at[1])
    own_qkv.start()
    own_out.start()

    barrier = pltpu.get_barrier_semaphore()
    pl.semaphore_signal(barrier, inc=1, device_id=(r, other), device_id_type=MESH)
    near = neighbours()
    for _, *chips in near:
        for chip in chips:
            pl.semaphore_signal(barrier, inc=1, device_id=(chip, core), device_id_type=MESH)

    def push(k, src, dst):
        return pltpu.make_async_remote_copy(
            src_ref=src, dst_ref=dst, send_sem=w_send.at[k], recv_sem=w_recv.at[k],
            device_id=(r, other), device_id_type=MESH,
        )

    def ff_push(j):
        out = []
        for q in range(4):
            cols = pl.ds(pl.multiple_of(q * 1280 + j * 256, 256), 256)
            out.append(push(3 + 5 * j + q, gu_w.at[:, cols], gu_far.at[:, cols]))
        cols = pl.ds(pl.multiple_of(j * 256, 256), 256)
        out.append(push(3 + 5 * j + 4, down_w.at[:, cols], down_far.at[:, cols]))
        return out

    def loads(j):
        slot = lax.rem(j, 2)
        out = []
        for q in range(4):
            cols = pl.ds(pl.multiple_of(q * 1280 + j * 256, 256), 256)
            for i, (src, rows) in enumerate(((gu_w, mine480), (gu_far, other480))):
                out.append(pltpu.make_async_copy(src.at[:, cols], wg.at[slot, q, rows], load_sem.at[slot, 2 * q + i]))
        cols = pl.ds(pl.multiple_of(j * 256, 256), 256)
        out.append(pltpu.make_async_copy(down_w.at[:, cols], wd.at[slot, core], load_sem.at[slot, 8]))
        out.append(pltpu.make_async_copy(down_far.at[:, cols], wd.at[slot, other], load_sem.at[slot, 9]))
        return out

    def start_loads(j):
        for c in ff_push(j):
            c.wait_recv()
        for c in loads(j):
            c.start()

    lane = lax.broadcasted_iota(jnp.int32, (TOK, LANES), 1)
    low = lane < HEAD_SIZE
    early = lax.rem(lane, HEAD_SIZE) < HEAD_SIZE // 2

    def swap(t):
        return jnp.where(early, pltpu.roll(t, LANES - 32, 1), pltpu.roll(t, 32, 1))

    def rope(t):
        return t * cosine[...] + swap(t) * sine[...]

    def rope_back(t):
        return t * cosine[...] - swap(t) * sine[...]

    def transpose(t):
        return jnp.transpose(t.astype(F32)).astype(BF16)

    line = starts[...].astype(F32)
    row = lax.broadcasted_iota(jnp.int32, (TOK, TOK), 0)
    column = lax.broadcasted_iota(jnp.int32, (TOK, TOK), 1)
    across = jnp.broadcast_to(line, (TOK, TOK))
    down_col = jnp.sum(jnp.where(row == column, across, 0.0), axis=1, keepdims=True)
    bias[...] = jnp.where((down_col == across) & (row >= column), 0.0, HIDDEN)
    position = lax.broadcasted_iota(jnp.int32, (TOK, LANES), 0).astype(F32) - down_col
    index = lax.rem(lane, 32).astype(F32)
    freq = jnp.exp(-jnp.log(jnp.full((TOK, LANES), 10000.0, F32)) * index * 2.0 / HEAD_SIZE)
    angle = position * freq
    cosine[...] = jnp.cos(angle)
    sine[...] = jnp.where(early, -jnp.sin(angle), jnp.sin(angle))

    copy_tok.wait()
    copy_dy.wait()
    for t in range(8):
        w = min(LANES, D - t * LANES)
        place = slice(t * LANES, t * LANES + w)
        tok[:, place] = transpose(h2t[place, :])
        dyp[:, place] = transpose(dyt[place, :])

    pl.semaphore_wait(barrier, 1 + 3 * len(near))
    push_gain = push(0, gains, gain_far)
    push_qkv = push(1, qkv_w, wqkv.at[mine480])
    push_out = push(2, out_w, wout.at[mine480])
    push_gain.start()
    push_qkv.start()
    push_out.start()
    for j in range(FF_CHUNKS):
        for c in ff_push(j):
            c.start()
    push_gain.wait_recv()

    def gain(k):
        return (gains[k : k + 1, :].astype(F32) + gain_far[k : k + 1, :].astype(F32))[:, :D]

    def rows_of(i):
        return pl.ds(pl.multiple_of(i * BLOCK, BLOCK), BLOCK)

    def normed(x):
        inv = lax.rsqrt(jnp.mean(x * x, axis=-1, keepdims=True) + EPSILON)
        return x * inv, inv

    def norm_one(i, _):
        rows = rows_of(i)
        n, _inv = normed(tok[rows, :].astype(F32))
        hbuf[rows, :] = (n * gain(0)).astype(BF16)
        return 0

    lax.fori_loop(0, TOK // BLOCK, norm_one, 0)

    def transposed(dst, src):
        for t in range(8):
            w = min(LANES, D - t * LANES)
            dst[t * LANES : t * LANES + w, :] = transpose(src[:, t * LANES : t * LANES + w])

    transposed(h1t, hbuf)

    own_qkv.wait()
    push_qkv.wait_recv()
    for n0 in range(0, QKV, 256):
        width = min(256, QKV - n0)
        joint = mm(hbuf[...], wqkv[:, n0 : n0 + width])
        for c0 in range(0, width, LANES):
            t = (n0 + c0) // LANES
            if c0 + LANES <= width:
                tile = joint[:, c0 : c0 + LANES]
            else:
                piece = joint[:, c0:width]
                tile = jnp.concatenate([piece, piece], axis=1)
            turned = rope(tile) if t < 10 else tile
            if t < 8:
                flipped = transpose(turned)
                w = min(LANES, D - t * LANES)
                qt[t * LANES : t * LANES + w, :] = flipped[:w]
            for part in range(2):
                b = 2 * t + part
                here = low if part == 0 else jnp.logical_not(low)
                if b < QUERY_HEADS:
                    qs[b] = jnp.where(here, turned, 0.0).astype(BF16)
                elif b < QUERY_HEADS + 2 * KEY_VALUE_HEADS:
                    both = jnp.where(here, turned, pltpu.roll(turned, HEAD_SIZE, 1)).astype(BF16)
                    if b < QUERY_HEADS + KEY_VALUE_HEADS:
                        ks[b - QUERY_HEADS] = both
                    else:
                        vs[b - QUERY_HEADS - KEY_VALUE_HEADS] = both

    start_loads(0)
    start_loads(1)

    def attend(g, _):
        for i in range(GROUP):
            h = GROUP * g + i
            s = mm_nt(qs[h], ks[g]) * SCALE + bias[...]
            e = jnp.exp(s - jnp.max(s, axis=-1, keepdims=True))
            p = (e * (1.0 / jnp.sum(e, axis=-1, keepdims=True))).astype(BF16)
            ps[h] = p
            os[h] = mm(p, vs[g]).astype(BF16)
        return 0

    lax.fori_loop(0, KEY_VALUE_HEADS, attend, 0)

    def pair_tile(t):
        a = os[2 * t].astype(F32)
        if 2 * t + 1 < QUERY_HEADS:
            a = jnp.where(low, a, os[2 * t + 1].astype(F32))
        return a

    for t in range(8):
        w = min(LANES, D - t * LANES)
        tile = pair_tile(t)
        hbuf[:, t * LANES : t * LANES + w] = tile[:, :w].astype(BF16)
        ot[t * LANES : t * LANES + w, :] = jnp.transpose(tile).astype(BF16)[:w]

    own_out.wait()
    push_out.wait_recv()
    for n0 in range(0, D, 256):
        cols = slice(n0, min(D, n0 + 256))
        x1[:, cols] = tok[:, cols].astype(F32) + mm(hbuf[...], wout[:, cols])

    def norm_two(i, _):
        rows = rows_of(i)
        x = x1[rows, :]
        n, _inv = normed(x)
        hbuf[rows, :] = (n * gain(1)).astype(BF16)
        yacc[rows, :] = x
        dh2[rows, :] = jnp.zeros((BLOCK, D), F32)
        return 0

    lax.fori_loop(0, TOK // BLOCK, norm_two, 0)
    transposed(h2t, hbuf)

    def pair(k, slot, first, count, base):
        return pltpu.make_async_remote_copy(
            src_ref=box.at[slot, other, pl.ds(first, count)],
            dst_ref=work.at[pl.ds(base + first, count)],
            send_sem=pair_send.at[k],
            recv_sem=pair_recv.at[k],
            device_id=(r, other),
            device_id_type=MESH,
        )

    def tile_columns(slot, half, at, value, count):
        for c in range(count):
            block = value[:, c * LANES : (c + 1) * LANES]
            n = block.shape[0] // ROWS
            box[slot, half, pl.ds(at + c * n, n)] = block.astype(BF16).reshape(n, ROWS, LANES)

    def folded(value):
        n = value.shape[0] // 2
        left = lax.broadcasted_iota(jnp.int32, (n, LANES), 1) < HEAD_SIZE
        return jnp.where(left, value[:n], value[n:])

    def feed_forward(tick):
        j, s = lax.div(tick, 2), lax.rem(tick, 2)
        slot = lax.rem(j, 2)

        @pl.when(s == 0)
        def _():
            for c in loads(j):
                c.wait()

        gate = mm(hbuf[...], wg[slot, s])
        upper = mm(hbuf[...], wg[slot, 2 + s])
        grad = mm(dyp[:, :D], wd[slot, s])
        sigma = jax.nn.sigmoid(gate)
        silu = gate * sigma
        inner_low = (silu * upper).astype(BF16)
        dgate = (grad * upper * sigma * (1.0 + gate * (1.0 - sigma))).astype(BF16)
        dupper = (grad * silu).astype(BF16)
        yacc[...] += mm_nt(inner_low, wd[slot, s])
        dh2[...] += mm_nt(dgate, wg[slot, s]) + mm_nt(dupper, wg[slot, 2 + s])
        for half in range(2):
            left = h2t[half * HALF : (half + 1) * HALF, :]
            tile_columns(slot, half, s * 120, mm(left, dgate), 2)
            tile_columns(slot, half, s * 120 + 60, mm(left, dupper), 2)
        tile_columns(slot, s, 240, mm(dyt[...], inner_low), 2)

        @pl.when(s == 1)
        def _():
            pair(j, slot, 0, FF_USED, j * FF_TILES).start()

            @pl.when(j + 2 < FF_CHUNKS)
            def _():
                start_loads(j + 2)

    def gain_rows(value):
        return jnp.sum(value.reshape(BLOCK // 8, 8, D), axis=0)

    def output_projection():
        gacc2[...] = jnp.zeros((8, D), F32)

        def back_two(i, _):
            rows = rows_of(i)
            n, inv = normed(x1[rows, :])
            d = dh2[rows, :]
            gacc2[...] += gain_rows(d * n)
            dn = d * gain(1)
            dx = dyp[rows, :D].astype(F32) + inv * (dn - n * jnp.mean(dn * n, axis=-1, keepdims=True))
            dh2[rows, :] = dx
            da = dx.astype(BF16)
            dyp[rows, : 7 * LANES] = da[:, : 7 * LANES]
            last = da[:, 7 * LANES :]
            dyp[rows, 7 * LANES :] = jnp.concatenate([last, last], axis=1)
            return 0

        lax.fori_loop(0, TOK // BLOCK, back_two, 0)
        transposed(h2t, yacc)
        pltpu.make_async_copy(h2t, mixed, out_sem.at[0]).start()
        for half in range(2):
            v = mm(ot[half * HALF : (half + 1) * HALF, :], dyp[...])
            tile_columns(1, half, 0, v, 7)
            tile_columns(1, half, 210, folded(v[:, 7 * LANES :]), 1)
        pair(5, 1, 0, OUT_USED, OUT_BASE).start()
        for n0 in range(0, D, 256):
            width = min(256, D - n0)
            v = mm_nt(dyp[:, :D], wout[n0 : n0 + width, :])
            for c0 in range(0, width, LANES):
                t = (n0 + c0) // LANES
                if c0 + LANES <= width:
                    tile = v[:, c0 : c0 + LANES]
                else:
                    piece = v[:, c0:width]
                    tile = jnp.concatenate([piece, piece], axis=1)
                w = min(LANES, D - t * LANES)
                dot_[t * LANES : t * LANES + w, :] = transpose(tile)[:w]
                qs[2 * t] = jnp.where(low, tile, 0.0).astype(BF16)
                if 2 * t + 1 < QUERY_HEADS:
                    qs[2 * t + 1] = jnp.where(low, 0.0, tile).astype(BF16)

    def attend_back(g):
        key_t = jnp.zeros((HEAD_SIZE, TOK), F32)
        value_t = jnp.zeros((HEAD_SIZE, TOK), F32)
        for i in range(GROUP):
            h = GROUP * g + i
            dp = mm_nt(qs[h], vs[g])
            low_p = ps[h]
            p = low_p.astype(F32)
            delta = jnp.sum(dp * p, axis=-1, keepdims=True)
            ds = (p * (dp - delta)).astype(BF16)
            os[h] = rope_back(mm(ds, ks[g]) * SCALE).astype(BF16)
            rows = pl.ds(pl.multiple_of(h * HEAD_SIZE, HEAD_SIZE), HEAD_SIZE)
            key_t = key_t + mm(qt[rows, :], ds)
            value_t = value_t + mm(dot_[rows, :], low_p)
        kvt[pl.ds(pl.multiple_of(HEAD_SIZE * (1 + g), HEAD_SIZE), HEAD_SIZE), :] = key_t * SCALE
        kvt[pl.ds(pl.multiple_of(HEAD_SIZE * (6 + g), HEAD_SIZE), HEAD_SIZE), :] = value_t
        kvt[HEAD_SIZE * 11 : HEAD_SIZE * 12, :] = value_t

    def joint_projection():
        for t in range(13):
            if t < 7:
                tile = pair_tile(t)
            else:
                tile = jnp.transpose(kvt[(t - 7) * LANES : (t - 6) * LANES, :])
                if t < 10:
                    tile = rope_back(tile)
                if t == 7:
                    tile = jnp.where(low, pair_tile(7), tile)
            dqkv[:, t * LANES : (t + 1) * LANES] = tile.astype(BF16)
        for half in range(2):
            left = h1t[half * HALF : (half + 1) * HALF, :]
            for n0 in range(0, 1536, 256):
                v = mm(left, dqkv[:, n0 : n0 + 256])
                tile_columns(0, half, n0 // LANES * 30, v, 2)
            v = mm(left, dqkv[:, 1536:])
            tile_columns(0, half, 360, folded(v), 1)
        pair(6, 0, 0, QKV_USED, QKV_BASE).start()
        for n0 in range(0, D, 256):
            cols = slice(n0, min(D, n0 + 256))
            yacc[:, cols] = mm_nt(dqkv[:, :QKV], wqkv[cols, :])
        gacc1[...] = jnp.zeros((8, D), F32)

        def back_one(i, _):
            rows = rows_of(i)
            n, inv = normed(tok[rows, :].astype(F32))
            d = yacc[rows, :]
            gacc1[...] += gain_rows(d * n)
            dn = d * gain(0)
            dh2[rows, :] += inv * (dn - n * jnp.mean(dn * n, axis=-1, keepdims=True))
            return 0

        lax.fori_loop(0, TOK // BLOCK, back_one, 0)
        for t in range(8):
            place = slice(t * LANES, min(D, (t + 1) * LANES))
            kvt[place, :] = jnp.transpose(dh2[:, place])
        pltpu.make_async_copy(kvt, input_grad, out_sem.at[1]).start()
        gain_sum[...] = jnp.zeros((ROWS, LANES), F32)
        for k, acc in enumerate((gacc1, gacc2)):
            total = jnp.sum(acc[...], axis=0, keepdims=True)
            for t in range(8):
                w = min(LANES, D - t * LANES)
                gain_sum[8 * k + t : 8 * k + t + 1, :w] = total[:, t * LANES : t * LANES + w]
        for half in range(2):
            box[0, half, GAIN_TILE] = gain_sum[...].astype(BF16)
        pair(7, 0, GAIN_TILE, 1, QKV_BASE).start()

    def add_own(slot, base, count):
        def step(i, _):
            o = i * 5
            total = work[pl.ds(base + o, 5)].astype(F32) + box[slot, core, pl.ds(o, 5)].astype(F32)
            work[pl.ds(base + o, 5)] = total.astype(BF16)
            return 0

        lax.fori_loop(0, count // 5, step, 0)

    ff_travel = functools.partial(Travel, near, core, work, extra, result, sems)

    def of_ff(g):
        return ff_travel(g, g * FF_TILES, g * FF_EXTRA, UNITS, FF_HOPS)

    of_out = ff_travel(5, OUT_BASE, OUT_EXTRA_BASE, OUT_UNITS, OUT_HOPS)
    of_qkv = ff_travel(6, QKV_BASE, QKV_EXTRA_BASE, UNITS, QKV_HOPS)

    def travel(tick):
        for k in range(steps_of(FF_HOPS) - 1, -1, -1):
            since = tick - 2 - 2 * k
            turn = lax.rem(since + 64, 4)

            @pl.when((since >= 0) & (since <= 2 * FF_CHUNKS - 2) & ((turn == 0) | (turn == 3)))
            def _(k=k, since=since):
                g = lax.div(since, 2)
                if k == 0:
                    c = pair(g, lax.rem(g, 2), 0, FF_USED, g * FF_TILES)
                    c.wait()
                    add_own(lax.rem(g, 2), g * FF_TILES, FF_USED)
                of_ff(g).step(k)

        @pl.when(tick > OUT_TICK)
        def _():
            for k in range(steps_of(OUT_HOPS)):

                @pl.when(tick == OUT_TICK + 1 + k)
                def _(k=k):
                    if k == 0:
                        pair(5, 1, 0, OUT_USED, OUT_BASE).wait()
                        add_own(1, OUT_BASE, OUT_USED)
                    of_out.step(k)

        @pl.when(tick > LAST_TICK)
        def _():
            for k in range(steps_of(QKV_HOPS)):

                @pl.when(tick == LAST_TICK + 1 + k)
                def _(k=k):
                    if k == 0:
                        pair(6, 0, 0, QKV_USED, QKV_BASE).wait()
                        add_own(0, QKV_BASE, QKV_USED)
                        pair(7, 0, GAIN_TILE, 1, QKV_BASE).wait()
                        at = QKV_BASE + GAIN_TILE
                        work[at] = (work[at].astype(F32) + box[0, core, GAIN_TILE].astype(F32)).astype(BF16)
                    of_qkv.step(k)

    def tick_body(tick, _):
        @pl.when(tick < OUT_TICK)
        def _():
            feed_forward(tick)

        @pl.when(tick == OUT_TICK)
        def _():
            output_projection()

        @pl.when((tick >= ATTN_TICK) & (tick < LAST_TICK))
        def _():
            attend_back(tick - ATTN_TICK)

        @pl.when(tick == LAST_TICK)
        def _():
            joint_projection()

        travel(tick)
        return 0

    lax.fori_loop(0, TICKS, tick_body, 0)

    pltpu.make_async_copy(h2t, mixed, out_sem.at[0]).wait()
    pltpu.make_async_copy(kvt, input_grad, out_sem.at[1]).wait()
    push_gain.wait_send()
    push_qkv.wait_send()
    push_out.wait_send()

    def finish(g, _):
        for c in ff_push(g):
            c.wait_send()
        of_ff(g).finish()
        return 0

    lax.fori_loop(0, FF_CHUNKS, finish, 0)
    of_out.finish()
    of_qkv.finish()


def layer(tokens, starts, out_grad, gains, qkv_w, out_w, gu_w, down_w):
    vm = pltpu.VMEM
    dma = pltpu.SemaphoreType.DMA
    hbm = pl.BlockSpec(memory_space=pl.ANY)
    near = pl.BlockSpec(memory_space=pltpu.VMEM)
    shape = jax.ShapeDtypeStruct
    return pl.pallas_call(
        layer_kernel,
        out_shape=[
            shape((D, TOK), BF16),
            shape((D, TOK), F32),
            shape((TILES, ROWS, LANES), BF16),
            shape((HALF, 2 * FF), BF16),
            shape((D, FF // 2), BF16),
        ],
        in_specs=[hbm, near, hbm, near, hbm, hbm, hbm, hbm],
        out_specs=[hbm] * 5,
        scratch_shapes=[
            vm((TOK, D), BF16),
            vm((D, TOK), BF16),
            vm((TOK, 1024), BF16),
            vm((16, 1024), BF16),
            vm((D, QKV), BF16),
            vm((D, D), BF16),
            vm((2, 4, D, 256), BF16),
            vm((2, 2, D, 256), BF16),
            vm((TOK, LANES), F32),
            vm((TOK, LANES), F32),
            vm((TOK, TOK), F32),
            vm((TOK, D), BF16),
            vm((D, TOK), BF16),
            vm((D, TOK), BF16),
            vm((QUERY_HEADS, TOK, LANES), BF16),
            vm((KEY_VALUE_HEADS, TOK, LANES), BF16),
            vm((KEY_VALUE_HEADS, TOK, LANES), BF16),
            vm((QUERY_HEADS, TOK, TOK), BF16),
            vm((QUERY_HEADS, TOK, LANES), BF16),
            vm((D, TOK), BF16),
            vm((D, TOK), BF16),
            vm((D, TOK), BF16),
            vm((TOK, D), F32),
            vm((TOK, D), F32),
            vm((TOK, D), F32),
            vm((D, TOK), F32),
            vm((TOK, 13 * LANES), BF16),
            vm((8, D), F32),
            vm((8, D), F32),
            vm((ROWS, LANES), F32),
            vm((2, 2, BOX, ROWS, LANES), BF16),
            vm((TILES, ROWS, LANES), BF16),
            vm((EXTRA, ROWS, LANES), BF16),
            dma((2,)), dma((2,)), dma((2, 10)),
            dma((28,)), dma((28,)), dma((8,)), dma((8,)), dma((2,)),
            dma((7,)), dma((7, 27)), dma((7,)), dma((7, 27)), dma((7, 3)),
        ],
        compiler_params=pltpu.CompilerParams(
            collective_id=0, has_side_effects=True, vmem_limit_bytes=VMEM_LIMIT
        ),
        name="layer",
    )(tokens, starts, out_grad, gains, qkv_w, out_w, gu_w, down_w)


VMEM_LIMIT = 64 * 1024 * 1024 - 256 * 1024


def widen_kernel(
    res, mixed_in, grad_in, down, gu, qkv, out, gain, mixed, grad,
    rv, down_v, gu_v, qkv_v, out_v, mixed_v, grad_v, in_sem, out_sem, pass_sem,
):
    bounds = [FF_TILES * j for j in range(FF_CHUNKS)] + [OUT_BASE, QKV_BASE]
    counts = [FF_USED] * FF_CHUNKS + [OUT_USED, QKV_USED + 1]
    loads = [
        pltpu.make_async_copy(res.at[pl.ds(b, n)], rv.at[pl.ds(b, n)], in_sem.at[i])
        for i, (b, n) in enumerate(zip(bounds, counts))
    ]
    for c in loads:
        c.start()
    passed = [
        pltpu.make_async_copy(mixed_in, mixed_v, pass_sem.at[0]),
        pltpu.make_async_copy(grad_in, grad_v, pass_sem.at[1]),
    ]
    for c in passed:
        c.start()
    stores = []

    def store(src, dst):
        c = pltpu.make_async_copy(src, dst, out_sem.at[len(stores)])
        c.start()
        stores.append(c)

    def column(at, n):
        return rv[pl.ds(at, n)].astype(F32).reshape(n * ROWS, LANES)

    def last_column(at, n):
        both = column(at, n)
        return both[:, :HEAD_SIZE], pltpu.roll(both, HEAD_SIZE, 1)[:, :HEAD_SIZE]

    for j in range(FF_CHUNKS):
        loads[j].wait()
        base = FF_TILES * j
        for s in range(2):
            for w in range(2):
                first = w * FF + s * 1280 + j * 256
                for c in range(2):
                    gu_v[:, first + c * LANES : first + (c + 1) * LANES] = column(base + (s * 2 + w) * 60 + c * 30, 30)
                cols = pl.ds(first, 256)
                store(gu_v.at[:, cols], gu.at[:, cols])
        first = 256 * j
        for c in range(2):
            down_v[:, first + c * LANES : first + (c + 1) * LANES] = column(base + 240 + c * 60, 60)
        cols = pl.ds(first, 256)
        store(down_v.at[:, cols], down.at[:, cols])
    loads[5].wait()
    for c in range(7):
        out_v[:, c * LANES : (c + 1) * LANES] = column(OUT_BASE + c * 30, 30)
    a, b = last_column(OUT_BASE + 210, 15)
    out_v[:240, 7 * LANES :] = a
    out_v[240:, 7 * LANES :] = b
    store(out_v, out)
    loads[6].wait()
    for c in range(12):
        qkv_v[:, c * LANES : (c + 1) * LANES] = column(QKV_BASE + c * 30, 30)
    a, b = last_column(QKV_BASE + 360, 15)
    qkv_v[:240, 12 * LANES :] = a
    qkv_v[240:, 12 * LANES :] = b
    store(qkv_v, qkv)
    gain[...] = rv[QKV_BASE + GAIN_TILE].astype(F32)
    for c, src, dst in zip(passed, (mixed_v, grad_v), (mixed, grad)):
        c.wait()
        store(src, dst)
    for c in stores:
        c.wait()


def widened(result, mixed, grad):
    vm = pltpu.VMEM
    dma = pltpu.SemaphoreType.DMA
    hbm = pl.BlockSpec(memory_space=pl.ANY)
    shape = jax.ShapeDtypeStruct
    sizes = [(D, FF // 2), (HALF, 2 * FF), (HALF, QKV), (HALF, D)]
    return pl.pallas_call(
        widen_kernel,
        out_shape=[shape(s, F32) for s in sizes]
        + [shape((ROWS, LANES), F32), shape((D, TOK), BF16), shape((D, TOK), F32)],
        in_specs=[hbm] * 3,
        out_specs=[hbm] * 4 + [pl.BlockSpec(memory_space=vm), hbm, hbm],
        scratch_shapes=[
            vm((TILES, ROWS, LANES), BF16),
            *[vm(s, F32) for s in sizes],
            vm((D, TOK), BF16),
            vm((D, TOK), F32),
            dma((7,)), dma((29,)), dma((2,)),
        ],
        compiler_params=pltpu.CompilerParams(vmem_limit_bytes=VMEM_LIMIT),
        name="widen",
    )(result, mixed, grad)


def per_device(
    tokens, starts, out_grad, norm_attn, norm_mlp, qkv_weight, out_weight, gate_up_weight, down_weight
):
    core = lax.axis_index("shard")
    both = jnp.stack([norm_attn, norm_mlp])
    gains = jnp.where(
        core == 0, jnp.pad(both, ((0, 14), (0, 544))), jnp.pad(both, ((0, 14), (HALF, 64)))
    )
    mixed, input_grad, result, _, _ = layer(
        tokens.T, starts.reshape(1, TOK), out_grad.T, gains, qkv_weight, out_weight, gate_up_weight, down_weight.T
    )
    down, gu, qkv, out, gain, mixed, input_grad = widened(result, mixed, input_grad)
    first = core * HALF
    gain_one = lax.dynamic_slice(gain[:8].reshape(1024), (first,), (HALF,))
    gain_two = lax.dynamic_slice(gain[8:].reshape(1024), (first,), (HALF,))
    return mixed.T, input_grad.T, gain_one, gain_two, qkv, out, gu, down.T


def solution(mesh):
    rows, weights = P(("replica", "shard"), None), P("shard", None)
    return jax.shard_map(
        per_device,
        mesh=mesh,
        in_specs=(
            rows, P(("replica", "shard")), rows, P("shard"), P("shard"), weights, weights, weights, weights,
        ),
        out_specs=(rows, rows, P("shard"), P("shard"), weights, weights, weights, weights),
        check_vma=False,
    )
```

```python
import functools

import jax
import jax.numpy as jnp
from jax import lax
from jax.experimental import pallas as pl
from jax.experimental.pallas import tpu as pltpu
from jax.sharding import PartitionSpec as P

D = 960
HALF = D // 2
QUERY_HEADS = 15
KEY_VALUE_HEADS = 5
GROUP = QUERY_HEADS // KEY_VALUE_HEADS
HEAD_SIZE = 64
FF = 2560
TOK = 384
QKV = 1600
EPSILON = 1e-05
SCALE = HEAD_SIZE**-0.5
HIDDEN = -1e30

MESH = pl.DeviceIdType.MESH
F32 = jnp.float32
BF16 = jnp.bfloat16
LANES = 128
ROWS = 16
BLOCK = 48

FF_CHUNKS = 5
FF_TILES = 384
FF_USED = 360
OUT_BASE = FF_CHUNKS * FF_TILES
OUT_TILES = 256
OUT_USED = 225
QKV_BASE = OUT_BASE + OUT_TILES
QKV_TILES = 384
QKV_USED = 375
GAIN_TILE = 375
TILES = QKV_BASE + QKV_TILES
BOX = 376
UNITS = (2, 2, 2)
OUT_UNITS = (2, 2)
FF_EXTRA = 378
OUT_EXTRA_BASE = FF_CHUNKS * FF_EXTRA
QKV_EXTRA_BASE = OUT_EXTRA_BASE + 252
EXTRA = QKV_EXTRA_BASE + FF_EXTRA
FF_HOPS = (2, 1, 1)
OUT_HOPS = (2, 1, 1)
QKV_HOPS = (2, 1, 1)


def steps_of(hops):
    return 7 + 2 * sum(h - 1 for h in hops)


OUT_TICK = 2 * FF_CHUNKS
ATTN_TICK = OUT_TICK + 1
LAST_TICK = ATTN_TICK + KEY_VALUE_HEADS
STEP_TICKS = (
    (3, 5, 6, 7, 8, 9, 15, 16, 20),
    (5, 7, 9, 11, 13, 14, 15, 19, 31),
    (6, 8, 14, 16, 18, 19, 23, 25, 29),
    (8, 9, 13, 14, 15, 18, 21, 26, 31),
    (10, 12, 14, 17, 22, 24, 27, 30, 32),
    (11, 13, 15, 18, 21, 23, 26, 28, 31),
    (17, 18, 19, 22, 23, 26, 27, 30, 32),
)
TICKS = 1 + max(t[-1] for t in STEP_TICKS)


def mm(a, b):
    return lax.dot_general(a, b, (((1,), (0,)), ((), ())), preferred_element_type=F32)


def mm_nt(a, b):
    return lax.dot_general(a, b, (((1,), (1,)), ((), ())), preferred_element_type=F32)


def neighbours():
    r = lax.axis_index("replica")
    x = lax.rem(r, 4)
    y = lax.rem(lax.div(r, 4), 4)
    z = lax.div(r, 16)
    out = []
    for place, stride in ((x, 1), (y, 4), (z, 16)):
        ahead = r + stride * (lax.rem(place + 1, 4) - place)
        behind = r + stride * (lax.rem(place + 3, 4) - place)
        across = r + stride * (lax.rem(place + 2, 4) - place)
        out.append((place, ahead, behind, across))
    return out


def add_into(dst, at, terms, count):
    block = 8 if count % 8 == 0 else count

    def step(i, _):
        o = i * block
        total = dst[pl.ds(at + o, block)].astype(F32)
        for ref, off in terms:
            total = total + ref[pl.ds(off + o, block)].astype(F32)
        dst[pl.ds(at + o, block)] = total.astype(BF16)
        return 0

    if count == block:
        step(0, 0)
    else:
        lax.fori_loop(0, count // block, step, 0)


class Travel:
    def __init__(self, near, core, work, extra, result, sems, group, base, extra_base, units, hops):
        self.work, self.extra, self.result = work, extra, result
        send, recv, back_send, back_recv, keep_sem = sems
        self.hops, self.units = hops, units
        self.there, self.back, self.keeps = [[], [], []], [[], [], []], []
        self.sent = 63 * sum(units)

        def copy(src, dst, send_sem, recv_sem, to):
            return pltpu.make_async_remote_copy(
                src_ref=src, dst_ref=dst, send_sem=send_sem, recv_sem=recv_sem, device_id=(to, core), device_id_type=MESH
            )

        partner = near[0][1]
        self.all_sent = [
            lambda sem=sem: copy(
                work.at[pl.ds(0, self.sent)], extra.at[pl.ds(0, self.sent)], sem.at[group], recv.at[group, 0], partner
            ).wait_send()
            for sem in (send, back_send)
        ]
        for color, n in enumerate(units):
            seg = base + 64 * sum(units[:color])
            at = extra_base + 63 * sum(units[:color])
            for phase in range(3):
                place, ahead, behind, across = near[(color + phase) % 3]
                chunk = (16, 4, 1)[phase] * n
                first = chunk // 2
                second = chunk - first
                mine = seg + chunk * place
                plus = seg + chunk * lax.rem(place + 1, 4)
                minus = seg + chunk * lax.rem(place + 3, 4)
                far = seg + chunk * lax.rem(place + 2, 4)
                xa, xb, yp, ym = at, at + first, at + chunk, at + 2 * chunk
                at = at + 3 * chunk
                slot = color * 9 + phase * 3

                def out(k, src, count, dst, to, slot=slot):
                    return lambda: copy(
                        work.at[pl.ds(src, count)], extra.at[pl.ds(dst, count)], send.at[group], recv.at[group, slot + k], to
                    )

                def home(k, source, at, count, to, slot=slot):
                    return lambda: copy(
                        source.at[pl.ds(at, count)], result.at[pl.ds(at, count)],
                        back_send.at[group], back_recv.at[group, slot + k], to,
                    )

                source = work if phase == 2 else result
                if hops[phase] == 2:
                    copies = (
                        out(0, far, first, xa, ahead),
                        out(1, far + first, second, xb, behind),
                        out(2, plus + first, second, yp + first, ahead),
                        out(2, minus, first, ym, behind),
                        out(2, plus, first, yp, ahead),
                        out(2, minus + first, second, ym + first, behind),
                        out(2, seg, 2 * chunk, yp, ahead),
                    )
                    backs = (
                        home(0, source, mine, chunk, ahead),
                        home(1, source, mine, chunk, behind),
                        home(2, result, minus, first, ahead),
                        home(2, result, plus + first, second, behind),
                        home(2, result, seg, chunk, ahead),
                    )
                else:
                    copies = (
                        out(0, far, chunk, xa, across),
                        out(0, plus, chunk, yp, ahead),
                        out(0, minus, chunk, ym, behind),
                        out(0, seg, 3 * chunk, xa, ahead),
                    )
                    backs = (
                        home(0, source, mine, chunk, across),
                        home(0, source, mine, chunk, ahead),
                        home(0, source, mine, chunk, behind),
                        home(0, result, seg, 3 * chunk, ahead),
                    )
                self.there[phase].append((copies, (first, second, chunk, xa, xb, yp, ym, mine, plus, minus)))
                self.back[phase].append(backs)
                if phase == 2:
                    self.keeps.append(
                        lambda mine=mine, chunk=chunk, color=color: pltpu.make_async_copy(
                            work.at[pl.ds(mine, chunk)],
                            result.at[pl.ds(mine, chunk)],
                            keep_sem.at[group, color],
                        )
                    )
                seg = mine

    def start(self, phase, color):
        for i in range(4 if self.hops[phase] == 2 else 3):
            self.there[phase][color][0][i]().start()

    def mid(self, phase, color):
        c, (first, second, chunk, xa, xb, yp, ym, mine, plus, minus) = self.there[phase][color]
        c[0]().wait_recv()
        add_into(self.work, plus, [(self.extra, xa)], first)
        c[4]().start()
        c[1]().wait_recv()
        add_into(self.work, minus + first, [(self.extra, xb)], second)
        c[5]().start()

    def end(self, phase, color):
        c, (first, second, chunk, xa, xb, yp, ym, mine, plus, minus) = self.there[phase][color]
        terms = [(self.extra, yp), (self.extra, ym)]
        if self.hops[phase] == 1:
            terms.append((self.extra, xa))
        c[-1]().wait_recv()
        add_into(self.work, mine, terms, chunk)

    def back_start(self, phase, color):
        c = self.back[phase][color]
        for i in range(2 if self.hops[phase] == 2 else 3):
            c[i]().start()
        if phase == 2:
            self.keeps[color]().start()

    def back_mid(self, phase, color):
        c = self.back[phase][color]
        c[0]().wait_recv()
        c[2]().start()
        c[1]().wait_recv()
        c[3]().start()

    def back_end(self, phase, color):
        self.back[phase][color][-1]().wait_recv()
        if phase == 2:
            self.keeps[color]().wait()

    def step(self, k):
        steps = [("start", 0)]
        for phase in range(3):
            if self.hops[phase] == 2:
                steps.append(("mid", phase))
            steps.append(("turn", phase))
        for phase in (2, 1, 0):
            if self.hops[phase] == 2:
                steps.append(("back_mid", phase))
            steps.append(("back_turn", phase))
        kind, phase = steps[k]
        for color in range(len(self.units)):
            if kind == "start":
                self.start(phase, color)
            elif kind == "mid":
                self.mid(phase, color)
            elif kind == "back_mid":
                self.back_mid(phase, color)
            elif kind == "turn":
                self.end(phase, color)
                if phase < 2:
                    self.start(phase + 1, color)
                else:
                    self.back_start(2, color)
            else:
                self.back_end(phase, color)
                if phase > 0:
                    self.back_start(phase - 1, color)

    def finish(self):
        for wait in self.all_sent:
            wait()


def layer_kernel(
    tokens, starts, out_grad, gains, qkv_w, out_w, gu_w, down_w,
    mixed, input_grad, result, gu_far, down_far,
    tok, dyt, dyp, gain_far, wqkv, wout, wg, wd,
    cosine, sine, bias, hbuf, h1t, h2t, qs, ks, vs, ps, os, qt, dot_, ot,
    x1, yacc, dh2, kvt, dqkv, gacc1, gacc2, gain_sum, box, work, extra,
    in_sem, own_sem, load_sem, w_send, w_recv, pair_send, pair_recv, out_sem,
    send, recv, back_send, back_recv, keep_sem,
):
    r = lax.axis_index("replica")
    core = lax.axis_index("shard")
    other = 1 - core
    sems = (send, recv, back_send, back_recv, keep_sem)

    copy_tok = pltpu.make_async_copy(tokens, h2t, in_sem.at[0])
    copy_dy = pltpu.make_async_copy(out_grad, dyt, in_sem.at[1])
    copy_tok.start()
    copy_dy.start()
    mine480 = pl.ds(pl.multiple_of(core * HALF, 16), HALF)
    other480 = pl.ds(pl.multiple_of(other * HALF, 16), HALF)
    own_qkv = pltpu.make_async_copy(qkv_w, wqkv.at[mine480], own_sem.at[0])
    own_out = pltpu.make_async_copy(out_w, wout.at[mine480], own_sem.at[1])
    own_qkv.start()
    own_out.start()

    barrier = pltpu.get_barrier_semaphore()
    pl.semaphore_signal(barrier, inc=1, device_id=(r, other), device_id_type=MESH)
    near = neighbours()
    for _, *chips in near:
        for chip in chips:
            pl.semaphore_signal(barrier, inc=1, device_id=(chip, core), device_id_type=MESH)

    def push(k, src, dst):
        return pltpu.make_async_remote_copy(
            src_ref=src, dst_ref=dst, send_sem=w_send.at[k], recv_sem=w_recv.at[k],
            device_id=(r, other), device_id_type=MESH,
        )

    def ff_push(j):
        out = []
        for q in range(4):
            cols = pl.ds(pl.multiple_of(q * 1280 + j * 256, 256), 256)
            out.append(push(3 + 5 * j + q, gu_w.at[:, cols], gu_far.at[:, cols]))
        cols = pl.ds(pl.multiple_of(j * 256, 256), 256)
        out.append(push(3 + 5 * j + 4, down_w.at[:, cols], down_far.at[:, cols]))
        return out

    def loads(j):
        slot = lax.rem(j, 2)
        out = []
        for q in range(4):
            cols = pl.ds(pl.multiple_of(q * 1280 + j * 256, 256), 256)
            for i, (src, rows) in enumerate(((gu_w, mine480), (gu_far, other480))):
                out.append(pltpu.make_async_copy(src.at[:, cols], wg.at[slot, q, rows], load_sem.at[slot, 2 * q + i]))
        cols = pl.ds(pl.multiple_of(j * 256, 256), 256)
        out.append(pltpu.make_async_copy(down_w.at[:, cols], wd.at[slot, core], load_sem.at[slot, 8]))
        out.append(pltpu.make_async_copy(down_far.at[:, cols], wd.at[slot, other], load_sem.at[slot, 9]))
        return out

    def start_loads(j):
        for c in ff_push(j):
            c.wait_recv()
        for c in loads(j):
            c.start()

    lane = lax.broadcasted_iota(jnp.int32, (TOK, LANES), 1)
    low = lane < HEAD_SIZE
    early = lax.rem(lane, HEAD_SIZE) < HEAD_SIZE // 2

    def swap(t):
        return jnp.where(early, pltpu.roll(t, LANES - 32, 1), pltpu.roll(t, 32, 1))

    def rope(t):
        return t * cosine[...] + swap(t) * sine[...]

    def rope_back(t):
        return t * cosine[...] - swap(t) * sine[...]

    def transpose(t):
        return jnp.transpose(t.astype(F32)).astype(BF16)

    line = starts[...].astype(F32)
    row = lax.broadcasted_iota(jnp.int32, (TOK, TOK), 0)
    column = lax.broadcasted_iota(jnp.int32, (TOK, TOK), 1)
    across = jnp.broadcast_to(line, (TOK, TOK))
    down_col = jnp.sum(jnp.where(row == column, across, 0.0), axis=1, keepdims=True)
    bias[...] = jnp.where((down_col == across) & (row >= column), 0.0, HIDDEN)
    position = lax.broadcasted_iota(jnp.int32, (TOK, LANES), 0).astype(F32) - down_col
    index = lax.rem(lane, 32).astype(F32)
    freq = jnp.exp(-jnp.log(jnp.full((TOK, LANES), 10000.0, F32)) * index * 2.0 / HEAD_SIZE)
    angle = position * freq
    cosine[...] = jnp.cos(angle)
    sine[...] = jnp.where(early, -jnp.sin(angle), jnp.sin(angle))

    copy_tok.wait()
    copy_dy.wait()
    for t in range(8):
        w = min(LANES, D - t * LANES)
        place = slice(t * LANES, t * LANES + w)
        tok[:, place] = transpose(h2t[place, :])
        dyp[:, place] = transpose(dyt[place, :])

    pl.semaphore_wait(barrier, 1 + 3 * len(near))
    push_gain = push(0, gains, gain_far)
    push_qkv = push(1, qkv_w, wqkv.at[mine480])
    push_out = push(2, out_w, wout.at[mine480])
    push_gain.start()
    push_qkv.start()
    push_out.start()
    for j in range(FF_CHUNKS):
        for c in ff_push(j):
            c.start()
    push_gain.wait_recv()

    def gain(k):
        return (gains[k : k + 1, :].astype(F32) + gain_far[k : k + 1, :].astype(F32))[:, :D]

    def rows_of(i):
        return pl.ds(pl.multiple_of(i * BLOCK, BLOCK), BLOCK)

    def normed(x):
        inv = lax.rsqrt(jnp.mean(x * x, axis=-1, keepdims=True) + EPSILON)
        return x * inv, inv

    def norm_one(i, _):
        rows = rows_of(i)
        n, _inv = normed(tok[rows, :].astype(F32))
        hbuf[rows, :] = (n * gain(0)).astype(BF16)
        return 0

    lax.fori_loop(0, TOK // BLOCK, norm_one, 0)

    def transposed(dst, src):
        for t in range(8):
            w = min(LANES, D - t * LANES)
            dst[t * LANES : t * LANES + w, :] = transpose(src[:, t * LANES : t * LANES + w])

    transposed(h1t, hbuf)

    own_qkv.wait()
    push_qkv.wait_recv()
    for n0 in range(0, QKV, 256):
        width = min(256, QKV - n0)
        joint = mm(hbuf[...], wqkv[:, n0 : n0 + width])
        for c0 in range(0, width, LANES):
            t = (n0 + c0) // LANES
            if c0 + LANES <= width:
                tile = joint[:, c0 : c0 + LANES]
            else:
                piece = joint[:, c0:width]
                tile = jnp.concatenate([piece, piece], axis=1)
            turned = rope(tile) if t < 10 else tile
            if t < 8:
                flipped = transpose(turned)
                w = min(LANES, D - t * LANES)
                qt[t * LANES : t * LANES + w, :] = flipped[:w]
            for part in range(2):
                b = 2 * t + part
                here = low if part == 0 else jnp.logical_not(low)
                if b < QUERY_HEADS:
                    qs[b] = jnp.where(here, turned, 0.0).astype(BF16)
                elif b < QUERY_HEADS + 2 * KEY_VALUE_HEADS:
                    both = jnp.where(here, turned, pltpu.roll(turned, HEAD_SIZE, 1)).astype(BF16)
                    if b < QUERY_HEADS + KEY_VALUE_HEADS:
                        ks[b - QUERY_HEADS] = both
                    else:
                        vs[b - QUERY_HEADS - KEY_VALUE_HEADS] = both

    start_loads(0)
    start_loads(1)

    def attend(g, _):
        for i in range(GROUP):
            h = GROUP * g + i
            s = mm_nt(qs[h], ks[g]) * SCALE + bias[...]
            e = jnp.exp(s - jnp.max(s, axis=-1, keepdims=True))
            p = (e * (1.0 / jnp.sum(e, axis=-1, keepdims=True))).astype(BF16)
            ps[h] = p
            os[h] = mm(p, vs[g]).astype(BF16)
        return 0

    lax.fori_loop(0, KEY_VALUE_HEADS, attend, 0)

    def pair_tile(t):
        a = os[2 * t].astype(F32)
        if 2 * t + 1 < QUERY_HEADS:
            a = jnp.where(low, a, os[2 * t + 1].astype(F32))
        return a

    for t in range(8):
        w = min(LANES, D - t * LANES)
        tile = pair_tile(t)
        hbuf[:, t * LANES : t * LANES + w] = tile[:, :w].astype(BF16)
        ot[t * LANES : t * LANES + w, :] = jnp.transpose(tile).astype(BF16)[:w]

    own_out.wait()
    push_out.wait_recv()
    for n0 in range(0, D, 256):
        cols = slice(n0, min(D, n0 + 256))
        x1[:, cols] = tok[:, cols].astype(F32) + mm(hbuf[...], wout[:, cols])

    def norm_two(i, _):
        rows = rows_of(i)
        x = x1[rows, :]
        n, _inv = normed(x)
        hbuf[rows, :] = (n * gain(1)).astype(BF16)
        yacc[rows, :] = x
        dh2[rows, :] = jnp.zeros((BLOCK, D), F32)
        return 0

    lax.fori_loop(0, TOK // BLOCK, norm_two, 0)
    transposed(h2t, hbuf)

    def pair(k, slot, first, count, base):
        return pltpu.make_async_remote_copy(
            src_ref=box.at[slot, other, pl.ds(first, count)],
            dst_ref=work.at[pl.ds(base + first, count)],
            send_sem=pair_send.at[k],
            recv_sem=pair_recv.at[k],
            device_id=(r, other),
            device_id_type=MESH,
        )

    def tile_columns(slot, half, at, value, count):
        for c in range(count):
            block = value[:, c * LANES : (c + 1) * LANES]
            n = block.shape[0] // ROWS
            box[slot, half, pl.ds(at + c * n, n)] = block.astype(BF16).reshape(n, ROWS, LANES)

    def folded(value):
        n = value.shape[0] // 2
        left = lax.broadcasted_iota(jnp.int32, (n, LANES), 1) < HEAD_SIZE
        return jnp.where(left, value[:n], value[n:])

    def feed_forward(tick):
        j, s = lax.div(tick, 2), lax.rem(tick, 2)
        slot = lax.rem(j, 2)

        @pl.when(s == 0)
        def _():
            for c in loads(j):
                c.wait()

        gate = mm(hbuf[...], wg[slot, s])
        upper = mm(hbuf[...], wg[slot, 2 + s])
        grad = mm(dyp[:, :D], wd[slot, s])
        sigma = jax.nn.sigmoid(gate)
        silu = gate * sigma
        inner_low = (silu * upper).astype(BF16)
        dgate = (grad * upper * sigma * (1.0 + gate * (1.0 - sigma))).astype(BF16)
        dupper = (grad * silu).astype(BF16)
        yacc[...] += mm_nt(inner_low, wd[slot, s])
        dh2[...] += mm_nt(dgate, wg[slot, s]) + mm_nt(dupper, wg[slot, 2 + s])
        for half in range(2):
            left = h2t[half * HALF : (half + 1) * HALF, :]
            tile_columns(slot, half, s * 120, mm(left, dgate), 2)
            tile_columns(slot, half, s * 120 + 60, mm(left, dupper), 2)
        tile_columns(slot, s, 240, mm(dyt[...], inner_low), 2)

        @pl.when(s == 1)
        def _():
            pair(j, slot, 0, FF_USED, j * FF_TILES).start()

            @pl.when(j + 2 < FF_CHUNKS)
            def _():
                start_loads(j + 2)

    def gain_rows(value):
        return jnp.sum(value.reshape(BLOCK // 8, 8, D), axis=0)

    def output_projection():
        gacc2[...] = jnp.zeros((8, D), F32)

        def back_two(i, _):
            rows = rows_of(i)
            n, inv = normed(x1[rows, :])
            d = dh2[rows, :]
            gacc2[...] += gain_rows(d * n)
            dn = d * gain(1)
            dx = dyp[rows, :D].astype(F32) + inv * (dn - n * jnp.mean(dn * n, axis=-1, keepdims=True))
            dh2[rows, :] = dx
            da = dx.astype(BF16)
            dyp[rows, : 7 * LANES] = da[:, : 7 * LANES]
            last = da[:, 7 * LANES :]
            dyp[rows, 7 * LANES :] = jnp.concatenate([last, last], axis=1)
            return 0

        lax.fori_loop(0, TOK // BLOCK, back_two, 0)
        transposed(h2t, yacc)
        pltpu.make_async_copy(h2t, mixed, out_sem.at[0]).start()
        for half in range(2):
            v = mm(ot[half * HALF : (half + 1) * HALF, :], dyp[...])
            tile_columns(1, half, 0, v, 7)
            tile_columns(1, half, 210, folded(v[:, 7 * LANES :]), 1)
        pair(5, 1, 0, OUT_USED, OUT_BASE).start()
        for n0 in range(0, D, 256):
            width = min(256, D - n0)
            v = mm_nt(dyp[:, :D], wout[n0 : n0 + width, :])
            for c0 in range(0, width, LANES):
                t = (n0 + c0) // LANES
                if c0 + LANES <= width:
                    tile = v[:, c0 : c0 + LANES]
                else:
                    piece = v[:, c0:width]
                    tile = jnp.concatenate([piece, piece], axis=1)
                w = min(LANES, D - t * LANES)
                dot_[t * LANES : t * LANES + w, :] = transpose(tile)[:w]
                qs[2 * t] = jnp.where(low, tile, 0.0).astype(BF16)
                if 2 * t + 1 < QUERY_HEADS:
                    qs[2 * t + 1] = jnp.where(low, 0.0, tile).astype(BF16)

    def attend_back(g):
        key_t = jnp.zeros((HEAD_SIZE, TOK), F32)
        value_t = jnp.zeros((HEAD_SIZE, TOK), F32)
        for i in range(GROUP):
            h = GROUP * g + i
            dp = mm_nt(qs[h], vs[g])
            low_p = ps[h]
            p = low_p.astype(F32)
            delta = jnp.sum(dp * p, axis=-1, keepdims=True)
            ds = (p * (dp - delta)).astype(BF16)
            os[h] = rope_back(mm(ds, ks[g]) * SCALE).astype(BF16)
            rows = pl.ds(pl.multiple_of(h * HEAD_SIZE, HEAD_SIZE), HEAD_SIZE)
            key_t = key_t + mm(qt[rows, :], ds)
            value_t = value_t + mm(dot_[rows, :], low_p)
        kvt[pl.ds(pl.multiple_of(HEAD_SIZE * (1 + g), HEAD_SIZE), HEAD_SIZE), :] = key_t * SCALE
        kvt[pl.ds(pl.multiple_of(HEAD_SIZE * (6 + g), HEAD_SIZE), HEAD_SIZE), :] = value_t
        kvt[HEAD_SIZE * 11 : HEAD_SIZE * 12, :] = value_t

    def joint_projection():
        for t in range(13):
            if t < 7:
                tile = pair_tile(t)
            else:
                tile = jnp.transpose(kvt[(t - 7) * LANES : (t - 6) * LANES, :])
                if t < 10:
                    tile = rope_back(tile)
                if t == 7:
                    tile = jnp.where(low, pair_tile(7), tile)
            dqkv[:, t * LANES : (t + 1) * LANES] = tile.astype(BF16)
        for half in range(2):
            left = h1t[half * HALF : (half + 1) * HALF, :]
            for n0 in range(0, 1536, 256):
                v = mm(left, dqkv[:, n0 : n0 + 256])
                tile_columns(0, half, n0 // LANES * 30, v, 2)
            v = mm(left, dqkv[:, 1536:])
            tile_columns(0, half, 360, folded(v), 1)
        pair(6, 0, 0, QKV_USED, QKV_BASE).start()
        for n0 in range(0, D, 256):
            cols = slice(n0, min(D, n0 + 256))
            yacc[:, cols] = mm_nt(dqkv[:, :QKV], wqkv[cols, :])
        gacc1[...] = jnp.zeros((8, D), F32)

        def back_one(i, _):
            rows = rows_of(i)
            n, inv = normed(tok[rows, :].astype(F32))
            d = yacc[rows, :]
            gacc1[...] += gain_rows(d * n)
            dn = d * gain(0)
            dh2[rows, :] += inv * (dn - n * jnp.mean(dn * n, axis=-1, keepdims=True))
            return 0

        lax.fori_loop(0, TOK // BLOCK, back_one, 0)
        for t in range(8):
            place = slice(t * LANES, min(D, (t + 1) * LANES))
            kvt[place, :] = jnp.transpose(dh2[:, place])
        pltpu.make_async_copy(kvt, input_grad, out_sem.at[1]).start()
        gain_sum[...] = jnp.zeros((ROWS, LANES), F32)
        for k, acc in enumerate((gacc1, gacc2)):
            total = jnp.sum(acc[...], axis=0, keepdims=True)
            for t in range(8):
                w = min(LANES, D - t * LANES)
                gain_sum[8 * k + t : 8 * k + t + 1, :w] = total[:, t * LANES : t * LANES + w]
        for half in range(2):
            box[0, half, GAIN_TILE] = gain_sum[...].astype(BF16)
        pair(7, 0, GAIN_TILE, 1, QKV_BASE).start()

    def add_own(slot, base, count):
        def step(i, _):
            o = i * 5
            total = work[pl.ds(base + o, 5)].astype(F32) + box[slot, core, pl.ds(o, 5)].astype(F32)
            work[pl.ds(base + o, 5)] = total.astype(BF16)
            return 0

        lax.fori_loop(0, count // 5, step, 0)

    ff_travel = functools.partial(Travel, near, core, work, extra, result, sems)

    def of_ff(g):
        return ff_travel(g, g * FF_TILES, g * FF_EXTRA, UNITS, FF_HOPS)

    of_out = ff_travel(5, OUT_BASE, OUT_EXTRA_BASE, OUT_UNITS, OUT_HOPS)
    of_qkv = ff_travel(6, QKV_BASE, QKV_EXTRA_BASE, UNITS, QKV_HOPS)

    groups = [of_ff(g) for g in range(FF_CHUNKS)] + [of_out, of_qkv]
    chunks = [(g % 2, FF_USED, g * FF_TILES) for g in range(FF_CHUNKS)]
    chunks += [(1, OUT_USED, OUT_BASE), (0, QKV_USED, QKV_BASE)]

    def take_step(g, k):
        if k == 0:
            slot, used, base = chunks[g]
            pair(g, slot, 0, used, base).wait()
            add_own(slot, base, used)
            if g == 6:
                pair(7, 0, GAIN_TILE, 1, QKV_BASE).wait()
                at = QKV_BASE + GAIN_TILE
                work[at] = (work[at].astype(F32) + box[0, core, GAIN_TILE].astype(F32)).astype(BF16)
        groups[g].step(k)

    def travel(tick):
        def some(first, count):
            @pl.when((tick >= first) & (tick < first + count))
            def _():
                if count > 1:
                    for i in range(0, count, count // 4 if count > 4 else 1):
                        some(first + i, count // 4 if count > 4 else 1)
                    return
                now = [(g, k) for g in range(7) for k, t in enumerate(STEP_TICKS[g]) if t == first]
                for g, k in sorted(now, key=lambda s: (s[0] if s[0] > 4 else 0, -s[1])):
                    take_step(g, k)

        for first in range(0, TICKS, 16):
            some(first, 16)

    def tick_body(tick, _):
        @pl.when(tick < OUT_TICK)
        def _():
            feed_forward(tick)

        @pl.when(tick == OUT_TICK)
        def _():
            output_projection()

        @pl.when((tick >= ATTN_TICK) & (tick < LAST_TICK))
        def _():
            attend_back(tick - ATTN_TICK)

        @pl.when(tick == LAST_TICK)
        def _():
            joint_projection()

        travel(tick)
        return 0

    lax.fori_loop(0, TICKS, tick_body, 0)

    pltpu.make_async_copy(h2t, mixed, out_sem.at[0]).wait()
    pltpu.make_async_copy(kvt, input_grad, out_sem.at[1]).wait()
    push_gain.wait_send()
    push_qkv.wait_send()
    push_out.wait_send()

    def finish(g, _):
        for c in ff_push(g):
            c.wait_send()
        of_ff(g).finish()
        return 0

    lax.fori_loop(0, FF_CHUNKS, finish, 0)
    of_out.finish()
    of_qkv.finish()


def layer(tokens, starts, out_grad, gains, qkv_w, out_w, gu_w, down_w):
    vm = pltpu.VMEM
    dma = pltpu.SemaphoreType.DMA
    hbm = pl.BlockSpec(memory_space=pl.ANY)
    near = pl.BlockSpec(memory_space=pltpu.VMEM)
    shape = jax.ShapeDtypeStruct
    return pl.pallas_call(
        layer_kernel,
        out_shape=[
            shape((D, TOK), BF16),
            shape((D, TOK), F32),
            shape((TILES, ROWS, LANES), BF16),
            shape((HALF, 2 * FF), BF16),
            shape((D, FF // 2), BF16),
        ],
        in_specs=[hbm, near, hbm, near, hbm, hbm, hbm, hbm],
        out_specs=[hbm] * 5,
        scratch_shapes=[
            vm((TOK, D), BF16),
            vm((D, TOK), BF16),
            vm((TOK, 1024), BF16),
            vm((16, 1024), BF16),
            vm((D, QKV), BF16),
            vm((D, D), BF16),
            vm((2, 4, D, 256), BF16),
            vm((2, 2, D, 256), BF16),
            vm((TOK, LANES), F32),
            vm((TOK, LANES), F32),
            vm((TOK, TOK), F32),
            vm((TOK, D), BF16),
            vm((D, TOK), BF16),
            vm((D, TOK), BF16),
            vm((QUERY_HEADS, TOK, LANES), BF16),
            vm((KEY_VALUE_HEADS, TOK, LANES), BF16),
            vm((KEY_VALUE_HEADS, TOK, LANES), BF16),
            vm((QUERY_HEADS, TOK, TOK), BF16),
            vm((QUERY_HEADS, TOK, LANES), BF16),
            vm((D, TOK), BF16),
            vm((D, TOK), BF16),
            vm((D, TOK), BF16),
            vm((TOK, D), F32),
            vm((TOK, D), F32),
            vm((TOK, D), F32),
            vm((D, TOK), F32),
            vm((TOK, 13 * LANES), BF16),
            vm((8, D), F32),
            vm((8, D), F32),
            vm((ROWS, LANES), F32),
            vm((2, 2, BOX, ROWS, LANES), BF16),
            vm((TILES, ROWS, LANES), BF16),
            vm((EXTRA, ROWS, LANES), BF16),
            dma((2,)), dma((2,)), dma((2, 10)),
            dma((28,)), dma((28,)), dma((8,)), dma((8,)), dma((2,)),
            dma((7,)), dma((7, 27)), dma((7,)), dma((7, 27)), dma((7, 3)),
        ],
        compiler_params=pltpu.CompilerParams(
            collective_id=0, has_side_effects=True, vmem_limit_bytes=VMEM_LIMIT
        ),
        name="layer",
    )(tokens, starts, out_grad, gains, qkv_w, out_w, gu_w, down_w)


VMEM_LIMIT = 64 * 1024 * 1024 - 256 * 1024


def widen_kernel(
    res, mixed_in, grad_in, down, gu, qkv, out, gain, mixed, grad,
    rv, down_v, gu_v, qkv_v, out_v, mixed_v, grad_v, in_sem, out_sem, pass_sem,
):
    bounds = [FF_TILES * j for j in range(FF_CHUNKS)] + [OUT_BASE, QKV_BASE]
    counts = [FF_USED] * FF_CHUNKS + [OUT_USED, QKV_USED + 1]
    loads = [
        pltpu.make_async_copy(res.at[pl.ds(b, n)], rv.at[pl.ds(b, n)], in_sem.at[i])
        for i, (b, n) in enumerate(zip(bounds, counts))
    ]
    for c in loads:
        c.start()
    passed = [
        pltpu.make_async_copy(mixed_in, mixed_v, pass_sem.at[0]),
        pltpu.make_async_copy(grad_in, grad_v, pass_sem.at[1]),
    ]
    for c in passed:
        c.start()
    stores = []

    def store(src, dst):
        c = pltpu.make_async_copy(src, dst, out_sem.at[len(stores)])
        c.start()
        stores.append(c)

    def column(at, n):
        return rv[pl.ds(at, n)].astype(F32).reshape(n * ROWS, LANES)

    def last_column(at, n):
        both = column(at, n)
        return both[:, :HEAD_SIZE], pltpu.roll(both, HEAD_SIZE, 1)[:, :HEAD_SIZE]

    for j in range(FF_CHUNKS):
        loads[j].wait()
        base = FF_TILES * j
        for s in range(2):
            for w in range(2):
                first = w * FF + s * 1280 + j * 256
                for c in range(2):
                    gu_v[:, first + c * LANES : first + (c + 1) * LANES] = column(base + (s * 2 + w) * 60 + c * 30, 30)
                cols = pl.ds(first, 256)
                store(gu_v.at[:, cols], gu.at[:, cols])
        first = 256 * j
        for c in range(2):
            down_v[:, first + c * LANES : first + (c + 1) * LANES] = column(base + 240 + c * 60, 60)
        cols = pl.ds(first, 256)
        store(down_v.at[:, cols], down.at[:, cols])
    loads[5].wait()
    for c in range(7):
        out_v[:, c * LANES : (c + 1) * LANES] = column(OUT_BASE + c * 30, 30)
    a, b = last_column(OUT_BASE + 210, 15)
    out_v[:240, 7 * LANES :] = a
    out_v[240:, 7 * LANES :] = b
    store(out_v, out)
    loads[6].wait()
    for c in range(12):
        qkv_v[:, c * LANES : (c + 1) * LANES] = column(QKV_BASE + c * 30, 30)
    a, b = last_column(QKV_BASE + 360, 15)
    qkv_v[:240, 12 * LANES :] = a
    qkv_v[240:, 12 * LANES :] = b
    store(qkv_v, qkv)
    gain[...] = rv[QKV_BASE + GAIN_TILE].astype(F32)
    for c, src, dst in zip(passed, (mixed_v, grad_v), (mixed, grad)):
        c.wait()
        store(src, dst)
    for c in stores:
        c.wait()


def widened(result, mixed, grad):
    vm = pltpu.VMEM
    dma = pltpu.SemaphoreType.DMA
    hbm = pl.BlockSpec(memory_space=pl.ANY)
    shape = jax.ShapeDtypeStruct
    sizes = [(D, FF // 2), (HALF, 2 * FF), (HALF, QKV), (HALF, D)]
    return pl.pallas_call(
        widen_kernel,
        out_shape=[shape(s, F32) for s in sizes]
        + [shape((ROWS, LANES), F32), shape((D, TOK), BF16), shape((D, TOK), F32)],
        in_specs=[hbm] * 3,
        out_specs=[hbm] * 4 + [pl.BlockSpec(memory_space=vm), hbm, hbm],
        scratch_shapes=[
            vm((TILES, ROWS, LANES), BF16),
            *[vm(s, F32) for s in sizes],
            vm((D, TOK), BF16),
            vm((D, TOK), F32),
            dma((7,)), dma((29,)), dma((2,)),
        ],
        compiler_params=pltpu.CompilerParams(vmem_limit_bytes=VMEM_LIMIT),
        name="widen",
    )(result, mixed, grad)


def per_device(
    tokens, starts, out_grad, norm_attn, norm_mlp, qkv_weight, out_weight, gate_up_weight, down_weight
):
    core = lax.axis_index("shard")
    both = jnp.stack([norm_attn, norm_mlp])
    gains = jnp.where(
        core == 0, jnp.pad(both, ((0, 14), (0, 544))), jnp.pad(both, ((0, 14), (HALF, 64)))
    )
    mixed, input_grad, result, _, _ = layer(
        tokens.T, starts.reshape(1, TOK), out_grad.T, gains, qkv_weight, out_weight, gate_up_weight, down_weight.T
    )
    down, gu, qkv, out, gain, mixed, input_grad = widened(result, mixed, input_grad)
    first = core * HALF
    gain_one = lax.dynamic_slice(gain[:8].reshape(1024), (first,), (HALF,))
    gain_two = lax.dynamic_slice(gain[8:].reshape(1024), (first,), (HALF,))
    return mixed.T, input_grad.T, gain_one, gain_two, qkv, out, gu, down.T


def solution(mesh):
    rows, weights = P(("replica", "shard"), None), P("shard", None)
    return jax.shard_map(
        per_device,
        mesh=mesh,
        in_specs=(
            rows, P(("replica", "shard")), rows, P("shard"), P("shard"), weights, weights, weights, weights,
        ),
        out_specs=(rows, rows, P("shard"), P("shard"), weights, weights, weights, weights),
        check_vma=False,
    )
```

```python
import functools

import jax
import jax.numpy as jnp
from jax import lax
from jax.experimental import pallas as pl
from jax.experimental.pallas import tpu as pltpu
from jax.sharding import PartitionSpec as P

D = 960
HALF = D // 2
QUERY_HEADS = 15
KEY_VALUE_HEADS = 5
GROUP = QUERY_HEADS // KEY_VALUE_HEADS
HEAD_SIZE = 64
FF = 2560
TOK = 384
QKV = 1600
EPSILON = 1e-05
SCALE = HEAD_SIZE**-0.5
HIDDEN = -1e30

MESH = pl.DeviceIdType.MESH
F32 = jnp.float32
BF16 = jnp.bfloat16
LANES = 128
ROWS = 16
BLOCK = 48

FF_CHUNKS = 5
FF_TILES = 384
FF_USED = 360
OUT_BASE = FF_CHUNKS * FF_TILES
OUT_TILES = 256
OUT_USED = 225
QKV_BASE = OUT_BASE + OUT_TILES
QKV_TILES = 384
QKV_USED = 375
GAIN_TILE = 375
TILES = QKV_BASE + QKV_TILES
BOX = 376
UNITS = (2, 2, 2)
OUT_UNITS = (2, 2)
FF_EXTRA = 378
OUT_EXTRA_BASE = FF_CHUNKS * FF_EXTRA
QKV_EXTRA_BASE = OUT_EXTRA_BASE + 252
EXTRA = QKV_EXTRA_BASE + FF_EXTRA
FF_HOPS = (2, 1, 1)
OUT_HOPS = (2, 1, 1)
QKV_HOPS = (2, 1, 1)


def steps_of(hops):
    return 7 + 2 * sum(h - 1 for h in hops)


OUT_TICK = 2 * FF_CHUNKS
ATTN_TICK = OUT_TICK + 1
LAST_TICK = ATTN_TICK + KEY_VALUE_HEADS
STEP_TICKS = (
    (3, 4, 5, 6, 7, 8, 9, 15, 17),
    (4, 5, 7, 8, 9, 11, 14, 21, 32),
    (6, 7, 9, 12, 15, 16, 22, 27, 31),
    (8, 10, 14, 17, 19, 20, 24, 29, 33),
    (10, 13, 15, 19, 23, 25, 28, 31, 34),
    (13, 15, 19, 21, 24, 27, 30, 31, 34),
    (17, 19, 21, 23, 24, 27, 29, 30, 33),
)
TICKS = 1 + max(t[-1] for t in STEP_TICKS)


def mm(a, b):
    return lax.dot_general(a, b, (((1,), (0,)), ((), ())), preferred_element_type=F32)


def mm_nt(a, b):
    return lax.dot_general(a, b, (((1,), (1,)), ((), ())), preferred_element_type=F32)


def neighbours():
    r = lax.axis_index("replica")
    x = lax.rem(r, 4)
    y = lax.rem(lax.div(r, 4), 4)
    z = lax.div(r, 16)
    out = []
    for place, stride in ((x, 1), (y, 4), (z, 16)):
        ahead = r + stride * (lax.rem(place + 1, 4) - place)
        behind = r + stride * (lax.rem(place + 3, 4) - place)
        across = r + stride * (lax.rem(place + 2, 4) - place)
        out.append((place, ahead, behind, across))
    return out


def add_into(dst, at, terms, count):
    block = 8 if count % 8 == 0 else count

    def step(i, _):
        o = i * block
        total = dst[pl.ds(at + o, block)].astype(F32)
        for ref, off in terms:
            total = total + ref[pl.ds(off + o, block)].astype(F32)
        dst[pl.ds(at + o, block)] = total.astype(BF16)
        return 0

    if count == block:
        step(0, 0)
    else:
        lax.fori_loop(0, count // block, step, 0)


class Travel:
    def __init__(self, near, core, work, extra, result, sems, group, base, extra_base, units, hops):
        self.work, self.extra, self.result = work, extra, result
        send, recv, back_send, back_recv, keep_sem = sems
        self.hops, self.units = hops, units
        self.there, self.back, self.keeps = [[], [], []], [[], [], []], []
        self.sent = 63 * sum(units)

        def copy(src, dst, send_sem, recv_sem, to):
            return pltpu.make_async_remote_copy(
                src_ref=src, dst_ref=dst, send_sem=send_sem, recv_sem=recv_sem, device_id=(to, core), device_id_type=MESH
            )

        partner = near[0][1]
        self.all_sent = [
            lambda sem=sem: copy(
                work.at[pl.ds(0, self.sent)], extra.at[pl.ds(0, self.sent)], sem.at[group], recv.at[group, 0], partner
            ).wait_send()
            for sem in (send, back_send)
        ]
        for color, n in enumerate(units):
            seg = base + 64 * sum(units[:color])
            at = extra_base + 63 * sum(units[:color])
            for phase in range(3):
                place, ahead, behind, across = near[(color + phase) % 3]
                chunk = (16, 4, 1)[phase] * n
                first = chunk // 2
                second = chunk - first
                mine = seg + chunk * place
                plus = seg + chunk * lax.rem(place + 1, 4)
                minus = seg + chunk * lax.rem(place + 3, 4)
                far = seg + chunk * lax.rem(place + 2, 4)
                xa, xb, yp, ym = at, at + first, at + chunk, at + 2 * chunk
                at = at + 3 * chunk
                slot = color * 9 + phase * 3

                def out(k, src, count, dst, to, slot=slot):
                    return lambda: copy(
                        work.at[pl.ds(src, count)], extra.at[pl.ds(dst, count)], send.at[group], recv.at[group, slot + k], to
                    )

                def home(k, source, at, count, to, slot=slot):
                    return lambda: copy(
                        source.at[pl.ds(at, count)], result.at[pl.ds(at, count)],
                        back_send.at[group], back_recv.at[group, slot + k], to,
                    )

                source = work if phase == 2 else result
                if hops[phase] == 2:
                    copies = (
                        out(0, far, first, xa, ahead),
                        out(1, far + first, second, xb, behind),
                        out(2, plus + first, second, yp + first, ahead),
                        out(2, minus, first, ym, behind),
                        out(2, plus, first, yp, ahead),
                        out(2, minus + first, second, ym + first, behind),
                        out(2, seg, 2 * chunk, yp, ahead),
                    )
                    backs = (
                        home(0, source, mine, chunk, ahead),
                        home(1, source, mine, chunk, behind),
                        home(2, result, minus, first, ahead),
                        home(2, result, plus + first, second, behind),
                        home(2, result, seg, chunk, ahead),
                    )
                else:
                    copies = (
                        out(0, far, chunk, xa, across),
                        out(0, plus, chunk, yp, ahead),
                        out(0, minus, chunk, ym, behind),
                        out(0, seg, 3 * chunk, xa, ahead),
                    )
                    backs = (
                        home(0, source, mine, chunk, across),
                        home(0, source, mine, chunk, ahead),
                        home(0, source, mine, chunk, behind),
                        home(0, result, seg, 3 * chunk, ahead),
                    )
                self.there[phase].append((copies, (first, second, chunk, xa, xb, yp, ym, mine, plus, minus)))
                self.back[phase].append(backs)
                if phase == 2:
                    self.keeps.append(
                        lambda mine=mine, chunk=chunk, color=color: pltpu.make_async_copy(
                            work.at[pl.ds(mine, chunk)],
                            result.at[pl.ds(mine, chunk)],
                            keep_sem.at[group, color],
                        )
                    )
                seg = mine

    def start(self, phase, color):
        for i in range(4 if self.hops[phase] == 2 else 3):
            self.there[phase][color][0][i]().start()

    def mid(self, phase, color):
        c, (first, second, chunk, xa, xb, yp, ym, mine, plus, minus) = self.there[phase][color]
        c[0]().wait_recv()
        add_into(self.work, plus, [(self.extra, xa)], first)
        c[4]().start()
        c[1]().wait_recv()
        add_into(self.work, minus + first, [(self.extra, xb)], second)
        c[5]().start()

    def end(self, phase, color):
        c, (first, second, chunk, xa, xb, yp, ym, mine, plus, minus) = self.there[phase][color]
        terms = [(self.extra, yp), (self.extra, ym)]
        if self.hops[phase] == 1:
            terms.append((self.extra, xa))
        c[-1]().wait_recv()
        add_into(self.work, mine, terms, chunk)

    def back_start(self, phase, color):
        c = self.back[phase][color]
        for i in range(2 if self.hops[phase] == 2 else 3):
            c[i]().start()
        if phase == 2:
            self.keeps[color]().start()

    def back_mid(self, phase, color):
        c = self.back[phase][color]
        c[0]().wait_recv()
        c[2]().start()
        c[1]().wait_recv()
        c[3]().start()

    def back_end(self, phase, color):
        self.back[phase][color][-1]().wait_recv()
        if phase == 2:
            self.keeps[color]().wait()

    def step(self, k):
        steps = [("start", 0)]
        for phase in range(3):
            if self.hops[phase] == 2:
                steps.append(("mid", phase))
            steps.append(("turn", phase))
        for phase in (2, 1, 0):
            if self.hops[phase] == 2:
                steps.append(("back_mid", phase))
            steps.append(("back_turn", phase))
        kind, phase = steps[k]
        for color in range(len(self.units)):
            if kind == "start":
                self.start(phase, color)
            elif kind == "mid":
                self.mid(phase, color)
            elif kind == "back_mid":
                self.back_mid(phase, color)
            elif kind == "turn":
                self.end(phase, color)
                if phase < 2:
                    self.start(phase + 1, color)
                else:
                    self.back_start(2, color)
            else:
                self.back_end(phase, color)
                if phase > 0:
                    self.back_start(phase - 1, color)

    def finish(self):
        for wait in self.all_sent:
            wait()


def layer_kernel(
    tokens, starts, out_grad, gains, qkv_w, out_w, gu_w, down_w,
    mixed, input_grad, result, gu_far, down_far,
    tok, dyt, dyp, gain_far, wqkv, wout, wg, wd,
    cosine, sine, bias, hbuf, h1t, h2t, qs, ks, vs, ps, os, qt, dot_, ot,
    x1, yacc, dh2, kvt, dqkv, gacc1, gacc2, gain_sum, box, work, extra,
    in_sem, own_sem, load_sem, w_send, w_recv, pair_send, pair_recv, out_sem,
    send, recv, back_send, back_recv, keep_sem,
):
    r = lax.axis_index("replica")
    core = lax.axis_index("shard")
    other = 1 - core
    sems = (send, recv, back_send, back_recv, keep_sem)

    copy_tok = pltpu.make_async_copy(tokens, h2t, in_sem.at[0])
    copy_dy = pltpu.make_async_copy(out_grad, dyt, in_sem.at[1])
    copy_tok.start()
    copy_dy.start()
    mine480 = pl.ds(pl.multiple_of(core * HALF, 16), HALF)
    other480 = pl.ds(pl.multiple_of(other * HALF, 16), HALF)
    own_qkv = pltpu.make_async_copy(qkv_w, wqkv.at[mine480], own_sem.at[0])
    own_out = pltpu.make_async_copy(out_w, wout.at[mine480], own_sem.at[1])
    own_qkv.start()
    own_out.start()

    barrier = pltpu.get_barrier_semaphore()
    pl.semaphore_signal(barrier, inc=1, device_id=(r, other), device_id_type=MESH)
    near = neighbours()
    for _, *chips in near:
        for chip in chips:
            pl.semaphore_signal(barrier, inc=1, device_id=(chip, core), device_id_type=MESH)

    def push(k, src, dst):
        return pltpu.make_async_remote_copy(
            src_ref=src, dst_ref=dst, send_sem=w_send.at[k], recv_sem=w_recv.at[k],
            device_id=(r, other), device_id_type=MESH,
        )

    def ff_push(j):
        out = []
        for q in range(4):
            cols = pl.ds(pl.multiple_of(q * 1280 + j * 256, 256), 256)
            out.append(push(3 + 5 * j + q, gu_w.at[:, cols], gu_far.at[:, cols]))
        cols = pl.ds(pl.multiple_of(j * 256, 256), 256)
        out.append(push(3 + 5 * j + 4, down_w.at[:, cols], down_far.at[:, cols]))
        return out

    def loads(j):
        slot = lax.rem(j, 2)
        out = []
        for q in range(4):
            cols = pl.ds(pl.multiple_of(q * 1280 + j * 256, 256), 256)
            for i, (src, rows) in enumerate(((gu_w, mine480), (gu_far, other480))):
                out.append(pltpu.make_async_copy(src.at[:, cols], wg.at[slot, q, rows], load_sem.at[slot, 2 * q + i]))
        cols = pl.ds(pl.multiple_of(j * 256, 256), 256)
        out.append(pltpu.make_async_copy(down_w.at[:, cols], wd.at[slot, core], load_sem.at[slot, 8]))
        out.append(pltpu.make_async_copy(down_far.at[:, cols], wd.at[slot, other], load_sem.at[slot, 9]))
        return out

    def start_loads(j):
        for c in ff_push(j):
            c.wait_recv()
        for c in loads(j):
            c.start()

    lane = lax.broadcasted_iota(jnp.int32, (TOK, LANES), 1)
    low = lane < HEAD_SIZE
    early = lax.rem(lane, HEAD_SIZE) < HEAD_SIZE // 2

    def swap(t):
        return jnp.where(early, pltpu.roll(t, LANES - 32, 1), pltpu.roll(t, 32, 1))

    def rope(t):
        return t * cosine[...] + swap(t) * sine[...]

    def rope_back(t):
        return t * cosine[...] - swap(t) * sine[...]

    def transpose(t):
        return jnp.transpose(t.astype(F32)).astype(BF16)

    line = starts[...].astype(F32)
    row = lax.broadcasted_iota(jnp.int32, (TOK, TOK), 0)
    column = lax.broadcasted_iota(jnp.int32, (TOK, TOK), 1)
    across = jnp.broadcast_to(line, (TOK, TOK))
    down_col = jnp.sum(jnp.where(row == column, across, 0.0), axis=1, keepdims=True)
    bias[...] = jnp.where((down_col == across) & (row >= column), 0.0, HIDDEN)
    position = lax.broadcasted_iota(jnp.int32, (TOK, LANES), 0).astype(F32) - down_col
    index = lax.rem(lane, 32).astype(F32)
    freq = jnp.exp(-jnp.log(jnp.full((TOK, LANES), 10000.0, F32)) * index * 2.0 / HEAD_SIZE)
    angle = position * freq
    cosine[...] = jnp.cos(angle)
    sine[...] = jnp.where(early, -jnp.sin(angle), jnp.sin(angle))

    copy_tok.wait()
    copy_dy.wait()
    for t in range(8):
        w = min(LANES, D - t * LANES)
        place = slice(t * LANES, t * LANES + w)
        tok[:, place] = transpose(h2t[place, :])
        dyp[:, place] = transpose(dyt[place, :])

    pl.semaphore_wait(barrier, 1 + 3 * len(near))
    push_gain = push(0, gains, gain_far)
    push_qkv = push(1, qkv_w, wqkv.at[mine480])
    push_out = push(2, out_w, wout.at[mine480])
    push_gain.start()
    push_qkv.start()
    push_out.start()
    for j in range(FF_CHUNKS):
        for c in ff_push(j):
            c.start()
    push_gain.wait_recv()

    def gain(k):
        return (gains[k : k + 1, :].astype(F32) + gain_far[k : k + 1, :].astype(F32))[:, :D]

    def rows_of(i):
        return pl.ds(pl.multiple_of(i * BLOCK, BLOCK), BLOCK)

    def normed(x):
        inv = lax.rsqrt(jnp.mean(x * x, axis=-1, keepdims=True) + EPSILON)
        return x * inv, inv

    def norm_one(i, _):
        rows = rows_of(i)
        n, _inv = normed(tok[rows, :].astype(F32))
        hbuf[rows, :] = (n * gain(0)).astype(BF16)
        return 0

    lax.fori_loop(0, TOK // BLOCK, norm_one, 0)

    def transposed(dst, src):
        for t in range(8):
            w = min(LANES, D - t * LANES)
            dst[t * LANES : t * LANES + w, :] = transpose(src[:, t * LANES : t * LANES + w])

    transposed(h1t, hbuf)

    own_qkv.wait()
    push_qkv.wait_recv()
    for n0 in range(0, QKV, 256):
        width = min(256, QKV - n0)
        joint = mm(hbuf[...], wqkv[:, n0 : n0 + width])
        for c0 in range(0, width, LANES):
            t = (n0 + c0) // LANES
            if c0 + LANES <= width:
                tile = joint[:, c0 : c0 + LANES]
            else:
                piece = joint[:, c0:width]
                tile = jnp.concatenate([piece, piece], axis=1)
            turned = rope(tile) if t < 10 else tile
            if t < 8:
                flipped = transpose(turned)
                w = min(LANES, D - t * LANES)
                qt[t * LANES : t * LANES + w, :] = flipped[:w]
            for part in range(2):
                b = 2 * t + part
                here = low if part == 0 else jnp.logical_not(low)
                if b < QUERY_HEADS:
                    qs[b] = jnp.where(here, turned, 0.0).astype(BF16)
                elif b < QUERY_HEADS + 2 * KEY_VALUE_HEADS:
                    both = jnp.where(here, turned, pltpu.roll(turned, HEAD_SIZE, 1)).astype(BF16)
                    if b < QUERY_HEADS + KEY_VALUE_HEADS:
                        ks[b - QUERY_HEADS] = both
                    else:
                        vs[b - QUERY_HEADS - KEY_VALUE_HEADS] = both

    start_loads(0)
    start_loads(1)

    def attend(g, _):
        for i in range(GROUP):
            h = GROUP * g + i
            s = mm_nt(qs[h], ks[g]) * SCALE + bias[...]
            e = jnp.exp(s - jnp.max(s, axis=-1, keepdims=True))
            p = (e * (1.0 / jnp.sum(e, axis=-1, keepdims=True))).astype(BF16)
            ps[h] = p
            os[h] = mm(p, vs[g]).astype(BF16)
        return 0

    lax.fori_loop(0, KEY_VALUE_HEADS, attend, 0)

    def pair_tile(t):
        a = os[2 * t].astype(F32)
        if 2 * t + 1 < QUERY_HEADS:
            a = jnp.where(low, a, os[2 * t + 1].astype(F32))
        return a

    for t in range(8):
        w = min(LANES, D - t * LANES)
        tile = pair_tile(t)
        hbuf[:, t * LANES : t * LANES + w] = tile[:, :w].astype(BF16)
        ot[t * LANES : t * LANES + w, :] = jnp.transpose(tile).astype(BF16)[:w]

    own_out.wait()
    push_out.wait_recv()
    for n0 in range(0, D, 256):
        cols = slice(n0, min(D, n0 + 256))
        x1[:, cols] = tok[:, cols].astype(F32) + mm(hbuf[...], wout[:, cols])

    def norm_two(i, _):
        rows = rows_of(i)
        x = x1[rows, :]
        n, _inv = normed(x)
        hbuf[rows, :] = (n * gain(1)).astype(BF16)
        yacc[rows, :] = x
        dh2[rows, :] = jnp.zeros((BLOCK, D), F32)
        return 0

    lax.fori_loop(0, TOK // BLOCK, norm_two, 0)
    transposed(h2t, hbuf)

    def pair(k, slot, first, count, base):
        return pltpu.make_async_remote_copy(
            src_ref=box.at[slot, other, pl.ds(first, count)],
            dst_ref=work.at[pl.ds(base + first, count)],
            send_sem=pair_send.at[k],
            recv_sem=pair_recv.at[k],
            device_id=(r, other),
            device_id_type=MESH,
        )

    def tile_columns(slot, half, at, value, count):
        for c in range(count):
            block = value[:, c * LANES : (c + 1) * LANES]
            n = block.shape[0] // ROWS
            box[slot, half, pl.ds(at + c * n, n)] = block.astype(BF16).reshape(n, ROWS, LANES)

    def folded(value):
        n = value.shape[0] // 2
        left = lax.broadcasted_iota(jnp.int32, (n, LANES), 1) < HEAD_SIZE
        return jnp.where(left, value[:n], value[n:])

    def feed_forward(tick):
        j, s = lax.div(tick, 2), lax.rem(tick, 2)
        slot = lax.rem(j, 2)

        @pl.when(s == 0)
        def _():
            for c in loads(j):
                c.wait()

        gate = mm(hbuf[...], wg[slot, s])
        upper = mm(hbuf[...], wg[slot, 2 + s])
        grad = mm(dyp[:, :D], wd[slot, s])
        sigma = jax.nn.sigmoid(gate)
        silu = gate * sigma
        inner_low = (silu * upper).astype(BF16)
        dgate = (grad * upper * sigma * (1.0 + gate * (1.0 - sigma))).astype(BF16)
        dupper = (grad * silu).astype(BF16)
        yacc[...] += mm_nt(inner_low, wd[slot, s])
        dh2[...] += mm_nt(dgate, wg[slot, s]) + mm_nt(dupper, wg[slot, 2 + s])
        for half in range(2):
            left = h2t[half * HALF : (half + 1) * HALF, :]
            tile_columns(slot, half, s * 120, mm(left, dgate), 2)
            tile_columns(slot, half, s * 120 + 60, mm(left, dupper), 2)
        tile_columns(slot, s, 240, mm(dyt[...], inner_low), 2)

        @pl.when(s == 1)
        def _():
            pair(j, slot, 0, FF_USED, j * FF_TILES).start()

            @pl.when(j + 2 < FF_CHUNKS)
            def _():
                start_loads(j + 2)

    def gain_rows(value):
        return jnp.sum(value.reshape(BLOCK // 8, 8, D), axis=0)

    def output_projection():
        gacc2[...] = jnp.zeros((8, D), F32)

        def back_two(i, _):
            rows = rows_of(i)
            n, inv = normed(x1[rows, :])
            d = dh2[rows, :]
            gacc2[...] += gain_rows(d * n)
            dn = d * gain(1)
            dx = dyp[rows, :D].astype(F32) + inv * (dn - n * jnp.mean(dn * n, axis=-1, keepdims=True))
            dh2[rows, :] = dx
            da = dx.astype(BF16)
            dyp[rows, : 7 * LANES] = da[:, : 7 * LANES]
            last = da[:, 7 * LANES :]
            dyp[rows, 7 * LANES :] = jnp.concatenate([last, last], axis=1)
            return 0

        lax.fori_loop(0, TOK // BLOCK, back_two, 0)
        transposed(h2t, yacc)
        pltpu.make_async_copy(h2t, mixed, out_sem.at[0]).start()
        for half in range(2):
            v = mm(ot[half * HALF : (half + 1) * HALF, :], dyp[...])
            tile_columns(1, half, 0, v, 7)
            tile_columns(1, half, 210, folded(v[:, 7 * LANES :]), 1)
        pair(5, 1, 0, OUT_USED, OUT_BASE).start()
        for n0 in range(0, D, 256):
            width = min(256, D - n0)
            v = mm_nt(dyp[:, :D], wout[n0 : n0 + width, :])
            for c0 in range(0, width, LANES):
                t = (n0 + c0) // LANES
                if c0 + LANES <= width:
                    tile = v[:, c0 : c0 + LANES]
                else:
                    piece = v[:, c0:width]
                    tile = jnp.concatenate([piece, piece], axis=1)
                w = min(LANES, D - t * LANES)
                dot_[t * LANES : t * LANES + w, :] = transpose(tile)[:w]
                qs[2 * t] = jnp.where(low, tile, 0.0).astype(BF16)
                if 2 * t + 1 < QUERY_HEADS:
                    qs[2 * t + 1] = jnp.where(low, 0.0, tile).astype(BF16)

    def attend_back(g):
        key_t = jnp.zeros((HEAD_SIZE, TOK), F32)
        value_t = jnp.zeros((HEAD_SIZE, TOK), F32)
        for i in range(GROUP):
            h = GROUP * g + i
            dp = mm_nt(qs[h], vs[g])
            low_p = ps[h]
            p = low_p.astype(F32)
            delta = jnp.sum(dp * p, axis=-1, keepdims=True)
            ds = (p * (dp - delta)).astype(BF16)
            os[h] = rope_back(mm(ds, ks[g]) * SCALE).astype(BF16)
            rows = pl.ds(pl.multiple_of(h * HEAD_SIZE, HEAD_SIZE), HEAD_SIZE)
            key_t = key_t + mm(qt[rows, :], ds)
            value_t = value_t + mm(dot_[rows, :], low_p)
        kvt[pl.ds(pl.multiple_of(HEAD_SIZE * (1 + g), HEAD_SIZE), HEAD_SIZE), :] = key_t * SCALE
        kvt[pl.ds(pl.multiple_of(HEAD_SIZE * (6 + g), HEAD_SIZE), HEAD_SIZE), :] = value_t
        kvt[HEAD_SIZE * 11 : HEAD_SIZE * 12, :] = value_t

    def joint_projection():
        for t in range(13):
            if t < 7:
                tile = pair_tile(t)
            else:
                tile = jnp.transpose(kvt[(t - 7) * LANES : (t - 6) * LANES, :])
                if t < 10:
                    tile = rope_back(tile)
                if t == 7:
                    tile = jnp.where(low, pair_tile(7), tile)
            dqkv[:, t * LANES : (t + 1) * LANES] = tile.astype(BF16)
        for half in range(2):
            left = h1t[half * HALF : (half + 1) * HALF, :]
            for n0 in range(0, 1536, 256):
                v = mm(left, dqkv[:, n0 : n0 + 256])
                tile_columns(0, half, n0 // LANES * 30, v, 2)
            v = mm(left, dqkv[:, 1536:])
            tile_columns(0, half, 360, folded(v), 1)
        pair(6, 0, 0, QKV_USED, QKV_BASE).start()
        for n0 in range(0, D, 256):
            cols = slice(n0, min(D, n0 + 256))
            yacc[:, cols] = mm_nt(dqkv[:, :QKV], wqkv[cols, :])
        gacc1[...] = jnp.zeros((8, D), F32)

        def back_one(i, _):
            rows = rows_of(i)
            n, inv = normed(tok[rows, :].astype(F32))
            d = yacc[rows, :]
            gacc1[...] += gain_rows(d * n)
            dn = d * gain(0)
            dh2[rows, :] += inv * (dn - n * jnp.mean(dn * n, axis=-1, keepdims=True))
            return 0

        lax.fori_loop(0, TOK // BLOCK, back_one, 0)
        for t in range(8):
            place = slice(t * LANES, min(D, (t + 1) * LANES))
            kvt[place, :] = jnp.transpose(dh2[:, place])
        pltpu.make_async_copy(kvt, input_grad, out_sem.at[1]).start()
        gain_sum[...] = jnp.zeros((ROWS, LANES), F32)
        for k, acc in enumerate((gacc1, gacc2)):
            total = jnp.sum(acc[...], axis=0, keepdims=True)
            for t in range(8):
                w = min(LANES, D - t * LANES)
                gain_sum[8 * k + t : 8 * k + t + 1, :w] = total[:, t * LANES : t * LANES + w]
        for half in range(2):
            box[0, half, GAIN_TILE] = gain_sum[...].astype(BF16)
        pair(7, 0, GAIN_TILE, 1, QKV_BASE).start()

    def add_own(slot, base, count):
        def step(i, _):
            o = i * 5
            total = work[pl.ds(base + o, 5)].astype(F32) + box[slot, core, pl.ds(o, 5)].astype(F32)
            work[pl.ds(base + o, 5)] = total.astype(BF16)
            return 0

        lax.fori_loop(0, count // 5, step, 0)

    ff_travel = functools.partial(Travel, near, core, work, extra, result, sems)

    def of_ff(g):
        return ff_travel(g, g * FF_TILES, g * FF_EXTRA, UNITS, FF_HOPS)

    of_out = ff_travel(5, OUT_BASE, OUT_EXTRA_BASE, OUT_UNITS, OUT_HOPS)
    of_qkv = ff_travel(6, QKV_BASE, QKV_EXTRA_BASE, UNITS, QKV_HOPS)

    groups = [of_ff(g) for g in range(FF_CHUNKS)] + [of_out, of_qkv]
    chunks = [(g % 2, FF_USED, g * FF_TILES) for g in range(FF_CHUNKS)]
    chunks += [(1, OUT_USED, OUT_BASE), (0, QKV_USED, QKV_BASE)]

    def take_step(g, k):
        if k == 0:
            slot, used, base = chunks[g]
            pair(g, slot, 0, used, base).wait()
            add_own(slot, base, used)
            if g == 6:
                pair(7, 0, GAIN_TILE, 1, QKV_BASE).wait()
                at = QKV_BASE + GAIN_TILE
                work[at] = (work[at].astype(F32) + box[0, core, GAIN_TILE].astype(F32)).astype(BF16)
        groups[g].step(k)

    def travel(tick):
        def some(first, count):
            @pl.when((tick >= first) & (tick < first + count))
            def _():
                if count > 1:
                    for i in range(0, count, count // 4 if count > 4 else 1):
                        some(first + i, count // 4 if count > 4 else 1)
                    return
                now = [(g, k) for g in range(7) for k, t in enumerate(STEP_TICKS[g]) if t == first]
                for g, k in sorted(now, key=lambda s: (s[0] if s[0] > 4 else 0, -s[1])):
                    take_step(g, k)

        for first in range(0, TICKS, 16):
            some(first, 16)

    def tick_body(tick, _):
        @pl.when(tick < OUT_TICK)
        def _():
            feed_forward(tick)

        @pl.when(tick == OUT_TICK)
        def _():
            output_projection()

        @pl.when((tick >= ATTN_TICK) & (tick < LAST_TICK))
        def _():
            attend_back(tick - ATTN_TICK)

        @pl.when(tick == LAST_TICK)
        def _():
            joint_projection()

        travel(tick)
        return 0

    lax.fori_loop(0, TICKS, tick_body, 0)

    pltpu.make_async_copy(h2t, mixed, out_sem.at[0]).wait()
    pltpu.make_async_copy(kvt, input_grad, out_sem.at[1]).wait()
    push_gain.wait_send()
    push_qkv.wait_send()
    push_out.wait_send()

    def finish(g, _):
        for c in ff_push(g):
            c.wait_send()
        of_ff(g).finish()
        return 0

    lax.fori_loop(0, FF_CHUNKS, finish, 0)
    of_out.finish()
    of_qkv.finish()


def layer(tokens, starts, out_grad, gains, qkv_w, out_w, gu_w, down_w):
    vm = pltpu.VMEM
    dma = pltpu.SemaphoreType.DMA
    hbm = pl.BlockSpec(memory_space=pl.ANY)
    near = pl.BlockSpec(memory_space=pltpu.VMEM)
    shape = jax.ShapeDtypeStruct
    return pl.pallas_call(
        layer_kernel,
        out_shape=[
            shape((D, TOK), BF16),
            shape((D, TOK), F32),
            shape((TILES, ROWS, LANES), BF16),
            shape((HALF, 2 * FF), BF16),
            shape((D, FF // 2), BF16),
        ],
        in_specs=[hbm, near, hbm, near, hbm, hbm, hbm, hbm],
        out_specs=[hbm] * 5,
        scratch_shapes=[
            vm((TOK, D), BF16),
            vm((D, TOK), BF16),
            vm((TOK, 1024), BF16),
            vm((16, 1024), BF16),
            vm((D, QKV), BF16),
            vm((D, D), BF16),
            vm((2, 4, D, 256), BF16),
            vm((2, 2, D, 256), BF16),
            vm((TOK, LANES), F32),
            vm((TOK, LANES), F32),
            vm((TOK, TOK), F32),
            vm((TOK, D), BF16),
            vm((D, TOK), BF16),
            vm((D, TOK), BF16),
            vm((QUERY_HEADS, TOK, LANES), BF16),
            vm((KEY_VALUE_HEADS, TOK, LANES), BF16),
            vm((KEY_VALUE_HEADS, TOK, LANES), BF16),
            vm((QUERY_HEADS, TOK, TOK), BF16),
            vm((QUERY_HEADS, TOK, LANES), BF16),
            vm((D, TOK), BF16),
            vm((D, TOK), BF16),
            vm((D, TOK), BF16),
            vm((TOK, D), F32),
            vm((TOK, D), F32),
            vm((TOK, D), F32),
            vm((D, TOK), F32),
            vm((TOK, 13 * LANES), BF16),
            vm((8, D), F32),
            vm((8, D), F32),
            vm((ROWS, LANES), F32),
            vm((2, 2, BOX, ROWS, LANES), BF16),
            vm((TILES, ROWS, LANES), BF16),
            vm((EXTRA, ROWS, LANES), BF16),
            dma((2,)), dma((2,)), dma((2, 10)),
            dma((28,)), dma((28,)), dma((8,)), dma((8,)), dma((2,)),
            dma((7,)), dma((7, 27)), dma((7,)), dma((7, 27)), dma((7, 3)),
        ],
        compiler_params=pltpu.CompilerParams(
            collective_id=0, has_side_effects=True, vmem_limit_bytes=VMEM_LIMIT
        ),
        name="layer",
    )(tokens, starts, out_grad, gains, qkv_w, out_w, gu_w, down_w)


VMEM_LIMIT = 64 * 1024 * 1024 - 256 * 1024


def widen_kernel(
    res, mixed_in, grad_in, down, gu, qkv, out, gain, mixed, grad,
    rv, down_v, gu_v, qkv_v, out_v, mixed_v, grad_v, in_sem, out_sem, pass_sem,
):
    bounds = [FF_TILES * j for j in range(FF_CHUNKS)] + [OUT_BASE, QKV_BASE]
    counts = [FF_USED] * FF_CHUNKS + [OUT_USED, QKV_USED + 1]
    loads = [
        pltpu.make_async_copy(res.at[pl.ds(b, n)], rv.at[pl.ds(b, n)], in_sem.at[i])
        for i, (b, n) in enumerate(zip(bounds, counts))
    ]
    for c in loads:
        c.start()
    passed = [
        pltpu.make_async_copy(mixed_in, mixed_v, pass_sem.at[0]),
        pltpu.make_async_copy(grad_in, grad_v, pass_sem.at[1]),
    ]
    for c in passed:
        c.start()
    stores = []

    def store(src, dst):
        c = pltpu.make_async_copy(src, dst, out_sem.at[len(stores)])
        c.start()
        stores.append(c)

    def column(at, n):
        return rv[pl.ds(at, n)].astype(F32).reshape(n * ROWS, LANES)

    def last_column(at, n):
        both = column(at, n)
        return both[:, :HEAD_SIZE], pltpu.roll(both, HEAD_SIZE, 1)[:, :HEAD_SIZE]

    for j in range(FF_CHUNKS):
        loads[j].wait()
        base = FF_TILES * j
        for s in range(2):
            for w in range(2):
                first = w * FF + s * 1280 + j * 256
                for c in range(2):
                    gu_v[:, first + c * LANES : first + (c + 1) * LANES] = column(base + (s * 2 + w) * 60 + c * 30, 30)
                cols = pl.ds(first, 256)
                store(gu_v.at[:, cols], gu.at[:, cols])
        first = 256 * j
        for c in range(2):
            down_v[:, first + c * LANES : first + (c + 1) * LANES] = column(base + 240 + c * 60, 60)
        cols = pl.ds(first, 256)
        store(down_v.at[:, cols], down.at[:, cols])
    loads[5].wait()
    for c in range(7):
        out_v[:, c * LANES : (c + 1) * LANES] = column(OUT_BASE + c * 30, 30)
    a, b = last_column(OUT_BASE + 210, 15)
    out_v[:240, 7 * LANES :] = a
    out_v[240:, 7 * LANES :] = b
    store(out_v, out)
    loads[6].wait()
    for c in range(12):
        qkv_v[:, c * LANES : (c + 1) * LANES] = column(QKV_BASE + c * 30, 30)
    a, b = last_column(QKV_BASE + 360, 15)
    qkv_v[:240, 12 * LANES :] = a
    qkv_v[240:, 12 * LANES :] = b
    store(qkv_v, qkv)
    gain[...] = rv[QKV_BASE + GAIN_TILE].astype(F32)
    for c, src, dst in zip(passed, (mixed_v, grad_v), (mixed, grad)):
        c.wait()
        store(src, dst)
    for c in stores:
        c.wait()


def widened(result, mixed, grad):
    vm = pltpu.VMEM
    dma = pltpu.SemaphoreType.DMA
    hbm = pl.BlockSpec(memory_space=pl.ANY)
    shape = jax.ShapeDtypeStruct
    sizes = [(D, FF // 2), (HALF, 2 * FF), (HALF, QKV), (HALF, D)]
    return pl.pallas_call(
        widen_kernel,
        out_shape=[shape(s, F32) for s in sizes]
        + [shape((ROWS, LANES), F32), shape((D, TOK), BF16), shape((D, TOK), F32)],
        in_specs=[hbm] * 3,
        out_specs=[hbm] * 4 + [pl.BlockSpec(memory_space=vm), hbm, hbm],
        scratch_shapes=[
            vm((TILES, ROWS, LANES), BF16),
            *[vm(s, F32) for s in sizes],
            vm((D, TOK), BF16),
            vm((D, TOK), F32),
            dma((7,)), dma((29,)), dma((2,)),
        ],
        compiler_params=pltpu.CompilerParams(vmem_limit_bytes=VMEM_LIMIT),
        name="widen",
    )(result, mixed, grad)


def per_device(
    tokens, starts, out_grad, norm_attn, norm_mlp, qkv_weight, out_weight, gate_up_weight, down_weight
):
    core = lax.axis_index("shard")
    both = jnp.stack([norm_attn, norm_mlp])
    gains = jnp.where(
        core == 0, jnp.pad(both, ((0, 14), (0, 544))), jnp.pad(both, ((0, 14), (HALF, 64)))
    )
    mixed, input_grad, result, _, _ = layer(
        tokens.T, starts.reshape(1, TOK), out_grad.T, gains, qkv_weight, out_weight, gate_up_weight, down_weight.T
    )
    down, gu, qkv, out, gain, mixed, input_grad = widened(result, mixed, input_grad)
    first = core * HALF
    gain_one = lax.dynamic_slice(gain[:8].reshape(1024), (first,), (HALF,))
    gain_two = lax.dynamic_slice(gain[8:].reshape(1024), (first,), (HALF,))
    return mixed.T, input_grad.T, gain_one, gain_two, qkv, out, gu, down.T


def solution(mesh):
    rows, weights = P(("replica", "shard"), None), P("shard", None)
    return jax.shard_map(
        per_device,
        mesh=mesh,
        in_specs=(
            rows, P(("replica", "shard")), rows, P("shard"), P("shard"), weights, weights, weights, weights,
        ),
        out_specs=(rows, rows, P("shard"), P("shard"), weights, weights, weights, weights),
        check_vma=False,
    )
```
